256 devices in a mesh: gx: 16 (over x_hi, y, core), gy: 16 (over z, x_lo).
Axes of the slice: x: 4 (x_hi: 2, x_lo: 2; x = x_hi * 2 + x_lo), y: 4, z: 8, core: 2. Of those that a mesh axis runs over, the one named last changes fastest.
Arguments:
- fields: bfloat16 [256, 512, 256], P('gx', 'gy'), may hold values from -6 to 6
- w_down: bfloat16 [3, 3, 3, 32, 32], replicated, may hold values from -0.21875 to 0.21875
- w_pool: bfloat16 [2, 2, 2, 32, 64], replicated, may hold values from -0.375 to 0.375
- w_mid: bfloat16 [3, 3, 3, 64, 64], replicated, may hold values from -0.15625 to 0.15625
- w_unpool: bfloat16 [2, 2, 2, 64, 32], replicated, may hold values from -0.75 to 0.75
- w_up: bfloat16 [3, 3, 3, 32, 32], replicated, may hold values from -0.21875 to 0.21875
- cotangent: bfloat16 [256, 512, 256], P('gx', 'gy'), may hold values from -6 to 6
Outputs:
- output: bfloat16 [256, 512, 256], P('gx', 'gy')
- grad_fields: bfloat16 [256, 512, 256], P('gx', 'gy')
- grad_down: float32 [3, 3, 3, 32, 32], replicated
- grad_pool: float32 [2, 2, 2, 32, 64], replicated
- grad_mid: float32 [3, 3, 3, 64, 64], replicated
- grad_unpool: float32 [2, 2, 2, 64, 32], replicated
- grad_up: float32 [3, 3, 3, 32, 32], replicated
The draws below stay inside these ranges and needn't reach their ends.
All inputs are finite; a program needn't handle non-finite values.
Results may differ from the reference program's by a relative error of at most 0.0071.
Values may be sent and summed in bfloat16 or wider, within the bound.
No kernel may reach another device: no remote copies, remote signals or barrier semaphores. Data moves between devices by JAX's collectives and lax.ppermute only.
A program may use at most 128 MiB of HBM per device.

```python
import math
import jax
import jax.numpy as jnp
from jax import lax

CF = 32
CC = 64
ZS = 8
NX = 256
NY = 512


def levels(stream_key, extent, split, low, high):
    def one(dim, shards_of):
        heights = jax.random.uniform(jax.random.fold_in(jax.random.fold_in(stream_key, 6), dim), (shards_of,), jnp.float32, low / len(split), high / len(split))
        return jnp.repeat(jnp.exp(heights), extent[dim] // shards_of).reshape((-1,) + (1,) * (len(extent) - dim - 1))

    level = one(*split[0])
    for cut in split[1:]:
        level = level * one(*cut)
    return level


def bell_draw(own_key, extent, scale, reach, cuts=(), held_as=jnp.bfloat16):
    result = jax.random.normal(own_key, extent, jnp.float32) * scale
    if len(cuts) > 0:
        result = levels(own_key, extent, cuts, -0.22, 0.18) * result
    return jnp.clip(result, min=-reach, max=reach).astype(held_as)


def setup_inputs(seed: int = 0) -> dict:
    key_of = jax.random.split(jax.random.key(seed), 8)
    return {
        "fields": bell_draw(key_of[0], (NX, NY, ZS * CF), 1.0, 6.0, ((0, 16), (1, 16))),
        "w_down": bell_draw(key_of[1], (3, 3, 3, CF, CF), (27 * CF) ** -0.5, 0.21875),
        "w_pool": bell_draw(key_of[2], (2, 2, 2, CF, CC), (8 * CF) ** -0.5, 0.375),
        "w_mid": bell_draw(key_of[3], (3, 3, 3, CC, CC), (27 * CC) ** -0.5, 0.15625),
        "w_unpool": bell_draw(key_of[4], (2, 2, 2, CC, CF), CC ** -0.5, 0.75),
        "w_up": bell_draw(key_of[5], (3, 3, 3, CF, CF), (27 * CF) ** -0.5, 0.21875),
        "cotangent": bell_draw(key_of[6], (NX, NY, ZS * CF), 1.0, 6.0, ((0, 16), (1, 16))),
    }


def dsilu(value):
    sig = jax.nn.sigmoid(value)
    return sig * (1.0 + value * (1.0 - sig))

def plane_shifts(planes):
    return jnp.stack([jnp.eye(planes, k=1 - kk, dtype=jnp.float32) for kk in range(3)])

def band_matrix(weight, planes):
    shifts = plane_shifts(planes)
    band = jnp.einsum('kpz,abkco->abpczo', shifts, weight.astype(jnp.float32))
    return band.reshape(3, 3, planes * weight.shape[3], planes * weight.shape[4]).astype(jnp.bfloat16)

def band_to_weight(dband, planes, cin, cout):
    shifts = plane_shifts(planes)
    return jnp.einsum('kpz,abpczo->abkco', shifts, dband.reshape(3, 3, planes, cin, planes, cout))

def flipped(weight):
    return jnp.transpose(weight[::-1, ::-1, ::-1], (0, 1, 2, 4, 3))

def wrap_pad(field):
    return jnp.pad(field, ((1, 1), (1, 1), (0, 0)), mode='wrap')

def conv_whole(field, weight, planes):
    band = band_matrix(weight, planes)
    padded = wrap_pad(field)
    xs, ys, width = field.shape
    total = jnp.zeros((xs * ys, band.shape[3]), jnp.float32)
    for aa in range(3):
        for bb in range(3):
            piece = padded[aa:aa + xs, bb:bb + ys, :].reshape(xs * ys, width)
            total = total + jnp.dot(piece, band[aa, bb], preferred_element_type=jnp.float32)
    return total.reshape(xs, ys, -1)

def conv_weight_grad(field, dout, planes, cin, cout):
    padded = wrap_pad(field)
    xs, ys, width = field.shape
    flat = dout.reshape(xs * ys, -1)
    parts = []
    for aa in range(3):
        for bb in range(3):
            piece = padded[aa:aa + xs, bb:bb + ys, :].reshape(xs * ys, width)
            parts.append(lax.dot_general(piece, flat, (((0,), (0,)), ((), ())), preferred_element_type=jnp.float32))
    return band_to_weight(jnp.stack(parts), planes, cin, cout)

def split_fine(field):
    xs, ys, width = field.shape
    parts = field.reshape(xs // 2, 2, ys // 2, 2, width).transpose(0, 2, 1, 3, 4)
    return parts.reshape(xs // 2 * (ys // 2), 4 * width)

def merge_fine(flat, xs, ys):
    width = flat.shape[1] // 4
    return flat.reshape(xs // 2, ys // 2, 2, 2, width).transpose(0, 2, 1, 3, 4).reshape(xs, ys, width)

def pool_matrix(weight, half):
    eye = jnp.eye(half, dtype=jnp.float32)
    mat = jnp.einsum('yz,ijlco->ijylczo', eye, weight.astype(jnp.float32))
    return mat.reshape(-1, half * weight.shape[4]).astype(jnp.bfloat16)

def unpool_matrix(weight, half):
    eye = jnp.eye(half, dtype=jnp.float32)
    mat = jnp.einsum('yz,ijlof->yoijzlf', eye, weight.astype(jnp.float32))
    return mat.reshape(half * weight.shape[3], -1).astype(jnp.bfloat16)

def reference(fields, w_down, w_pool, w_mid, w_unpool, w_up, cotangent):
    cf = w_down.shape[3]
    cc = w_mid.shape[3]
    xs, ys = (fields.shape[0], fields.shape[1])
    half = ZS // 2
    pmat = pool_matrix(w_pool, half)
    umat = unpool_matrix(w_unpool, half)
    pre_down = conv_whole(fields, w_down, ZS)
    hidden = jax.nn.silu(pre_down).astype(jnp.bfloat16)
    hidden_parts = split_fine(hidden)
    pre_pool = jnp.dot(hidden_parts, pmat, preferred_element_type=jnp.float32).reshape(xs // 2, ys // 2, -1)
    coarse = jax.nn.silu(pre_pool).astype(jnp.bfloat16)
    pre_mid = conv_whole(coarse, w_mid, half)
    middle = (coarse.astype(jnp.float32) + jax.nn.silu(pre_mid)).astype(jnp.bfloat16)
    middle_flat = middle.reshape(-1, middle.shape[2])
    lifted = jnp.dot(middle_flat, umat, preferred_element_type=jnp.float32)
    pre_up = hidden.astype(jnp.float32) + merge_fine(lifted, xs, ys)
    skip = jax.nn.silu(pre_up).astype(jnp.bfloat16)
    output = (fields.astype(jnp.float32) + conv_whole(skip, w_up, ZS)).astype(jnp.bfloat16)
    d_up = (conv_whole(cotangent, flipped(w_up), ZS) * dsilu(pre_up)).astype(jnp.bfloat16)
    d_up_parts = split_fine(d_up)
    d_middle = lax.dot_general(d_up_parts, umat, (((1,), (1,)), ((), ())), preferred_element_type=jnp.float32)
    d_middle = d_middle.reshape(xs // 2, ys // 2, -1)
    d_mid = (d_middle * dsilu(pre_mid)).astype(jnp.bfloat16)
    d_coarse = d_middle + conv_whole(d_mid, flipped(w_mid), half)
    d_pool = (d_coarse * dsilu(pre_pool)).astype(jnp.bfloat16)
    d_pool_flat = d_pool.reshape(-1, d_pool.shape[2])
    back = lax.dot_general(d_pool_flat, pmat, (((1,), (1,)), ((), ())), preferred_element_type=jnp.float32)
    d_hidden = d_up.astype(jnp.float32) + merge_fine(back, xs, ys)
    d_down = (d_hidden * dsilu(pre_down)).astype(jnp.bfloat16)
    grad_fields = (cotangent.astype(jnp.float32) + conv_whole(d_down, flipped(w_down), ZS)).astype(jnp.bfloat16)
    scale = 1.0 / math.sqrt(xs * ys * ZS)
    grad_up = conv_weight_grad(skip, cotangent, ZS, cf, cf) * scale
    grad_mid = conv_weight_grad(coarse, d_mid, half, cc, cc) * scale
    grad_down = conv_weight_grad(fields, d_down, ZS, cf, cf) * scale
    eye = jnp.eye(half, dtype=jnp.float32)
    d_umat = lax.dot_general(middle_flat, d_up_parts, (((0,), (0,)), ((), ())), preferred_element_type=jnp.float32)
    grad_unpool = jnp.einsum('yz,yoijzlf->ijlof', eye, d_umat.reshape(half, cc, 2, 2, half, 2, cf)) * scale
    d_pmat = lax.dot_general(hidden_parts, d_pool_flat, (((0,), (0,)), ((), ())), preferred_element_type=jnp.float32)
    grad_pool = jnp.einsum('yz,ijylczo->ijlco', eye, d_pmat.reshape(2, 2, half, 2, cf, half, cc)) * scale
    return (output, grad_fields, grad_down, grad_pool, grad_mid, grad_unpool, grad_up)
```

```python
import functools
import math

import jax
import jax.numpy as jnp
from jax import lax
from jax.experimental import pallas as pl
from jax.experimental.pallas import tpu as pltpu
from jax.sharding import PartitionSpec as P

BF = jnp.bfloat16
F32 = jnp.float32
NN = (((1,), (0,)), ((), ()))
NT = (((1,), (1,)), ((), ()))

HF = 7
HC = 5
EX, EY = 32, 48
CX, CY = 16, 32
BX, BY = 16, 32
W = 256
TILES = 50


def dot(a, b, dims=NN):
    return lax.dot_general(a, b, dims, preferred_element_type=F32)


def rounded(v):
    return v.astype(BF).astype(F32)


def loop(n, body):
    def step(i, carry):
        body(i)
        return carry

    lax.fori_loop(0, n, step, 0)


def repeat_matrix(rows, cols, period, first):
    r = lax.broadcasted_iota(jnp.int32, (rows, cols), 0)
    c = lax.broadcasted_iota(jnp.int32, (rows, cols), 1)
    return (lax.rem(c, period) == r + first).astype(F32).astype(BF)


def bands_kernel(wd, wp, wm, wu, wup, bd, pm, bm, um, bu, wide, wide_mid):
    def band(w, out, wide, ch):
        planes = W // ch
        wide[...] = dot(w[...], repeat_matrix(ch, W, ch, 0))
        group = lax.broadcasted_iota(jnp.int32, (ch, W), 1) // ch

        def tap(t):
            base = pl.multiple_of(t * 3 * ch, ch)
            t0 = wide[pl.ds(base, ch), :]
            t1 = wide[pl.ds(base + ch, ch), :]
            t2 = wide[pl.ds(base + 2 * ch, ch), :]
            for p in range(planes):
                rows = jnp.where(group == p, t1, 0.0)
                if p + 1 < planes:
                    rows = jnp.where(group == p + 1, t0, rows)
                if p > 0:
                    rows = jnp.where(group == p - 1, t2, rows)
                out[pl.ds(pl.multiple_of(t * W + p * ch, ch), ch), :] = rows.astype(BF)

        loop(9, tap)

    band(wd, bd, wide, 32)
    band(wup, bu, wide, 32)
    band(wm, bm, wide_mid, 64)
    group = lax.broadcasted_iota(jnp.int32, (64, W), 1) // 64
    same = repeat_matrix(64, W, 64, 0)
    low = repeat_matrix(32, W, 64, 0)
    high = repeat_matrix(32, W, 64, 32)
    for q in range(4):
        pool = dot(wp[q], same)
        unpool = dot(wu[2 * q], low) + dot(wu[2 * q + 1], high)
        for y in range(4):
            rows = slice(q * W + y * 64, q * W + y * 64 + 64)
            pm[rows, :] = jnp.where(group == y, pool, 0.0).astype(BF)
            um[rows, :] = jnp.where(group == y, unpool, 0.0).astype(BF)


def build_bands(w_down, w_pool, w_mid, w_unpool, w_up):
    wide = jax.ShapeDtypeStruct((9 * W, W), BF)
    four = jax.ShapeDtypeStruct((4 * W, W), BF)
    return pl.pallas_call(
        bands_kernel,
        out_shape=(wide, four, wide, four, wide),
        scratch_shapes=[pltpu.VMEM((27 * 32, W), F32), pltpu.VMEM((27 * 64, W), F32)],
        compiler_params=pltpu.CompilerParams(vmem_limit_bytes=24 * 1024 * 1024),
        cost_estimate=pl.CostEstimate(flops=2 * 10**9, bytes_accessed=8 * 10**6, transcendentals=0),
        name="bands",
    )(
        w_down.reshape(27 * 32, 32),
        w_pool.reshape(4, 64, 64),
        w_mid.reshape(27 * 64, 64),
        w_unpool.reshape(8, 64, 32),
        w_up.reshape(27 * 32, 32),
    )


def get_row(src, row):
    if len(src.shape) == 3:
        return src[row]
    return jnp.concatenate([src[0, row], src[1, row]], axis=1)


def get_rows(src, rows):
    return jnp.concatenate([src[0, rows], src[1, rows]], axis=2)


def put_rows(dst, rows, value):
    dst[0, rows] = value[..., 0:128]
    dst[1, rows] = value[..., 128:256]


def get_every_second(src, row, first, count):
    at = pl.ds(first, count, stride=2)
    return jnp.concatenate([src[0, row, at, :], src[1, row, at, :]], axis=1)


def put_every_second(dst, row, first, value):
    at = pl.ds(first, value.shape[0], stride=2)
    dst[0, row, at, :] = value[:, 0:128]
    dst[1, row, at, :] = value[:, 128:256]


def taps_to_lanes(src, row, out, at, lo, size):
    v = get_row(src, row)
    n = v.shape[0]
    out[at, :, 0:W] = pltpu.roll(v, 1, 0)[lo : lo + size].astype(BF)
    out[at, :, W : 2 * W] = v[lo : lo + size].astype(BF)
    out[at, :, 2 * W : 3 * W] = pltpu.roll(v, n - 1, 0)[lo : lo + size].astype(BF)


def conv_rows(v3, first, rows, band):
    total = None
    for a in range(3):
        piece = v3[pl.ds(first + a, rows)]
        piece = piece.reshape(rows * piece.shape[1], 3 * W)
        part = dot(piece, band[a * 3 * W : (a + 1) * 3 * W, :])
        total = part if total is None else total + part
    return total


def conv_t_rows(v3, first, rows, band):
    total = None
    for a in range(3):
        piece = v3[pl.ds(first + a, rows)]
        piece = piece.reshape(rows * piece.shape[1], 3 * W)
        for b in range(3):
            tap = (2 - a) * 3 + (2 - b)
            part = dot(piece[:, b * W : (b + 1) * W], band[tap * W : (tap + 1) * W, :], NT)
            total = part if total is None else total + part
    return total


def pick(d, lanes, shift, ch, width):
    group = lax.broadcasted_iota(jnp.int32, (ch, 128), 1) // ch
    p0 = (lanes % width) // ch
    out = jnp.zeros((ch, 128), F32)
    for g in range(128 // ch):
        z = p0 + g - shift
        if 0 <= z < W // ch:
            out = jnp.where(group == g, d[z * ch : (z + 1) * ch, lanes : lanes + 128], out)
    return out


def put_split(value, hi, lo, row, lanes):
    top = value.astype(BF)
    hi[row : row + value.shape[0], lanes : lanes + 128] = top
    lo[row : row + value.shape[0], lanes : lanes + 128] = (value - top.astype(F32)).astype(BF)


def conv_weight_terms(dout_t, v3, rows, ch, hi, lo, dsc):
    units = 27 * ch
    pad = hi.shape[0] - units
    hi[units:, :] = jnp.zeros((pad, W), BF)
    lo[units:, :] = jnp.zeros((pad, W), BF)
    for a in range(3):
        piece = v3[a : a + rows]
        piece = piece.reshape(rows * piece.shape[1], 3 * W)
        dsc[...] = dot(dout_t, piece)
        for b in range(3):
            for k in range(3):
                unit = (a * 3 + b) * 3 + k
                for t in range(2):
                    value = pick(dsc, b * W + t * 128, k - 1, ch, W)
                    put_split(value, hi, lo, unit * ch, t * 128)


def main_kernel(
    fc, cc, xlo, xhi, ylo, yhi, clo, chi, bd, pm, bm, um, bu,
    out, gf, terms,
    fe, ce, hid, ds_down, skp, ds_up, dup, ddn,
    v3f, v3c, v3fl, v3s, v3d,
    parts, co, mid, ds_pool, ds_mid, dmid, v3m, v3dm, v3ml, local,
    hi, lo, him, lom, dsc,
):
    def gather(dst, count, center, off_x, off_y):
        def own(i):
            dst[8 + i, 0:8] = ylo[off_y + i].astype(F32)
            dst[8 + i, 8:40] = center[i].astype(F32)
            dst[8 + i, 40:48] = yhi[off_y + i].astype(F32)

        loop(BX, own)

        def edge(i):
            dst[8 - count + i, 0:8] = clo[off_x + i].astype(F32)
            dst[8 - count + i, 8:40] = xlo[off_x + i].astype(F32)
            dst[8 - count + i, 40:48] = chi[off_x + i].astype(F32)
            dst[24 + i, 0:8] = clo[HF + HC + off_x + i].astype(F32)
            dst[24 + i, 8:40] = xhi[off_x + i].astype(F32)
            dst[24 + i, 40:48] = chi[HF + HC + off_x + i].astype(F32)

        loop(count, edge)

    gather(fe, HF, fc, 0, 0)
    gather(ce, HC, cc, HF, BX)

    loop(30, lambda i: taps_to_lanes(fe, 1 + i, v3f, i, 0, EY))
    loop(18, lambda i: taps_to_lanes(fe, 7 + i, v3fl, i, 8, BY))
    zero = jnp.zeros((2, EY, W), F32)
    put_rows(hid, slice(0, 2), zero)
    put_rows(hid, slice(30, 32), zero)

    def down(i):
        pre = conv_rows(v3f, 4 * i, 4, bd)
        sig = jax.nn.sigmoid(pre)
        at = pl.ds(2 + 4 * i, 4)
        put_rows(hid, at, rounded(pre * sig).reshape(4, EY, W))
        put_rows(ds_down, at, (sig * (1.0 + pre * (1.0 - sig))).reshape(4, EY, W))

    loop(7, down)

    pad = jnp.zeros((CY - EY // 2, W), F32)

    def to_parts(src, x):
        for i in range(2):
            for j in range(2):
                half = get_every_second(src, 2 * x + i, j, EY // 2)
                parts[2 * i + j, x] = jnp.concatenate([half, pad], axis=0).astype(BF)

    loop(CX, lambda x: to_parts(hid, x))

    def pool(i):
        pre = None
        for q in range(4):
            piece = parts[q, pl.ds(4 * i, 4)].reshape(4 * CY, W)
            part = dot(piece, pm[q * W : (q + 1) * W, :])
            pre = part if pre is None else pre + part
        sig = jax.nn.sigmoid(pre)
        co[pl.ds(4 * i, 4)] = rounded(pre * sig).reshape(4, CY, W)
        ds_pool[pl.ds(4 * i, 4)] = (sig * (1.0 + pre * (1.0 - sig))).reshape(4, CY, W)

    loop(4, pool)

    loop(14, lambda i: taps_to_lanes(co, 1 + i, v3m, i, 0, CY))

    def middle(i):
        pre = conv_rows(v3m, 4 * i, 4, bm)
        sig = jax.nn.sigmoid(pre)
        own = co[pl.ds(2 + 4 * i, 4)].reshape(4 * CY, W)
        mid[pl.ds(2 + 4 * i, 4)] = (own + pre * sig).astype(BF).reshape(4, CY, W)
        ds_mid[pl.ds(2 + 4 * i, 4)] = (sig * (1.0 + pre * (1.0 - sig))).reshape(4, CY, W)

    loop(3, middle)

    def up(x):
        m = mid[pl.ds(2 + 2 * x, 2)].reshape(2 * CY, W)
        for i in range(2):
            for j in range(2):
                q = 2 * i + j
                lifted = dot(m, um[q * W : (q + 1) * W, :])
                for r in range(2):
                    row = 2 * (2 + 2 * x + r) + i
                    own = get_every_second(hid, row, j, EY // 2)
                    pre = own + lifted[r * CY : r * CY + EY // 2]
                    sig = jax.nn.sigmoid(pre)
                    put_every_second(skp, row, j, rounded(pre * sig))
                    put_every_second(ds_up, row, j, sig * (1.0 + pre * (1.0 - sig)))

    loop(6, up)

    loop(18, lambda i: taps_to_lanes(skp, 7 + i, v3s, i, 8, BY))

    def output(i):
        total = conv_rows(v3s, 4 * i, 4, bu).reshape(4, BY, W)
        out[pl.ds(4 * i, 4)] = (fc[pl.ds(4 * i, 4)].astype(F32) + total).astype(BF)

    loop(4, output)

    loop(26, lambda i: taps_to_lanes(ce, 3 + i, v3c, i, 0, EY))

    def d_up(i):
        total = conv_t_rows(v3c, 4 * i, 4, bu)
        at = pl.ds(4 + 4 * i, 4)
        put_rows(dup, at, rounded(total.reshape(4, EY, W) * get_rows(ds_up, at)))

    loop(6, d_up)

    cot_t = cc[...].reshape(BX * BY, W).astype(F32).T.astype(BF)
    fold = repeat_matrix(32, W, 32, 0)
    fold_mid = repeat_matrix(64, W, 64, 0)

    def fold_to(matrix, hi, lo, tile, count):
        total = dot(matrix, hi[...], NT) + dot(matrix, lo[...], NT)
        for t in range(count):
            rows = matrix.shape[0]
            terms[(tile * 32 + t * rows) : (tile * 32 + (t + 1) * rows), :] = total[
                :, t * 128 : (t + 1) * 128
            ]

    conv_weight_terms(cot_t, v3s, BX, 32, hi, lo, dsc)
    fold_to(fold, hi, lo, 7, 7)

    def own_parts(src, x):
        for i in range(2):
            for j in range(2):
                half = get_every_second(src, 8 + 2 * x + i, 8 + j, BY // 2)
                local[2 * i + j, x] = half.astype(BF)

    loop(8, lambda x: own_parts(dup, x))
    mid_t = mid[4:12].astype(F32)[:, 0:24][:, 4:20].reshape(128, W).T.astype(BF)

    def plain_terms(left, q, row):
        d = dot(left, local[q].reshape(128, W))
        for t in range(2):
            group = lax.broadcasted_iota(jnp.int32, (64, 128), 1) // 64
            low = d[(2 * t) * 64 : (2 * t + 1) * 64, t * 128 : (t + 1) * 128]
            high = d[(2 * t + 1) * 64 : (2 * t + 2) * 64, t * 128 : (t + 1) * 128]
            put_split(jnp.where(group == 0, low, high), him, lom, row, t * 128)

    for q in range(4):
        plain_terms(mid_t, q, 64 * q)
    fold_cols = (him[0:256, :], lom[0:256, :])
    unpool = dot(fold_cols[0], fold_mid, NT) + dot(fold_cols[1], fold_mid, NT)
    for q in range(4):
        half = (q % 2) * 64
        rows = slice(46 * 32 + (q // 2) * 64, 46 * 32 + (q // 2 + 1) * 64)
        terms[rows, half : half + 64] = unpool[q * 64 : (q + 1) * 64, :]

    loop(12, lambda x: to_parts(dup, 2 + x))

    def d_middle(i):
        total = None
        at = pl.ds(2 + 4 * i, 4)
        for q in range(4):
            piece = parts[q, at].reshape(4 * CY, W)
            part = dot(piece, um[q * W : (q + 1) * W, :], NT)
            total = part if total is None else total + part
        dmid[at] = rounded(total * ds_mid[at].reshape(4 * CY, W)).reshape(4, CY, W)
        ds_mid[at] = total.reshape(4, CY, W)

    loop(3, d_middle)

    loop(12, lambda i: taps_to_lanes(dmid, 2 + i, v3dm, i, 0, CY))

    def coarse_local(i):
        v = co[3 + i]
        for b in range(3):
            v3ml[i, :, b * W : (b + 1) * W] = v[3 + b : 19 + b].astype(BF)

    loop(10, coarse_local)
    dmid_t = dmid[4:12][:, 4:20].reshape(128, W).T.astype(BF)
    conv_weight_terms(dmid_t, v3ml, 8, 64, him, lom, dsc)
    fold_to(fold_mid, him, lom, 14, 14)

    def d_pool(i):
        at = pl.ds(3 + 2 * i, 2)
        total = conv_t_rows(v3dm, 2 * i, 2, bm).reshape(2, CY, W)
        ds_pool[at] = rounded((ds_mid[at] + total) * ds_pool[at])

    loop(5, d_pool)

    def d_down(i):
        dp = ds_pool[pl.ds(3 + 2 * i, 2)].reshape(2 * CY, W).astype(BF)
        for a in range(2):
            for j in range(2):
                q = 2 * a + j
                back = dot(dp, pm[q * W : (q + 1) * W, :], NT)
                for r in range(2):
                    row = 2 * (3 + 2 * i + r) + a
                    own = get_every_second(dup, row, j, EY // 2)
                    d_hidden = own + back[r * CY : r * CY + EY // 2]
                    slope = get_every_second(ds_down, row, j, EY // 2)
                    put_every_second(ddn, row, j, rounded(d_hidden * slope))

    loop(5, d_down)

    loop(18, lambda i: taps_to_lanes(ddn, 7 + i, v3d, i, 8, BY))

    down_t = get_rows(ddn, slice(8, 24))[:, 8:40].reshape(BX * BY, W).T.astype(BF)
    conv_weight_terms(down_t, v3fl, BX, 32, hi, lo, dsc)
    fold_to(fold, hi, lo, 0, 7)

    loop(8, lambda x: own_parts(hid, x))
    pool_t = ds_pool[4:12][:, 4:20].reshape(128, W).T.astype(BF)
    for q in range(4):
        plain_terms(pool_t, q, 64 * q)
    pooled = dot(fold_mid, him[0:256, :], NT) + dot(fold_mid, lom[0:256, :], NT)
    for t in range(2):
        terms[42 * 32 + t * 64 : 42 * 32 + (t + 1) * 64, :] = pooled[:, t * 128 : (t + 1) * 128]
    rest = terms.shape[0] - TILES * 32
    if rest > 0:
        terms[TILES * 32 :, :] = jnp.zeros((rest, 128), F32)

    def grad_fields(i):
        total = conv_t_rows(v3d, 4 * i, 4, bd).reshape(4, BY, W)
        gf[pl.ds(4 * i, 4)] = (cc[pl.ds(4 * i, 4)].astype(F32) + total).astype(BF)

    loop(4, grad_fields)


def main_call(fields, cot, halos, bands, term_rows):
    block = jax.ShapeDtypeStruct((BX, BY, W), BF)
    fine = pltpu.VMEM((EX, EY, W), F32)
    split = pltpu.VMEM((2, EX, EY, 128), F32)
    coarse = pltpu.VMEM((CX, CY, W), F32)
    return pl.pallas_call(
        main_kernel,
        out_shape=(block, block, jax.ShapeDtypeStruct((term_rows, 128), F32)),
        scratch_shapes=[fine] * 2
        + [split] * 6
        + [
            pltpu.VMEM((30, EY, 3 * W), BF),
            pltpu.VMEM((26, EY, 3 * W), BF),
            pltpu.VMEM((18, BY, 3 * W), BF),
            pltpu.VMEM((18, BY, 3 * W), BF),
            pltpu.VMEM((18, BY, 3 * W), BF),
            pltpu.VMEM((4, CX, CY, W), BF),
            coarse,
            pltpu.VMEM((CX, CY, W), BF),
            coarse,
            coarse,
            coarse,
            pltpu.VMEM((14, CY, 3 * W), BF),
            pltpu.VMEM((12, CY, 3 * W), BF),
            pltpu.VMEM((10, 16, 3 * W), BF),
            pltpu.VMEM((4, 8, 16, W), BF),
            pltpu.VMEM((28 * 32, W), BF),
            pltpu.VMEM((28 * 32, W), BF),
            pltpu.VMEM((28 * 64, W), BF),
            pltpu.VMEM((28 * 64, W), BF),
            pltpu.VMEM((W, 3 * W), F32),
        ],
        compiler_params=pltpu.CompilerParams(vmem_limit_bytes=52 * 1024 * 1024),
        cost_estimate=pl.CostEstimate(flops=10**10, bytes_accessed=10**7, transcendentals=10**6),
        name="network",
    )(fields, cot, *halos, *bands)


def unpack_kernel(terms, down, pool, mid, unpool, up):
    for u in range(27):
        row, lane = (u // 4) * 32, (u % 4) * 32
        down[u] = terms[row : row + 32, lane : lane + 32]
        up[u] = terms[224 + row : 224 + row + 32, lane : lane + 32]
        row, lane = 14 * 32 + (u // 2) * 64, (u % 2) * 64
        mid[u] = terms[row : row + 64, lane : lane + 64]
    for q in range(4):
        row, lane = 42 * 32 + (q // 2) * 64, (q % 2) * 64
        pool[q] = terms[row : row + 64, lane : lane + 64]
        for l in range(2):
            row, lane = 46 * 32 + (q // 2) * 64, (q % 2) * 64 + l * 32
            unpool[2 * q + l] = terms[row : row + 64, lane : lane + 32]


def unpack(terms):
    shape = lambda *s: jax.ShapeDtypeStruct(s, F32)
    return pl.pallas_call(
        unpack_kernel,
        out_shape=(
            shape(27, 32, 32), shape(4, 64, 64), shape(27, 64, 64), shape(8, 64, 32),
            shape(27, 32, 32),
        ),
        name="unpack",
    )(terms)


def ring(axis, step):
    n = lax.axis_size(axis)
    return [(i, (i + step) % n) for i in range(n)]


def exchange(fields, cot):
    def columns(a, b, lo):
        return jnp.concatenate([a[:, lo : lo + 8], b[:, lo : lo + 8]], axis=0)

    last = jnp.concatenate([fields[BX - HF :], cot[BX - HC :]], axis=0)
    first = jnp.concatenate([fields[:HF], cot[:HC]], axis=0)
    xlo = lax.ppermute(last, "gx", ring("gx", 1))
    xhi = lax.ppermute(first, "gx", ring("gx", -1))
    ylo = lax.ppermute(columns(fields, cot, BY - 8), "gy", ring("gy", 1))
    yhi = lax.ppermute(columns(fields, cot, 0), "gy", ring("gy", -1))
    clo = lax.ppermute(columns(xlo, xhi, BY - 8), "gy", ring("gy", 1))
    chi = lax.ppermute(columns(xlo, xhi, 0), "gy", ring("gy", -1))
    return (xlo, xhi, ylo, yhi, clo, chi)


def reduce_groups(nx, ny):
    flat = lambda x, y: x * ny + y
    near = [[flat(x, 2 * z + e) for x in range(nx) for e in range(2)] for z in range(ny // 2)]
    far = [[flat(x, 2 * z + e) for z in range(ny // 2)] for x in range(nx) for e in range(2)]
    return near, far


def per_device(fields, w_down, w_pool, w_mid, w_unpool, w_up, cotangent):
    nx, ny = lax.axis_size("gx"), lax.axis_size("gy")
    near, far = reduce_groups(nx, ny)
    n1, n2 = len(near[0]), len(far[0])
    rows = -(-TILES * 32 // (8 * n1)) * 8
    bands = build_bands(w_down, w_pool, w_mid, w_unpool, w_up)
    halos = exchange(fields, cotangent)
    output, grad_fields, terms = main_call(fields, cotangent, halos, bands, n1 * rows)
    swap = functools.partial(
        lax.all_to_all, axis_name=("gx", "gy"), split_axis=0, concat_axis=0, tiled=True
    )
    part = jnp.sum(swap(terms.reshape(n1, rows, 128), axis_index_groups=near), axis=0)
    part = swap(jnp.broadcast_to(part, (n2, rows, 128)), axis_index_groups=far)
    cells = fields.shape[0] * fields.shape[1] * 8 * nx * ny
    part = jnp.sum(part, axis=0) * (1.0 / math.sqrt(cells))
    whole = swap(jnp.broadcast_to(part, (n1, rows, 128)), axis_index_groups=near)
    down, pool, mid, unpool, up = unpack(whole.reshape(n1 * rows, 128))
    return (
        output,
        grad_fields,
        down.reshape(w_down.shape),
        pool.reshape(w_pool.shape),
        mid.reshape(w_mid.shape),
        unpool.reshape(w_unpool.shape),
        up.reshape(w_up.shape),
    )


def solution(mesh):
    placed = (P("gx", "gy", None), P(), P(), P(), P(), P(), P("gx", "gy", None))
    return jax.shard_map(
        per_device,
        mesh=mesh,
        in_specs=placed,
        out_specs=(P("gx", "gy", None), P("gx", "gy", None), P(), P(), P(), P(), P()),
        check_vma=False,
    )
```

```python
import functools
import math

import jax
import jax.numpy as jnp
from jax import lax
from jax.experimental import pallas as pl
from jax.experimental.pallas import tpu as pltpu
from jax.sharding import PartitionSpec as P

BF = jnp.bfloat16
F32 = jnp.float32
NN = (((1,), (0,)), ((), ()))
NT = (((1,), (1,)), ((), ()))
TN = (((0,), (0,)), ((), ()))

HF = 7
HC = 5
EX, EY = 32, 48
CX, CY = 16, 32
BX, BY = 16, 32
W = 256
TILES = 50


def dot(a, b, dims=NN):
    return lax.dot_general(a, b, dims, preferred_element_type=F32)


def rounded(v):
    return v.astype(BF).astype(F32)


def loop(n, body):
    def step(i, carry):
        body(i)
        return carry

    lax.fori_loop(0, n, step, 0)


def repeat_matrix(rows, cols, period, first):
    r = lax.broadcasted_iota(jnp.int32, (rows, cols), 0)
    c = lax.broadcasted_iota(jnp.int32, (rows, cols), 1)
    return (lax.rem(c, period) == r + first).astype(F32).astype(BF)


def bands_kernel(wd, wp, wm, wu, wup, bd, pm, bm, um, bu, wide, wide_mid):
    def band(w, out, wide, ch):
        planes = W // ch
        wide[...] = dot(w[...], repeat_matrix(ch, W, ch, 0))
        group = lax.broadcasted_iota(jnp.int32, (ch, W), 1) // ch

        def tap(t):
            base = pl.multiple_of(t * 3 * ch, ch)
            t0 = wide[pl.ds(base, ch), :]
            t1 = wide[pl.ds(base + ch, ch), :]
            t2 = wide[pl.ds(base + 2 * ch, ch), :]
            for p in range(planes):
                rows = jnp.where(group == p, t1, 0.0)
                if p + 1 < planes:
                    rows = jnp.where(group == p + 1, t0, rows)
                if p > 0:
                    rows = jnp.where(group == p - 1, t2, rows)
                out[pl.ds(pl.multiple_of(t * W + p * ch, ch), ch), :] = rows.astype(BF)

        loop(9, tap)

    band(wd, bd, wide, 32)
    band(wup, bu, wide, 32)
    band(wm, bm, wide_mid, 64)
    group = lax.broadcasted_iota(jnp.int32, (64, W), 1) // 64
    same = repeat_matrix(64, W, 64, 0)
    low = repeat_matrix(32, W, 64, 0)
    high = repeat_matrix(32, W, 64, 32)
    for q in range(4):
        pool = dot(wp[q], same)
        unpool = dot(wu[2 * q], low, TN) + dot(wu[2 * q + 1], high, TN)
        for y in range(4):
            rows = slice(q * W + y * 64, q * W + y * 64 + 64)
            pm[rows, :] = jnp.where(group == y, pool, 0.0).astype(BF)
            um[rows, :] = jnp.where(group == y, unpool, 0.0).astype(BF)


def build_bands(w_down, w_pool, w_mid, w_unpool, w_up):
    wide = jax.ShapeDtypeStruct((9 * W, W), BF)
    four = jax.ShapeDtypeStruct((4 * W, W), BF)
    return pl.pallas_call(
        bands_kernel,
        out_shape=(wide, four, wide, four, wide),
        scratch_shapes=[pltpu.VMEM((27 * 32, W), F32), pltpu.VMEM((27 * 64, W), F32)],
        compiler_params=pltpu.CompilerParams(vmem_limit_bytes=24 * 1024 * 1024),
        cost_estimate=pl.CostEstimate(flops=2 * 10**9, bytes_accessed=8 * 10**6, transcendentals=0),
        name="bands",
    )(
        w_down.reshape(27 * 32, 32),
        w_pool.reshape(4, 64, 64),
        w_mid.reshape(27 * 64, 64),
        w_unpool.transpose(0, 1, 2, 4, 3).reshape(8, 32, 64),
        w_up.reshape(27 * 32, 32),
    )


def get_row(src, row):
    if len(src.shape) == 3:
        return src[row]
    return jnp.concatenate([src[0, row], src[1, row]], axis=1)


def get_rows(src, rows):
    return jnp.concatenate([src[0, rows], src[1, rows]], axis=2)


def put_rows(dst, rows, value):
    dst[0, rows] = value[..., 0:128]
    dst[1, rows] = value[..., 128:256]


def get_every_second(src, row, first, count):
    at = pl.ds(first, count, stride=2)
    return jnp.concatenate([src[0, row, at, :], src[1, row, at, :]], axis=1)


def put_every_second(dst, row, first, value):
    at = pl.ds(first, value.shape[0], stride=2)
    dst[0, row, at, :] = value[:, 0:128]
    dst[1, row, at, :] = value[:, 128:256]


def taps_to_lanes(src, row, out, at, lo, size):
    v = get_row(src, row)
    n = v.shape[0]
    out[at, :, 0:W] = pltpu.roll(v, 1, 0)[lo : lo + size].astype(BF)
    out[at, :, W : 2 * W] = v[lo : lo + size].astype(BF)
    out[at, :, 2 * W : 3 * W] = pltpu.roll(v, n - 1, 0)[lo : lo + size].astype(BF)


def conv_rows(v3, first, rows, band):
    total = None
    for a in range(3):
        piece = v3[pl.ds(first + a, rows)]
        piece = piece.reshape(rows * piece.shape[1], 3 * W)
        part = dot(piece, band[a * 3 * W : (a + 1) * 3 * W, :])
        total = part if total is None else total + part
    return total


def conv_t_rows(v3, first, rows, band):
    total = None
    for a in range(3):
        piece = v3[pl.ds(first + a, rows)]
        piece = piece.reshape(rows * piece.shape[1], 3 * W)
        for b in range(3):
            tap = (2 - a) * 3 + (2 - b)
            part = dot(piece[:, b * W : (b + 1) * W], band[tap * W : (tap + 1) * W, :], NT)
            total = part if total is None else total + part
    return total


def pick(d, lanes, shift, ch, width):
    group = lax.broadcasted_iota(jnp.int32, (ch, 128), 1) // ch
    p0 = (lanes % width) // ch
    out = jnp.zeros((ch, 128), F32)
    for g in range(128 // ch):
        z = p0 + g - shift
        if 0 <= z < W // ch:
            out = jnp.where(group == g, d[z * ch : (z + 1) * ch, lanes : lanes + 128], out)
    return out


def put_split(value, hi, lo, row, lanes):
    top = value.astype(BF)
    hi[row : row + value.shape[0], lanes : lanes + 128] = top
    lo[row : row + value.shape[0], lanes : lanes + 128] = (value - top.astype(F32)).astype(BF)


def conv_weight_terms(dout_t, v3, rows, ch, hi, lo, dsc):
    units = 27 * ch
    pad = hi.shape[0] - units
    hi[units:, :] = jnp.zeros((pad, W), BF)
    lo[units:, :] = jnp.zeros((pad, W), BF)
    for a in range(3):
        piece = v3[a : a + rows]
        piece = piece.reshape(rows * piece.shape[1], 3 * W)
        dsc[...] = dot(dout_t, piece)
        for b in range(3):
            for k in range(3):
                unit = (a * 3 + b) * 3 + k
                for t in range(2):
                    value = pick(dsc, b * W + t * 128, k - 1, ch, W)
                    put_split(value, hi, lo, unit * ch, t * 128)


def main_kernel(
    fc, cc, xlo, xhi, ylo, yhi, clo, chi, bd, pm, bm, um, bu,
    terms, v3s, v3d,
    fe, ce, hid, ds_down, skp, ds_up, dup, ddn,
    v3f, v3c, v3fl,
    parts, co, mid, ds_pool, ds_mid, dmid, v3m, v3dm, v3ml, local,
    hi, lo, him, lom, dsc,
):
    def gather(dst, count, center, off_x, off_y):
        def own(i):
            dst[8 + i, 0:8] = ylo[off_y + i].astype(F32)
            dst[8 + i, 8:40] = center[i].astype(F32)
            dst[8 + i, 40:48] = yhi[off_y + i].astype(F32)

        loop(BX, own)

        def edge(i):
            dst[8 - count + i, 0:8] = clo[off_x + i].astype(F32)
            dst[8 - count + i, 8:40] = xlo[off_x + i].astype(F32)
            dst[8 - count + i, 40:48] = chi[off_x + i].astype(F32)
            dst[24 + i, 0:8] = clo[HF + HC + off_x + i].astype(F32)
            dst[24 + i, 8:40] = xhi[off_x + i].astype(F32)
            dst[24 + i, 40:48] = chi[HF + HC + off_x + i].astype(F32)

        loop(count, edge)

    gather(fe, HF, fc, 0, 0)
    gather(ce, HC, cc, HF, BX)

    loop(30, lambda i: taps_to_lanes(fe, 1 + i, v3f, i, 0, EY))
    loop(18, lambda i: taps_to_lanes(fe, 7 + i, v3fl, i, 8, BY))
    zero = jnp.zeros((2, EY, W), F32)
    put_rows(hid, slice(0, 2), zero)
    put_rows(hid, slice(30, 32), zero)

    def down(i):
        pre = conv_rows(v3f, 14 * i, 14, bd)
        sig = jax.nn.sigmoid(pre)
        at = pl.ds(2 + 14 * i, 14)
        put_rows(hid, at, rounded(pre * sig).reshape(14, EY, W))
        put_rows(ds_down, at, (sig * (1.0 + pre * (1.0 - sig))).reshape(14, EY, W))

    loop(2, down)

    pad = jnp.zeros((CY - EY // 2, W), F32)

    def to_parts(src, x):
        for i in range(2):
            for j in range(2):
                half = get_every_second(src, 2 * x + i, j, EY // 2)
                parts[2 * i + j, x] = jnp.concatenate([half, pad], axis=0).astype(BF)

    loop(CX, lambda x: to_parts(hid, x))

    def pool(i):
        pre = None
        for q in range(4):
            piece = parts[q, pl.ds(8 * i, 8)].reshape(8 * CY, W)
            part = dot(piece, pm[q * W : (q + 1) * W, :])
            pre = part if pre is None else pre + part
        sig = jax.nn.sigmoid(pre)
        co[pl.ds(8 * i, 8)] = rounded(pre * sig).reshape(8, CY, W)
        ds_pool[pl.ds(8 * i, 8)] = (sig * (1.0 + pre * (1.0 - sig))).reshape(8, CY, W)

    loop(2, pool)

    loop(14, lambda i: taps_to_lanes(co, 1 + i, v3m, i, 0, CY))

    pre_mid = conv_rows(v3m, 0, 12, bm)
    sig_mid = jax.nn.sigmoid(pre_mid)
    own_mid = co[2:14].reshape(12 * CY, W)
    mid[2:14] = (own_mid + pre_mid * sig_mid).astype(BF).reshape(12, CY, W)
    ds_mid[2:14] = (sig_mid * (1.0 + pre_mid * (1.0 - sig_mid))).reshape(12, CY, W)

    def up(x):
        m = mid[pl.ds(2 + 6 * x, 6)].reshape(6 * CY, W)
        for i in range(2):
            for j in range(2):
                q = 2 * i + j
                lifted = dot(m, um[q * W : (q + 1) * W, :])
                for r in range(6):
                    row = 2 * (2 + 6 * x + r) + i
                    own = get_every_second(hid, row, j, EY // 2)
                    pre = own + lifted[r * CY : r * CY + EY // 2]
                    sig = jax.nn.sigmoid(pre)
                    put_every_second(skp, row, j, rounded(pre * sig))
                    put_every_second(ds_up, row, j, sig * (1.0 + pre * (1.0 - sig)))

    loop(2, up)

    loop(18, lambda i: taps_to_lanes(skp, 7 + i, v3s, i, 8, BY))

    loop(26, lambda i: taps_to_lanes(ce, 3 + i, v3c, i, 0, EY))

    def d_up(i):
        total = conv_t_rows(v3c, 12 * i, 12, bu)
        at = pl.ds(4 + 12 * i, 12)
        put_rows(dup, at, rounded(total.reshape(12, EY, W) * get_rows(ds_up, at)))

    loop(2, d_up)

    cot_t = cc[...].reshape(BX * BY, W).astype(F32).T.astype(BF)
    fold = repeat_matrix(32, W, 32, 0)
    fold_mid = repeat_matrix(64, W, 64, 0)

    def fold_to(matrix, hi, lo, tile, count):
        total = dot(matrix, hi[...], NT) + dot(matrix, lo[...], NT)
        for t in range(count):
            rows = matrix.shape[0]
            part = total[:, t * 128 : (t + 1) * 128]
            terms[(tile * 32 + t * rows) : (tile * 32 + (t + 1) * rows), :] = part.astype(BF)

    conv_weight_terms(cot_t, v3s, BX, 32, hi, lo, dsc)
    fold_to(fold, hi, lo, 7, 7)

    def own_parts(src, x):
        for i in range(2):
            for j in range(2):
                half = get_every_second(src, 8 + 2 * x + i, 8 + j, BY // 2)
                local[2 * i + j, x] = half.astype(BF)

    loop(8, lambda x: own_parts(dup, x))
    mid_t = mid[4:12].astype(F32)[:, 0:24][:, 4:20].reshape(128, W).T.astype(BF)

    def fold_four(tile):
        total = dot(fold_mid, him[0:256, :], NT) + dot(fold_mid, lom[0:256, :], NT)
        for t in range(2):
            rows = slice(tile * 32 + t * 64, tile * 32 + (t + 1) * 64)
            terms[rows, :] = total[:, t * 128 : (t + 1) * 128].astype(BF)

    def plain_terms(left, q, row):
        d = dot(left, local[q].reshape(128, W))
        for t in range(2):
            group = lax.broadcasted_iota(jnp.int32, (64, 128), 1) // 64
            low = d[(2 * t) * 64 : (2 * t + 1) * 64, t * 128 : (t + 1) * 128]
            high = d[(2 * t + 1) * 64 : (2 * t + 2) * 64, t * 128 : (t + 1) * 128]
            put_split(jnp.where(group == 0, low, high), him, lom, row, t * 128)

    for q in range(4):
        plain_terms(mid_t, q, 64 * q)
    fold_four(46)

    loop(12, lambda x: to_parts(dup, 2 + x))

    d_middle = None
    for q in range(4):
        part = dot(parts[q, 2:14].reshape(12 * CY, W), um[q * W : (q + 1) * W, :], NT)
        d_middle = part if d_middle is None else d_middle + part
    dmid[2:14] = rounded(d_middle * ds_mid[2:14].reshape(12 * CY, W)).reshape(12, CY, W)
    ds_mid[2:14] = d_middle.reshape(12, CY, W)

    loop(12, lambda i: taps_to_lanes(dmid, 2 + i, v3dm, i, 0, CY))

    def coarse_local(i):
        v = co[3 + i]
        for b in range(3):
            v3ml[i, :, b * W : (b + 1) * W] = v[3 + b : 19 + b].astype(BF)

    loop(10, coarse_local)
    dmid_t = dmid[4:12][:, 4:20].reshape(128, W).T.astype(BF)
    conv_weight_terms(dmid_t, v3ml, 8, 64, him, lom, dsc)
    fold_to(fold_mid, him, lom, 14, 14)

    d_coarse = ds_mid[3:13] + conv_t_rows(v3dm, 0, 10, bm).reshape(10, CY, W)
    ds_pool[3:13] = rounded(d_coarse * ds_pool[3:13])

    dp = ds_pool[3:13].reshape(10 * CY, W).astype(BF)
    for i in range(2):
        for j in range(2):
            q = 2 * i + j
            back = dot(dp, pm[q * W : (q + 1) * W, :], NT)
            for r in range(10):
                row = 2 * (3 + r) + i
                own = get_every_second(dup, row, j, EY // 2)
                d_hidden = own + back[r * CY : r * CY + EY // 2]
                slope = get_every_second(ds_down, row, j, EY // 2)
                put_every_second(ddn, row, j, rounded(d_hidden * slope))

    loop(18, lambda i: taps_to_lanes(ddn, 7 + i, v3d, i, 8, BY))

    down_t = get_rows(ddn, slice(8, 24))[:, 8:40].reshape(BX * BY, W).T.astype(BF)
    conv_weight_terms(down_t, v3fl, BX, 32, hi, lo, dsc)
    fold_to(fold, hi, lo, 0, 7)

    loop(8, lambda x: own_parts(hid, x))
    pool_t = ds_pool[4:12][:, 4:20].reshape(128, W).T.astype(BF)
    for q in range(4):
        plain_terms(pool_t, q, 64 * q)
    fold_four(42)
    rest = terms.shape[0] - TILES * 32
    if rest > 0:
        terms[TILES * 32 :, :] = jnp.zeros((rest, 128), BF)


def finish_kernel(fc, cc, v3s, v3d, bd, bu, out, gf):
    total = conv_rows(v3s, 0, BX, bu).reshape(BX, BY, W)
    out[...] = (fc[...].astype(F32) + total).astype(BF)
    total = conv_t_rows(v3d, 0, BX, bd).reshape(BX, BY, W)
    gf[...] = (cc[...].astype(F32) + total).astype(BF)


def finish_call(fields, cot, v3s, v3d, bands):
    block = jax.ShapeDtypeStruct((BX, BY, W), BF)
    return pl.pallas_call(
        finish_kernel,
        out_shape=(block, block),
        compiler_params=pltpu.CompilerParams(vmem_limit_bytes=20 * 1024 * 1024),
        cost_estimate=pl.CostEstimate(flops=3 * 10**9, bytes_accessed=10**7, transcendentals=0),
        name="finish",
    )(fields, cot, v3s, v3d, bands[0], bands[4])


def main_call(fields, cot, halos, bands, term_rows):
    taps = jax.ShapeDtypeStruct((18, BY, 3 * W), BF)
    fine = pltpu.VMEM((EX, EY, W), F32)
    split = pltpu.VMEM((2, EX, EY, 128), F32)
    coarse = pltpu.VMEM((CX, CY, W), F32)
    return pl.pallas_call(
        main_kernel,
        out_shape=(jax.ShapeDtypeStruct((term_rows, 128), BF), taps, taps),
        scratch_shapes=[fine] * 2
        + [split] * 6
        + [
            pltpu.VMEM((30, EY, 3 * W), BF),
            pltpu.VMEM((26, EY, 3 * W), BF),
            pltpu.VMEM((18, BY, 3 * W), BF),
            pltpu.VMEM((4, CX, CY, W), BF),
            coarse,
            pltpu.VMEM((CX, CY, W), BF),
            coarse,
            coarse,
            coarse,
            pltpu.VMEM((14, CY, 3 * W), BF),
            pltpu.VMEM((12, CY, 3 * W), BF),
            pltpu.VMEM((10, 16, 3 * W), BF),
            pltpu.VMEM((4, 8, 16, W), BF),
            pltpu.VMEM((28 * 32, W), BF),
            pltpu.VMEM((28 * 32, W), BF),
            pltpu.VMEM((28 * 64, W), BF),
            pltpu.VMEM((28 * 64, W), BF),
            pltpu.VMEM((W, 3 * W), F32),
        ],
        compiler_params=pltpu.CompilerParams(vmem_limit_bytes=36 * 1024 * 1024),
        cost_estimate=pl.CostEstimate(flops=10**10, bytes_accessed=10**7, transcendentals=10**6),
        name="network",
    )(fields, cot, *halos, *bands)


def unpack_kernel(terms, down, pool, mid, unpool, up):
    for u in range(27):
        row, lane = (u // 4) * 32, (u % 4) * 32
        down[u] = terms[row : row + 32, lane : lane + 32].astype(F32)
        up[u] = terms[224 + row : 224 + row + 32, lane : lane + 32].astype(F32)
        row, lane = 14 * 32 + (u // 2) * 64, (u % 2) * 64
        mid[u] = terms[row : row + 64, lane : lane + 64].astype(F32)
    for q in range(4):
        row, lane = 42 * 32 + (q // 2) * 64, (q % 2) * 64
        pool[q] = terms[row : row + 64, lane : lane + 64].astype(F32)
        unpool[q] = terms[128 + row : 128 + row + 64, lane : lane + 64].astype(F32)


def unpack(terms):
    shape = lambda *s: jax.ShapeDtypeStruct(s, F32)
    return pl.pallas_call(
        unpack_kernel,
        out_shape=(
            shape(27, 32, 32), shape(4, 64, 64), shape(27, 64, 64), shape(4, 64, 64),
            shape(27, 32, 32),
        ),
        name="unpack",
    )(terms)


def ring(axis, step):
    n = lax.axis_size(axis)
    return [(i, (i + step) % n) for i in range(n)]


def exchange(fields, cot):
    def columns(a, b, lo):
        return jnp.concatenate([a[:, lo : lo + 8], b[:, lo : lo + 8]], axis=0)

    last = jnp.concatenate([fields[BX - HF :], cot[BX - HC :]], axis=0)
    first = jnp.concatenate([fields[:HF], cot[:HC]], axis=0)
    xlo = lax.ppermute(last, "gx", ring("gx", 1))
    xhi = lax.ppermute(first, "gx", ring("gx", -1))
    ylo = lax.ppermute(columns(fields, cot, BY - 8), "gy", ring("gy", 1))
    yhi = lax.ppermute(columns(fields, cot, 0), "gy", ring("gy", -1))
    clo = lax.ppermute(columns(xlo, xhi, BY - 8), "gy", ring("gy", 1))
    chi = lax.ppermute(columns(xlo, xhi, 0), "gy", ring("gy", -1))
    return (xlo, xhi, ylo, yhi, clo, chi)


def reduce_groups(nx, ny):
    flat = lambda x, y: x * ny + y
    near = [[flat(x, 2 * z + e) for x in range(nx) for e in range(2)] for z in range(ny // 2)]
    far = [[flat(x, 2 * z + e) for z in range(ny // 2)] for x in range(nx) for e in range(2)]
    return near, far


def per_device(fields, w_down, w_pool, w_mid, w_unpool, w_up, cotangent):
    nx, ny = lax.axis_size("gx"), lax.axis_size("gy")
    near, far = reduce_groups(nx, ny)
    n1, n2 = len(near[0]), len(far[0])
    rows = -(-TILES * 32 // (8 * n1)) * 8
    bands = build_bands(w_down, w_pool, w_mid, w_unpool, w_up)
    halos = exchange(fields, cotangent)
    terms, v3s, v3d = main_call(fields, cotangent, halos, bands, n1 * rows)
    swap = functools.partial(
        lax.all_to_all, axis_name=("gx", "gy"), split_axis=0, concat_axis=0, tiled=True
    )
    part = swap(terms.reshape(n1, rows, 128), axis_index_groups=near)
    output, grad_fields = finish_call(fields, cotangent, v3s, v3d, bands)
    part = jnp.sum(part.astype(F32), axis=0)
    part = swap(jnp.broadcast_to(part, (n2, rows, 128)), axis_index_groups=far)
    cells = fields.shape[0] * fields.shape[1] * 8 * nx * ny
    part = (jnp.sum(part, axis=0) * (1.0 / math.sqrt(cells))).astype(BF)
    whole = swap(jnp.broadcast_to(part, (n1, rows, 128)), axis_index_groups=near)
    down, pool, mid, unpool, up = unpack(whole.reshape(n1 * rows, 128))
    return (
        output,
        grad_fields,
        down.reshape(w_down.shape),
        pool.reshape(w_pool.shape),
        mid.reshape(w_mid.shape),
        unpool.reshape(2, 2, 2, 32, 64).transpose(0, 1, 2, 4, 3),
        up.reshape(w_up.shape),
    )


def solution(mesh):
    placed = (P("gx", "gy", None), P(), P(), P(), P(), P(), P("gx", "gy", None))
    return jax.shard_map(
        per_device,
        mesh=mesh,
        in_specs=placed,
        out_specs=(P("gx", "gy", None), P("gx", "gy", None), P(), P(), P(), P(), P()),
        check_vma=False,
    )
```

```python
import functools
import math

import jax
import jax.numpy as jnp
from jax import lax
from jax.experimental import pallas as pl
from jax.experimental.pallas import tpu as pltpu
from jax.sharding import PartitionSpec as P

BF = jnp.bfloat16
F32 = jnp.float32
NN = (((1,), (0,)), ((), ()))
NT = (((1,), (1,)), ((), ()))
TN = (((0,), (0,)), ((), ()))

HF = 7
HC = 5
EX, EY = 32, 48
CX, CY = 16, 32
BX, BY = 16, 32
W = 256
TILES = 50


def dot(a, b, dims=NN):
    return lax.dot_general(a, b, dims, preferred_element_type=F32)


def rounded(v):
    return v.astype(BF).astype(F32)


def loop(n, body):
    def step(i, carry):
        body(i)
        return carry

    lax.fori_loop(0, n, step, 0)


def repeat_matrix(rows, cols, period, first):
    r = lax.broadcasted_iota(jnp.int32, (rows, cols), 0)
    c = lax.broadcasted_iota(jnp.int32, (rows, cols), 1)
    return (lax.rem(c, period) == r + first).astype(F32).astype(BF)


def bands_kernel(wd, wp, wm, wu, wup, bd, pm, bm, um, bu, wide, wide_mid):
    def band(w, out, wide, ch):
        planes = W // ch
        wide[...] = dot(w[...], repeat_matrix(ch, W, ch, 0))
        group = lax.broadcasted_iota(jnp.int32, (ch, W), 1) // ch

        def tap(t):
            base = pl.multiple_of(t * 3 * ch, ch)
            t0 = wide[pl.ds(base, ch), :]
            t1 = wide[pl.ds(base + ch, ch), :]
            t2 = wide[pl.ds(base + 2 * ch, ch), :]
            for p in range(planes):
                rows = jnp.where(group == p, t1, 0.0)
                if p + 1 < planes:
                    rows = jnp.where(group == p + 1, t0, rows)
                if p > 0:
                    rows = jnp.where(group == p - 1, t2, rows)
                out[pl.ds(pl.multiple_of(t * W + p * ch, ch), ch), :] = rows.astype(BF)

        loop(9, tap)

    band(wd, bd, wide, 32)
    band(wup, bu, wide, 32)
    band(wm, bm, wide_mid, 64)
    group = lax.broadcasted_iota(jnp.int32, (64, W), 1) // 64
    same = repeat_matrix(64, W, 64, 0)
    low = repeat_matrix(32, W, 64, 0)
    high = repeat_matrix(32, W, 64, 32)
    for q in range(4):
        pool = dot(wp[q], same)
        unpool = dot(wu[2 * q], low, TN) + dot(wu[2 * q + 1], high, TN)
        for y in range(4):
            rows = slice(q * W + y * 64, q * W + y * 64 + 64)
            pm[rows, :] = jnp.where(group == y, pool, 0.0).astype(BF)
            um[rows, :] = jnp.where(group == y, unpool, 0.0).astype(BF)


def build_bands(w_down, w_pool, w_mid, w_unpool, w_up):
    wide = jax.ShapeDtypeStruct((9 * W, W), BF)
    four = jax.ShapeDtypeStruct((4 * W, W), BF)
    return pl.pallas_call(
        bands_kernel,
        out_shape=(wide, four, wide, four, wide),
        scratch_shapes=[pltpu.VMEM((27 * 32, W), F32), pltpu.VMEM((27 * 64, W), F32)],
        compiler_params=pltpu.CompilerParams(vmem_limit_bytes=24 * 1024 * 1024),
        cost_estimate=pl.CostEstimate(flops=2 * 10**9, bytes_accessed=8 * 10**6, transcendentals=0),
        name="bands",
    )(
        w_down.reshape(27 * 32, 32),
        w_pool.reshape(4, 64, 64),
        w_mid.reshape(27 * 64, 64),
        w_unpool.transpose(0, 1, 2, 4, 3).reshape(8, 32, 64),
        w_up.reshape(27 * 32, 32),
    )


def get_row(src, row):
    if len(src.shape) == 3 and src.shape[2] == 128:
        at = pl.ds(pl.multiple_of(row * EY, 8), EY)
        return jnp.concatenate([src[0, at, :], src[1, at, :]], axis=1)
    if len(src.shape) == 3:
        return src[row]
    return jnp.concatenate([src[0, row], src[1, row]], axis=1)


def clear_ends(src, half, row):
    for at in (0, 40):
        src[half, pl.ds(pl.multiple_of(row * EY + at, 8), 8), :] = jnp.zeros((8, 128), F32)


def get_rows(src, rows):
    return jnp.concatenate([src[0, rows], src[1, rows]], axis=2)


def put_row(dst, row, value):
    dst[row] = value.astype(BF)


def put_rows(dst, rows, value):
    dst[0, rows] = value[..., 0:128]
    dst[1, rows] = value[..., 128:256]


def get_every_second(src, row, first, count):
    at = pl.ds(first, count, stride=2)
    return jnp.concatenate([src[0, row, at, :], src[1, row, at, :]], axis=1)


def put_every_second(dst, row, first, value):
    at = pl.ds(first, value.shape[0], stride=2)
    dst[0, row, at, :] = value[:, 0:128]
    dst[1, row, at, :] = value[:, 128:256]


def taps_to_lanes(src, row, out, at, lo, size):
    v = get_row(src, row).astype(F32)
    n = v.shape[0]
    out[at, :, 0:W] = pltpu.roll(v, 1, 0)[lo : lo + size].astype(BF)
    out[at, :, W : 2 * W] = v[lo : lo + size].astype(BF)
    out[at, :, 2 * W : 3 * W] = pltpu.roll(v, n - 1, 0)[lo : lo + size].astype(BF)


def conv_rows(v3, first, rows, band):
    total = None
    for a in range(3):
        piece = v3[pl.ds(first + a, rows)]
        piece = piece.reshape(rows * piece.shape[1], 3 * W)
        part = dot(piece, band[a * 3 * W : (a + 1) * 3 * W, :])
        total = part if total is None else total + part
    return total


def conv_t_rows(v3, first, rows, band):
    total = None
    for a in range(3):
        piece = v3[pl.ds(first + a, rows)]
        piece = piece.reshape(rows * piece.shape[1], 3 * W)
        for b in range(3):
            tap = (2 - a) * 3 + (2 - b)
            part = dot(piece[:, b * W : (b + 1) * W], band[tap * W : (tap + 1) * W, :], NT)
            total = part if total is None else total + part
    return total


def pick(d, lanes, shift, ch, width):
    group = lax.broadcasted_iota(jnp.int32, (ch, 128), 1) // ch
    p0 = (lanes % width) // ch
    out = jnp.zeros((ch, 128), F32)
    for g in range(128 // ch):
        z = p0 + g - shift
        if 0 <= z < W // ch:
            out = jnp.where(group == g, d[z * ch : (z + 1) * ch, lanes : lanes + 128], out)
    return out


def put_split(value, hi, lo, row, lanes):
    top = value.astype(BF)
    hi[row : row + value.shape[0], lanes : lanes + 128] = top
    lo[row : row + value.shape[0], lanes : lanes + 128] = (value - top.astype(F32)).astype(BF)


def conv_weight_terms(dout_t, v3, rows, ch, hi, lo, dsc):
    units = 27 * ch
    pad = hi.shape[0] - units
    hi[units:, :] = jnp.zeros((pad, W), BF)
    lo[units:, :] = jnp.zeros((pad, W), BF)
    for a in range(3):
        piece = v3[a : a + rows]
        piece = piece.reshape(rows * piece.shape[1], 3 * W)
        dsc[...] = dot(dout_t, piece)
        for b in range(3):
            for k in range(3):
                unit = (a * 3 + b) * 3 + k
                for t in range(2):
                    value = pick(dsc, b * W + t * 128, k - 1, ch, W)
                    put_split(value, hi, lo, unit * ch, t * 128)


def main_kernel(
    fc, cc, xlo, xhi, ylo, yhi, clo, chi, bd, pm, bm, um, bu,
    terms, skip_rows, down_rows,
    fe, ce, hid, ds_down, skp, ds_up, dup, ddn,
    v3f, v3c, v3fl, v3s,
    parts, co, mid, ds_pool, ds_mid, dmid, v3m, v3dm, v3ml, local,
    hi, lo, him, lom, dsc,
):
    def gather(dst, count, center, off):
        def put(row, value):
            at = pl.ds(pl.multiple_of(row * EY + 8, 8), BY)
            dst[0, at, :] = value[:, 0:128]
            dst[1, at, :] = value[:, 128:256]

        loop(BX, lambda i: put(8 + i, center[i].astype(F32)))

        def edge(i):
            put(8 - count + i, xlo[off + i].astype(F32))
            put(24 + i, xhi[off + i].astype(F32))

        loop(count, edge)
        for c in range(count):
            for side, y, other in ((ylo, 8 - count + c, 0), (yhi, 40 + c, HF + HC)):
                column = jnp.concatenate(
                    [
                        clo[other + off + c].astype(F32),
                        side[off + c].astype(F32),
                        chi[other + off + c].astype(F32),
                    ],
                    axis=0,
                )
                for h in range(2):
                    dst[h, pl.ds(y, EX, stride=EY), :] = column[:, h * 128 : h * 128 + 128]

    for ext in (fe, ce):
        for h in range(2):
            loop(EX, lambda x: clear_ends(ext, h, x))
    gather(fe, HF, fc, 0)
    gather(ce, HC, cc, HF)

    loop(30, lambda i: taps_to_lanes(fe, 1 + i, v3f, i, 0, EY))
    loop(18, lambda i: taps_to_lanes(fe, 7 + i, v3fl, i, 8, BY))
    zero = jnp.zeros((2, EY, W), F32)
    put_rows(hid, slice(0, 2), zero)
    put_rows(hid, slice(30, 32), zero)

    def down(i):
        pre = conv_rows(v3f, 14 * i, 14, bd)
        sig = jax.nn.sigmoid(pre)
        at = pl.ds(2 + 14 * i, 14)
        put_rows(hid, at, rounded(pre * sig).reshape(14, EY, W))
        put_rows(ds_down, at, (sig * (1.0 + pre * (1.0 - sig))).reshape(14, EY, W))

    loop(2, down)

    pad = jnp.zeros((CY - EY // 2, W), F32)

    def to_parts(src, x):
        for i in range(2):
            for j in range(2):
                half = get_every_second(src, 2 * x + i, j, EY // 2)
                parts[2 * i + j, x] = jnp.concatenate([half, pad], axis=0).astype(BF)

    loop(CX, lambda x: to_parts(hid, x))

    def pool(i):
        pre = None
        for q in range(4):
            piece = parts[q, pl.ds(8 * i, 8)].reshape(8 * CY, W)
            part = dot(piece, pm[q * W : (q + 1) * W, :])
            pre = part if pre is None else pre + part
        sig = jax.nn.sigmoid(pre)
        co[pl.ds(8 * i, 8)] = rounded(pre * sig).reshape(8, CY, W)
        ds_pool[pl.ds(8 * i, 8)] = (sig * (1.0 + pre * (1.0 - sig))).reshape(8, CY, W)

    loop(2, pool)

    loop(14, lambda i: taps_to_lanes(co, 1 + i, v3m, i, 0, CY))

    pre_mid = conv_rows(v3m, 0, 12, bm)
    sig_mid = jax.nn.sigmoid(pre_mid)
    own_mid = co[2:14].reshape(12 * CY, W)
    mid[2:14] = (own_mid + pre_mid * sig_mid).astype(BF).reshape(12, CY, W)
    ds_mid[2:14] = (sig_mid * (1.0 + pre_mid * (1.0 - sig_mid))).reshape(12, CY, W)

    def up(x):
        m = mid[pl.ds(2 + 6 * x, 6)].reshape(6 * CY, W)
        for i in range(2):
            for j in range(2):
                q = 2 * i + j
                lifted = dot(m, um[q * W : (q + 1) * W, :])
                for r in range(6):
                    row = 2 * (2 + 6 * x + r) + i
                    own = get_every_second(hid, row, j, EY // 2)
                    pre = own + lifted[r * CY : r * CY + EY // 2]
                    sig = jax.nn.sigmoid(pre)
                    put_every_second(skp, row, j, rounded(pre * sig))
                    put_every_second(ds_up, row, j, sig * (1.0 + pre * (1.0 - sig)))

    loop(2, up)

    loop(18, lambda i: taps_to_lanes(skp, 7 + i, v3s, i, 8, BY))
    loop(18, lambda i: put_row(skip_rows, i, get_row(skp, 7 + i)))

    loop(26, lambda i: taps_to_lanes(ce, 3 + i, v3c, i, 0, EY))

    def d_up(i):
        total = conv_t_rows(v3c, 12 * i, 12, bu)
        at = pl.ds(4 + 12 * i, 12)
        put_rows(dup, at, rounded(total.reshape(12, EY, W) * get_rows(ds_up, at)))

    loop(2, d_up)

    cot_t = cc[...].reshape(BX * BY, W).astype(F32).T.astype(BF)
    fold = repeat_matrix(32, W, 32, 0)
    fold_mid = repeat_matrix(64, W, 64, 0)

    def fold_to(matrix, hi, lo, tile, count):
        total = dot(matrix, hi[...], NT) + dot(matrix, lo[...], NT)
        for t in range(count):
            rows = matrix.shape[0]
            part = total[:, t * 128 : (t + 1) * 128]
            terms[(tile * 32 + t * rows) : (tile * 32 + (t + 1) * rows), :] = part.astype(BF)

    conv_weight_terms(cot_t, v3s, BX, 32, hi, lo, dsc)
    fold_to(fold, hi, lo, 7, 7)

    def own_parts(src, x):
        for i in range(2):
            for j in range(2):
                half = get_every_second(src, 8 + 2 * x + i, 8 + j, BY // 2)
                local[2 * i + j, x] = half.astype(BF)

    loop(8, lambda x: own_parts(dup, x))
    mid_t = mid[4:12].astype(F32)[:, 0:24][:, 4:20].reshape(128, W).T.astype(BF)

    def fold_four(tile):
        total = dot(fold_mid, him[0:256, :], NT) + dot(fold_mid, lom[0:256, :], NT)
        for t in range(2):
            rows = slice(tile * 32 + t * 64, tile * 32 + (t + 1) * 64)
            terms[rows, :] = total[:, t * 128 : (t + 1) * 128].astype(BF)

    def plain_terms(left, q, row):
        d = dot(left, local[q].reshape(128, W))
        for t in range(2):
            group = lax.broadcasted_iota(jnp.int32, (64, 128), 1) // 64
            low = d[(2 * t) * 64 : (2 * t + 1) * 64, t * 128 : (t + 1) * 128]
            high = d[(2 * t + 1) * 64 : (2 * t + 2) * 64, t * 128 : (t + 1) * 128]
            put_split(jnp.where(group == 0, low, high), him, lom, row, t * 128)

    for q in range(4):
        plain_terms(mid_t, q, 64 * q)
    fold_four(46)

    loop(12, lambda x: to_parts(dup, 2 + x))

    d_middle = None
    for q in range(4):
        part = dot(parts[q, 2:14].reshape(12 * CY, W), um[q * W : (q + 1) * W, :], NT)
        d_middle = part if d_middle is None else d_middle + part
    dmid[2:14] = rounded(d_middle * ds_mid[2:14].reshape(12 * CY, W)).reshape(12, CY, W)
    ds_mid[2:14] = d_middle.reshape(12, CY, W)

    loop(12, lambda i: taps_to_lanes(dmid, 2 + i, v3dm, i, 0, CY))

    def coarse_local(i):
        v = co[3 + i]
        for b in range(3):
            v3ml[i, :, b * W : (b + 1) * W] = v[3 + b : 19 + b].astype(BF)

    loop(10, coarse_local)
    dmid_t = dmid[4:12][:, 4:20].reshape(128, W).T.astype(BF)
    conv_weight_terms(dmid_t, v3ml, 8, 64, him, lom, dsc)
    fold_to(fold_mid, him, lom, 14, 14)

    d_coarse = ds_mid[3:13] + conv_t_rows(v3dm, 0, 10, bm).reshape(10, CY, W)
    ds_pool[3:13] = rounded(d_coarse * ds_pool[3:13])

    dp = ds_pool[3:13].reshape(10 * CY, W).astype(BF)
    for i in range(2):
        for j in range(2):
            q = 2 * i + j
            back = dot(dp, pm[q * W : (q + 1) * W, :], NT)
            for r in range(10):
                row = 2 * (3 + r) + i
                own = get_every_second(dup, row, j, EY // 2)
                d_hidden = own + back[r * CY : r * CY + EY // 2]
                slope = get_every_second(ds_down, row, j, EY // 2)
                put_every_second(ddn, row, j, rounded(d_hidden * slope))

    loop(18, lambda i: put_row(down_rows, i, get_row(ddn, 7 + i)))

    down_t = get_rows(ddn, slice(8, 24))[:, 8:40].reshape(BX * BY, W).T.astype(BF)
    conv_weight_terms(down_t, v3fl, BX, 32, hi, lo, dsc)
    fold_to(fold, hi, lo, 0, 7)

    loop(8, lambda x: own_parts(hid, x))
    pool_t = ds_pool[4:12][:, 4:20].reshape(128, W).T.astype(BF)
    for q in range(4):
        plain_terms(pool_t, q, 64 * q)
    fold_four(42)
    rest = terms.shape[0] - TILES * 32
    if rest > 0:
        terms[TILES * 32 :, :] = jnp.zeros((rest, 128), BF)


def finish_kernel(fc, cc, skip_rows, down_rows, bd, bu, out, gf, v3):
    loop(18, lambda i: taps_to_lanes(skip_rows, i, v3, i, 8, BY))
    total = conv_rows(v3, 0, BX, bu).reshape(BX, BY, W)
    out[...] = (fc[...].astype(F32) + total).astype(BF)
    loop(18, lambda i: taps_to_lanes(down_rows, i, v3, i, 8, BY))
    total = conv_t_rows(v3, 0, BX, bd).reshape(BX, BY, W)
    gf[...] = (cc[...].astype(F32) + total).astype(BF)


def finish_call(fields, cot, skip_rows, down_rows, bands):
    block = jax.ShapeDtypeStruct((BX, BY, W), BF)
    return pl.pallas_call(
        finish_kernel,
        out_shape=(block, block),
        scratch_shapes=[pltpu.VMEM((18, BY, 3 * W), BF)],
        compiler_params=pltpu.CompilerParams(vmem_limit_bytes=16 * 1024 * 1024),
        cost_estimate=pl.CostEstimate(flops=3 * 10**9, bytes_accessed=10**7, transcendentals=0),
        name="finish",
    )(fields, cot, skip_rows, down_rows, bands[0], bands[4])


def main_call(fields, cot, halos, bands, term_rows):
    some = jax.ShapeDtypeStruct((18, EY, W), BF)
    flat = pltpu.VMEM((2, EX * EY, 128), F32)
    split = pltpu.VMEM((2, EX, EY, 128), F32)
    coarse = pltpu.VMEM((CX, CY, W), F32)
    return pl.pallas_call(
        main_kernel,
        out_shape=(jax.ShapeDtypeStruct((term_rows, 128), BF), some, some),
        scratch_shapes=[flat] * 2
        + [split] * 6
        + [
            pltpu.VMEM((30, EY, 3 * W), BF),
            pltpu.VMEM((26, EY, 3 * W), BF),
            pltpu.VMEM((18, BY, 3 * W), BF),
            pltpu.VMEM((18, BY, 3 * W), BF),
            pltpu.VMEM((4, CX, CY, W), BF),
            coarse,
            pltpu.VMEM((CX, CY, W), BF),
            coarse,
            coarse,
            coarse,
            pltpu.VMEM((14, CY, 3 * W), BF),
            pltpu.VMEM((12, CY, 3 * W), BF),
            pltpu.VMEM((10, 16, 3 * W), BF),
            pltpu.VMEM((4, 8, 16, W), BF),
            pltpu.VMEM((28 * 32, W), BF),
            pltpu.VMEM((28 * 32, W), BF),
            pltpu.VMEM((28 * 64, W), BF),
            pltpu.VMEM((28 * 64, W), BF),
            pltpu.VMEM((W, 3 * W), F32),
        ],
        compiler_params=pltpu.CompilerParams(vmem_limit_bytes=36 * 1024 * 1024),
        cost_estimate=pl.CostEstimate(flops=10**10, bytes_accessed=10**7, transcendentals=10**6),
        name="network",
    )(fields, cot, *halos, *bands)


def unpack_kernel(
    terms, down, pool, mid, unpool, up, down_v, pool_v, mid_v, unpool_v, up_v, sems
):
    def send(k, src, dst):
        copy = pltpu.make_async_copy(src, dst, sems.at[k])
        copy.start()
        return copy

    copies = []
    for part in range(3):
        for u in range(9 * part, 9 * part + 9):
            row, lane = 14 * 32 + (u // 2) * 64, (u % 2) * 64
            mid_v[u] = terms[row : row + 64, lane : lane + 64].astype(F32)
        at = pl.ds(9 * part, 9)
        copies.append(send(part, mid_v.at[at], mid.at[at]))
    for first, src, dst in ((0, down_v, down), (224, up_v, up)):
        for u in range(27):
            row, lane = first + (u // 4) * 32, (u % 4) * 32
            src[u] = terms[row : row + 32, lane : lane + 32].astype(F32)
        copies.append(send(3 if first == 0 else 4, src, dst))
    for first, src, dst in ((42 * 32, pool_v, pool), (46 * 32, unpool_v, unpool)):
        for q in range(4):
            row, lane = first + (q // 2) * 64, (q % 2) * 64
            src[q] = terms[row : row + 64, lane : lane + 64].astype(F32)
        copies.append(send(5 if src is pool_v else 6, src, dst))
    for copy in copies:
        copy.wait()


def unpack(terms):
    shapes = ((27, 32, 32), (4, 64, 64), (27, 64, 64), (4, 64, 64), (27, 32, 32))
    return pl.pallas_call(
        unpack_kernel,
        out_shape=tuple(jax.ShapeDtypeStruct(s, F32) for s in shapes),
        in_specs=[pl.BlockSpec(memory_space=pltpu.VMEM)],
        out_specs=tuple(pl.BlockSpec(memory_space=pl.ANY) for _ in shapes),
        scratch_shapes=[pltpu.VMEM(s, F32) for s in shapes] + [pltpu.SemaphoreType.DMA((7,))],
        compiler_params=pltpu.CompilerParams(vmem_limit_bytes=8 * 1024 * 1024),
        name="unpack",
    )(terms)


def ring(axis, step):
    n = lax.axis_size(axis)
    return [(i, (i + step) % n) for i in range(n)]


def pack_kernel(fc, cc, first_x, last_x, first_y, last_y, wide):
    first_x[0:HF] = fc[0:HF]
    first_x[HF : HF + HC] = cc[0:HC]
    last_x[0:HF] = fc[BX - HF : BX]
    last_x[HF : HF + HC] = cc[BX - HC : BX]
    for src, count, at in ((fc, HF, 0), (cc, HC, HF)):
        for h in range(2):
            lanes = slice(h * 128, h * 128 + 128)
            wide[h] = src[:, :, lanes].reshape(BX * BY, 128).astype(F32)
        for c in range(count):
            for h in range(2):
                lanes = slice(h * 128, h * 128 + 128)
                column = wide[h, pl.ds(c, BX, stride=BY), :]
                first_y[at + c, :, lanes] = column.astype(BF)
                column = wide[h, pl.ds(BY - count + c, BX, stride=BY), :]
                last_y[at + c, :, lanes] = column.astype(BF)


def pack(fields, cot):
    rows = jax.ShapeDtypeStruct((HF + HC, BY, W), BF)
    columns = jax.ShapeDtypeStruct((HF + HC, BX, W), BF)
    return pl.pallas_call(
        pack_kernel,
        out_shape=(rows, rows, columns, columns),
        scratch_shapes=[pltpu.VMEM((2, BX * BY, 128), F32)],
        compiler_params=pltpu.CompilerParams(vmem_limit_bytes=8 * 1024 * 1024),
        name="pack",
    )(fields, cot)


def exchange(fields, cot):
    first_x, last_x, first_y, last_y = pack(fields, cot)
    ylo = lax.ppermute(last_y, "gy", ring("gy", 1))
    yhi = lax.ppermute(first_y, "gy", ring("gy", -1))
    xlo = lax.ppermute(last_x, "gx", ring("gx", 1))
    xhi = lax.ppermute(first_x, "gx", ring("gx", -1))
    last_c = jnp.concatenate([ylo[:, BX - 8 :], yhi[:, BX - 8 :]], axis=0)
    first_c = jnp.concatenate([ylo[:, :8], yhi[:, :8]], axis=0)
    clo = lax.ppermute(last_c, "gx", ring("gx", 1))
    chi = lax.ppermute(first_c, "gx", ring("gx", -1))
    return (xlo, xhi, ylo, yhi, clo, chi)


def reduce_groups(nx, ny):
    flat = lambda x, y: x * ny + y
    near = [[flat(x, 2 * z + e) for x in range(nx) for e in range(2)] for z in range(ny // 2)]
    far = [[flat(x, 2 * z + e) for z in range(ny // 2)] for x in range(nx) for e in range(2)]
    return near, far


def per_device(fields, w_down, w_pool, w_mid, w_unpool, w_up, cotangent):
    nx, ny = lax.axis_size("gx"), lax.axis_size("gy")
    near, far = reduce_groups(nx, ny)
    n1, n2 = len(near[0]), len(far[0])
    rows = -(-TILES * 32 // (8 * n1)) * 8
    bands = build_bands(w_down, w_pool, w_mid, w_unpool, w_up)
    halos = exchange(fields, cotangent)
    terms, skip_rows, down_rows = main_call(fields, cotangent, halos, bands, n1 * rows)
    swap = functools.partial(
        lax.all_to_all, axis_name=("gx", "gy"), split_axis=0, concat_axis=0, tiled=True
    )
    part = swap(terms.reshape(n1, rows, 128), axis_index_groups=near)
    output, grad_fields = finish_call(fields, cotangent, skip_rows, down_rows, bands)
    cells = fields.shape[0] * fields.shape[1] * 8 * nx * ny
    root = 1.0 / math.sqrt(math.sqrt(cells))
    part = (jnp.sum(part.astype(F32), axis=0) * root).astype(BF)
    part = swap(jnp.broadcast_to(part, (n2, rows, 128)), axis_index_groups=far).astype(F32)
    part = (jnp.sum(part, axis=0) * root).astype(BF)
    whole = swap(jnp.broadcast_to(part, (n1, rows, 128)), axis_index_groups=near)
    down, pool, mid, unpool, up = unpack(whole.reshape(n1 * rows, 128))
    return (
        output,
        grad_fields,
        down.reshape(w_down.shape),
        pool.reshape(w_pool.shape),
        mid.reshape(w_mid.shape),
        unpool.reshape(2, 2, 2, 32, 64).transpose(0, 1, 2, 4, 3),
        up.reshape(w_up.shape),
    )


def solution(mesh):
    placed = (P("gx", "gy", None), P(), P(), P(), P(), P(), P("gx", "gy", None))
    return jax.shard_map(
        per_device,
        mesh=mesh,
        in_specs=placed,
        out_specs=(P("gx", "gy", None), P("gx", "gy", None), P(), P(), P(), P(), P()),
        check_vma=False,
    )
```

```python
import functools
import math

import jax
import jax.numpy as jnp
from jax import lax
from jax.experimental import pallas as pl
from jax.experimental.pallas import tpu as pltpu
from jax.sharding import PartitionSpec as P

BF = jnp.bfloat16
F32 = jnp.float32
NN = (((1,), (0,)), ((), ()))
NT = (((1,), (1,)), ((), ()))
TN = (((0,), (0,)), ((), ()))

HF = 7
HC = 5
EX, EY = 32, 48
CX, CY = 16, 32
BX, BY = 16, 32
W = 256
TILES = 50


def dot(a, b, dims=NN):
    return lax.dot_general(a, b, dims, preferred_element_type=F32)


def rounded(v):
    return v.astype(BF).astype(F32)


MOST = 6


def loop(n, body, most=None):
    together = max(k for k in range(1, (most or MOST) + 1) if n % k == 0)

    def step(i, carry):
        for k in range(together):
            body(i * together + k)
        return carry

    if together == n:
        step(0, 0)
    else:
        lax.fori_loop(0, n // together, step, 0)


def aligned(at):
    return at if isinstance(at, int) else pl.multiple_of(at, 8)


def repeat_matrix(rows, cols, period, first):
    r = lax.broadcasted_iota(jnp.int32, (rows, cols), 0)
    c = lax.broadcasted_iota(jnp.int32, (rows, cols), 1)
    return (lax.rem(c, period) == r + first).astype(F32).astype(BF)


def bands_kernel(wd, wp, wm, wu, wup, bd, pm, bm, um, bu, wide, wide_mid):
    def band(w, out, wide, ch):
        planes = W // ch
        wide[...] = dot(w[...], repeat_matrix(ch, W, ch, 0))
        group = lax.broadcasted_iota(jnp.int32, (ch, W), 1) // ch

        def tap(t):
            base = t * 3 * ch if isinstance(t, int) else pl.multiple_of(t * 3 * ch, ch)
            t0 = wide[pl.ds(base, ch), :]
            t1 = wide[pl.ds(base + ch, ch), :]
            t2 = wide[pl.ds(base + 2 * ch, ch), :]
            for p in range(planes):
                rows = jnp.where(group == p, t1, 0.0)
                if p + 1 < planes:
                    rows = jnp.where(group == p + 1, t0, rows)
                if p > 0:
                    rows = jnp.where(group == p - 1, t2, rows)
                out[pl.ds(pl.multiple_of(t * W + p * ch, ch), ch), :] = rows.astype(BF)

        loop(9, tap, 3)

    band(wd, bd, wide, 32)
    band(wup, bu, wide, 32)
    band(wm, bm, wide_mid, 64)
    group = lax.broadcasted_iota(jnp.int32, (64, W), 1) // 64
    same = repeat_matrix(64, W, 64, 0)
    low = repeat_matrix(32, W, 64, 0)
    high = repeat_matrix(32, W, 64, 32)
    for q in range(4):
        pool = dot(wp[q], same)
        unpool = dot(wu[2 * q], low, TN) + dot(wu[2 * q + 1], high, TN)
        for y in range(4):
            rows = slice(q * W + y * 64, q * W + y * 64 + 64)
            pm[rows, :] = jnp.where(group == y, pool, 0.0).astype(BF)
            um[rows, :] = jnp.where(group == y, unpool, 0.0).astype(BF)


def build_bands(w_down, w_pool, w_mid, w_unpool, w_up):
    wide = jax.ShapeDtypeStruct((9 * W, W), BF)
    four = jax.ShapeDtypeStruct((4 * W, W), BF)
    return pl.pallas_call(
        bands_kernel,
        out_shape=(wide, four, wide, four, wide),
        scratch_shapes=[pltpu.VMEM((27 * 32, W), F32), pltpu.VMEM((27 * 64, W), F32)],
        compiler_params=pltpu.CompilerParams(vmem_limit_bytes=24 * 1024 * 1024),
        cost_estimate=pl.CostEstimate(flops=2 * 10**9, bytes_accessed=8 * 10**6, transcendentals=0),
        name="bands",
    )(
        w_down.reshape(27 * 32, 32),
        w_pool.reshape(4, 64, 64),
        w_mid.reshape(27 * 64, 64),
        w_unpool.transpose(0, 1, 2, 4, 3).reshape(8, 32, 64),
        w_up.reshape(27 * 32, 32),
    )


def get_row(src, row):
    if len(src.shape) == 3 and src.shape[2] == 128:
        at = pl.ds(aligned(row * EY), EY)
        return jnp.concatenate([src[0, at, :], src[1, at, :]], axis=1)
    if len(src.shape) == 3:
        return src[row]
    return jnp.concatenate([src[0, row], src[1, row]], axis=1)


def get_rows(src, rows):
    return jnp.concatenate([src[0, rows], src[1, rows]], axis=2)


def put_row(dst, row, value):
    dst[row] = value.astype(BF)


def put_rows(dst, rows, value):
    dst[0, rows] = value[..., 0:128]
    dst[1, rows] = value[..., 128:256]


def get_every_second(src, row, first, count):
    at = pl.ds(first, count, stride=2)
    return jnp.concatenate([src[0, row, at, :], src[1, row, at, :]], axis=1)


def put_every_second(dst, row, first, value):
    at = pl.ds(first, value.shape[0], stride=2)
    dst[0, row, at, :] = value[:, 0:128]
    dst[1, row, at, :] = value[:, 128:256]


def taps_to_lanes(src, row, out, at, lo, size):
    v = get_row(src, row).astype(F32)
    n = v.shape[0]
    out[at, :, 0:W] = pltpu.roll(v, 1, 0)[lo : lo + size].astype(BF)
    out[at, :, W : 2 * W] = v[lo : lo + size].astype(BF)
    out[at, :, 2 * W : 3 * W] = pltpu.roll(v, n - 1, 0)[lo : lo + size].astype(BF)


def conv_rows(v3, first, rows, band):
    total = None
    for a in range(3):
        piece = v3[pl.ds(first + a, rows)]
        piece = piece.reshape(rows * piece.shape[1], 3 * W)
        part = dot(piece, band[a * 3 * W : (a + 1) * 3 * W, :])
        total = part if total is None else total + part
    return total


def conv_t_rows(v3, first, rows, band):
    total = None
    for a in range(3):
        piece = v3[pl.ds(first + a, rows)]
        piece = piece.reshape(rows * piece.shape[1], 3 * W)
        for b in range(3):
            tap = (2 - a) * 3 + (2 - b)
            part = dot(piece[:, b * W : (b + 1) * W], band[tap * W : (tap + 1) * W, :], NT)
            total = part if total is None else total + part
    return total


def pick(d, lanes, shift, ch, width):
    group = lax.broadcasted_iota(jnp.int32, (ch, 128), 1) // ch
    p0 = (lanes % width) // ch
    out = jnp.zeros((ch, 128), F32)
    for g in range(128 // ch):
        z = p0 + g - shift
        if 0 <= z < W // ch:
            out = jnp.where(group == g, d[z * ch : (z + 1) * ch, lanes : lanes + 128], out)
    return out


def put_split(value, hi, lo, row, lanes):
    top = value.astype(BF)
    hi[row : row + value.shape[0], lanes : lanes + 128] = top
    lo[row : row + value.shape[0], lanes : lanes + 128] = (value - top.astype(F32)).astype(BF)


def conv_weight_terms(dout_t, v3, rows, ch, hi, lo, dsc):
    units = 27 * ch
    pad = hi.shape[0] - units
    hi[units:, :] = jnp.zeros((pad, W), BF)
    lo[units:, :] = jnp.zeros((pad, W), BF)
    for a in range(3):
        piece = v3[a : a + rows]
        piece = piece.reshape(rows * piece.shape[1], 3 * W)
        dsc[...] = dot(dout_t, piece)
        for b in range(3):
            for k in range(3):
                unit = (a * 3 + b) * 3 + k
                for t in range(2):
                    value = pick(dsc, b * W + t * 128, k - 1, ch, W)
                    put_split(value, hi, lo, unit * ch, t * 128)


def main_kernel(
    fc, cc, xlo, xhi, ylo, yhi, clo, chi, bd, pm, bm, um, bu,
    terms, skip_rows, down_rows,
    fe, ce, hid, ds_down, skp, ds_up, dup, ddn,
    v3f, v3c, v3fl, v3s,
    parts, co, mid, ds_pool, ds_mid, dmid, v3m, v3dm, v3ml, local,
    hi, lo, him, lom, dsc,
):
    def gather(dst, count, center, off):
        def put(row, value):
            at = pl.ds(aligned(row * EY + 8), BY)
            dst[0, at, :] = value[:, 0:128]
            dst[1, at, :] = value[:, 128:256]

        loop(BX, lambda i: put(8 + i, center[i].astype(F32)))

        def edge(i):
            put(8 - count + i, xlo[off + i].astype(F32))
            put(24 + i, xhi[off + i].astype(F32))

        loop(count, edge)
        for c in range(count):
            for side, y, other in ((ylo, 8 - count + c, 0), (yhi, 40 + c, HF + HC)):
                column = jnp.concatenate(
                    [
                        clo[other + off + c].astype(F32),
                        side[off + c].astype(F32),
                        chi[other + off + c].astype(F32),
                    ],
                    axis=0,
                )
                for h in range(2):
                    dst[h, pl.ds(y, EX, stride=EY), :] = column[:, h * 128 : h * 128 + 128]

    gather(fe, HF, fc, 0)
    gather(ce, HC, cc, HF)

    loop(30, lambda i: taps_to_lanes(fe, 1 + i, v3f, i, 0, EY))
    loop(18, lambda i: taps_to_lanes(fe, 7 + i, v3fl, i, 8, BY))
    zero = jnp.zeros((2, EY, W), F32)
    put_rows(hid, slice(0, 2), zero)
    put_rows(hid, slice(30, 32), zero)

    def down(i):
        pre = conv_rows(v3f, 14 * i, 14, bd)
        sig = jax.nn.sigmoid(pre)
        at = pl.ds(2 + 14 * i, 14)
        put_rows(hid, at, rounded(pre * sig).reshape(14, EY, W))
        put_rows(ds_down, at, (sig * (1.0 + pre * (1.0 - sig))).reshape(14, EY, W))

    loop(2, down, 1)

    pad = jnp.zeros((CY - EY // 2, W), F32)

    def to_parts(src, x):
        for i in range(2):
            for j in range(2):
                half = get_every_second(src, 2 * x + i, j, EY // 2)
                parts[2 * i + j, x] = jnp.concatenate([half, pad], axis=0).astype(BF)

    loop(CX, lambda x: to_parts(hid, x))

    def pool(i):
        pre = None
        for q in range(4):
            piece = parts[q, pl.ds(8 * i, 8)].reshape(8 * CY, W)
            part = dot(piece, pm[q * W : (q + 1) * W, :])
            pre = part if pre is None else pre + part
        sig = jax.nn.sigmoid(pre)
        co[pl.ds(8 * i, 8)] = rounded(pre * sig).reshape(8, CY, W)
        ds_pool[pl.ds(8 * i, 8)] = (sig * (1.0 + pre * (1.0 - sig))).reshape(8, CY, W)

    loop(2, pool, 1)

    loop(14, lambda i: taps_to_lanes(co, 1 + i, v3m, i, 0, CY))

    pre_mid = conv_rows(v3m, 0, 12, bm)
    sig_mid = jax.nn.sigmoid(pre_mid)
    own_mid = co[2:14].reshape(12 * CY, W)
    mid[2:14] = (own_mid + pre_mid * sig_mid).astype(BF).reshape(12, CY, W)
    ds_mid[2:14] = (sig_mid * (1.0 + pre_mid * (1.0 - sig_mid))).reshape(12, CY, W)

    def up(x):
        m = mid[pl.ds(2 + 6 * x, 6)].reshape(6 * CY, W)
        for i in range(2):
            for j in range(2):
                q = 2 * i + j
                lifted = dot(m, um[q * W : (q + 1) * W, :])
                for r in range(6):
                    row = 2 * (2 + 6 * x + r) + i
                    own = get_every_second(hid, row, j, EY // 2)
                    pre = own + lifted[r * CY : r * CY + EY // 2]
                    sig = jax.nn.sigmoid(pre)
                    put_every_second(skp, row, j, rounded(pre * sig))
                    put_every_second(ds_up, row, j, sig * (1.0 + pre * (1.0 - sig)))

    loop(2, up, 1)

    loop(18, lambda i: taps_to_lanes(skp, 7 + i, v3s, i, 8, BY))
    loop(18, lambda i: put_row(skip_rows, i, get_row(skp, 7 + i)))

    loop(26, lambda i: taps_to_lanes(ce, 3 + i, v3c, i, 0, EY))

    def d_up(i):
        total = conv_t_rows(v3c, 12 * i, 12, bu)
        at = pl.ds(4 + 12 * i, 12)
        put_rows(dup, at, rounded(total.reshape(12, EY, W) * get_rows(ds_up, at)))

    loop(2, d_up, 1)

    cot_t = cc[...].reshape(BX * BY, W).astype(F32).T.astype(BF)
    fold = repeat_matrix(32, W, 32, 0)
    fold_mid = repeat_matrix(64, W, 64, 0)

    def fold_to(matrix, hi, lo, tile, count):
        total = dot(matrix, hi[...], NT) + dot(matrix, lo[...], NT)
        for t in range(count):
            rows = matrix.shape[0]
            part = total[:, t * 128 : (t + 1) * 128]
            terms[(tile * 32 + t * rows) : (tile * 32 + (t + 1) * rows), :] = part.astype(BF)

    conv_weight_terms(cot_t, v3s, BX, 32, hi, lo, dsc)
    fold_to(fold, hi, lo, 7, 7)

    def own_parts(src, x):
        for i in range(2):
            for j in range(2):
                half = get_every_second(src, 8 + 2 * x + i, 8 + j, BY // 2)
                local[2 * i + j, x] = half.astype(BF)

    loop(8, lambda x: own_parts(dup, x))
    mid_t = mid[4:12].astype(F32)[:, 0:24][:, 4:20].reshape(128, W).T.astype(BF)

    def fold_four(tile):
        total = dot(fold_mid, him[0:256, :], NT) + dot(fold_mid, lom[0:256, :], NT)
        for t in range(2):
            rows = slice(tile * 32 + t * 64, tile * 32 + (t + 1) * 64)
            terms[rows, :] = total[:, t * 128 : (t + 1) * 128].astype(BF)

    def plain_terms(left, q, row):
        d = dot(left, local[q].reshape(128, W))
        for t in range(2):
            group = lax.broadcasted_iota(jnp.int32, (64, 128), 1) // 64
            low = d[(2 * t) * 64 : (2 * t + 1) * 64, t * 128 : (t + 1) * 128]
            high = d[(2 * t + 1) * 64 : (2 * t + 2) * 64, t * 128 : (t + 1) * 128]
            put_split(jnp.where(group == 0, low, high), him, lom, row, t * 128)

    for q in range(4):
        plain_terms(mid_t, q, 64 * q)
    fold_four(46)

    loop(12, lambda x: to_parts(dup, 2 + x))

    d_middle = None
    for q in range(4):
        part = dot(parts[q, 2:14].reshape(12 * CY, W), um[q * W : (q + 1) * W, :], NT)
        d_middle = part if d_middle is None else d_middle + part
    dmid[2:14] = rounded(d_middle * ds_mid[2:14].reshape(12 * CY, W)).reshape(12, CY, W)
    ds_mid[2:14] = d_middle.reshape(12, CY, W)

    loop(12, lambda i: taps_to_lanes(dmid, 2 + i, v3dm, i, 0, CY))

    def coarse_local(i):
        v = co[3 + i]
        for b in range(3):
            v3ml[i, :, b * W : (b + 1) * W] = v[3 + b : 19 + b].astype(BF)

    loop(10, coarse_local)
    dmid_t = dmid[4:12][:, 4:20].reshape(128, W).T.astype(BF)
    conv_weight_terms(dmid_t, v3ml, 8, 64, him, lom, dsc)
    fold_to(fold_mid, him, lom, 14, 14)

    d_coarse = ds_mid[3:13] + conv_t_rows(v3dm, 0, 10, bm).reshape(10, CY, W)
    ds_pool[3:13] = rounded(d_coarse * ds_pool[3:13])

    dp = ds_pool[3:13].reshape(10 * CY, W).astype(BF)
    for i in range(2):
        for j in range(2):
            q = 2 * i + j
            back = dot(dp, pm[q * W : (q + 1) * W, :], NT)
            for r in range(10):
                row = 2 * (3 + r) + i
                own = get_every_second(dup, row, j, EY // 2)
                d_hidden = own + back[r * CY : r * CY + EY // 2]
                slope = get_every_second(ds_down, row, j, EY // 2)
                put_every_second(ddn, row, j, rounded(d_hidden * slope))

    loop(18, lambda i: put_row(down_rows, i, get_row(ddn, 7 + i)))

    down_t = get_rows(ddn, slice(8, 24))[:, 8:40].reshape(BX * BY, W).T.astype(BF)
    conv_weight_terms(down_t, v3fl, BX, 32, hi, lo, dsc)
    fold_to(fold, hi, lo, 0, 7)

    loop(8, lambda x: own_parts(hid, x))
    pool_t = ds_pool[4:12][:, 4:20].reshape(128, W).T.astype(BF)
    for q in range(4):
        plain_terms(pool_t, q, 64 * q)
    fold_four(42)
    rest = terms.shape[0] - TILES * 32
    if rest > 0:
        terms[TILES * 32 :, :] = jnp.zeros((rest, 128), BF)


def finish_kernel(fc, cc, skip_rows, down_rows, bd, bu, out, gf, v3):
    loop(18, lambda i: taps_to_lanes(skip_rows, i, v3, i, 8, BY))
    total = conv_rows(v3, 0, BX, bu).reshape(BX, BY, W)
    out[...] = (fc[...].astype(F32) + total).astype(BF)
    loop(18, lambda i: taps_to_lanes(down_rows, i, v3, i, 8, BY))
    total = conv_t_rows(v3, 0, BX, bd).reshape(BX, BY, W)
    gf[...] = (cc[...].astype(F32) + total).astype(BF)


def finish_call(fields, cot, skip_rows, down_rows, bands):
    block = jax.ShapeDtypeStruct((BX, BY, W), BF)
    return pl.pallas_call(
        finish_kernel,
        out_shape=(block, block),
        scratch_shapes=[pltpu.VMEM((18, BY, 3 * W), BF)],
        compiler_params=pltpu.CompilerParams(vmem_limit_bytes=16 * 1024 * 1024),
        cost_estimate=pl.CostEstimate(flops=3 * 10**9, bytes_accessed=10**7, transcendentals=0),
        name="finish",
    )(fields, cot, skip_rows, down_rows, bands[0], bands[4])


def main_call(fields, cot, halos, bands, term_rows):
    some = jax.ShapeDtypeStruct((18, EY, W), BF)
    flat = pltpu.VMEM((2, EX * EY, 128), F32)
    split = pltpu.VMEM((2, EX, EY, 128), F32)
    coarse = pltpu.VMEM((CX, CY, W), F32)
    return pl.pallas_call(
        main_kernel,
        out_shape=(jax.ShapeDtypeStruct((term_rows, 128), BF), some, some),
        scratch_shapes=[flat] * 2
        + [split] * 6
        + [
            pltpu.VMEM((30, EY, 3 * W), BF),
            pltpu.VMEM((26, EY, 3 * W), BF),
            pltpu.VMEM((18, BY, 3 * W), BF),
            pltpu.VMEM((18, BY, 3 * W), BF),
            pltpu.VMEM((4, CX, CY, W), BF),
            coarse,
            pltpu.VMEM((CX, CY, W), BF),
            coarse,
            coarse,
            coarse,
            pltpu.VMEM((14, CY, 3 * W), BF),
            pltpu.VMEM((12, CY, 3 * W), BF),
            pltpu.VMEM((10, 16, 3 * W), BF),
            pltpu.VMEM((4, 8, 16, W), BF),
            pltpu.VMEM((28 * 32, W), BF),
            pltpu.VMEM((28 * 32, W), BF),
            pltpu.VMEM((28 * 64, W), BF),
            pltpu.VMEM((28 * 64, W), BF),
            pltpu.VMEM((W, 3 * W), F32),
        ],
        compiler_params=pltpu.CompilerParams(vmem_limit_bytes=36 * 1024 * 1024),
        cost_estimate=pl.CostEstimate(flops=10**10, bytes_accessed=10**7, transcendentals=10**6),
        name="network",
    )(fields, cot, *halos, *bands)


def unpack_kernel(
    terms, down, pool, mid, unpool, up, down_v, pool_v, mid_v, unpool_v, up_v, sems
):
    def send(k, src, dst):
        copy = pltpu.make_async_copy(src, dst, sems.at[k])
        copy.start()
        return copy

    copies = []
    for part in range(3):
        for u in range(9 * part, 9 * part + 9):
            row, lane = 14 * 32 + (u // 2) * 64, (u % 2) * 64
            mid_v[u] = terms[row : row + 64, lane : lane + 64].astype(F32)
        at = pl.ds(9 * part, 9)
        copies.append(send(part, mid_v.at[at], mid.at[at]))
    for first, src, dst in ((0, down_v, down), (224, up_v, up)):
        for u in range(27):
            row, lane = first + (u // 4) * 32, (u % 4) * 32
            src[u] = terms[row : row + 32, lane : lane + 32].astype(F32)
        copies.append(send(3 if first == 0 else 4, src, dst))
    for first, src, dst in ((42 * 32, pool_v, pool), (46 * 32, unpool_v, unpool)):
        for q in range(4):
            row, lane = first + (q // 2) * 64, (q % 2) * 64
            src[q] = terms[row : row + 64, lane : lane + 64].astype(F32)
        copies.append(send(5 if src is pool_v else 6, src, dst))
    for copy in copies:
        copy.wait()


def unpack(terms):
    shapes = ((27, 32, 32), (4, 64, 64), (27, 64, 64), (4, 64, 64), (27, 32, 32))
    return pl.pallas_call(
        unpack_kernel,
        out_shape=tuple(jax.ShapeDtypeStruct(s, F32) for s in shapes),
        in_specs=[pl.BlockSpec(memory_space=pltpu.VMEM)],
        out_specs=tuple(pl.BlockSpec(memory_space=pl.ANY) for _ in shapes),
        scratch_shapes=[pltpu.VMEM(s, F32) for s in shapes] + [pltpu.SemaphoreType.DMA((7,))],
        compiler_params=pltpu.CompilerParams(vmem_limit_bytes=8 * 1024 * 1024),
        name="unpack",
    )(terms)


def ring(axis, step):
    n = lax.axis_size(axis)
    return [(i, (i + step) % n) for i in range(n)]


def pack_kernel(fc, cc, first_x, last_x, first_y, last_y, side, wide, sems):
    copies = []

    def fetch(src, dst):
        copy = pltpu.make_async_copy(src, dst, sems.at[len(copies)])
        copy.start()
        copies.append(copy)

    for k, src in enumerate((fc, cc)):
        fetch(src.at[:, 0:16], side.at[2 * k])
        fetch(src.at[:, BY - 16 : BY], side.at[2 * k + 1])
    for src, count, at in ((fc, HF, 0), (cc, HC, HF)):
        fetch(src.at[0:count], first_x.at[at : at + count])
        fetch(src.at[BX - count : BX], last_x.at[at : at + count])
    for copy in copies[:4]:
        copy.wait()
    for k, (count, at) in enumerate(((HF, 0), (HC, HF))):
        for e, (out, first) in enumerate(((first_y, 0), (last_y, 16 - count))):
            for h in range(2):
                lanes = slice(h * 128, h * 128 + 128)
                wide[h] = side[2 * k + e, :, :, lanes].reshape(BX * 16, 128).astype(F32)
            for c in range(count):
                for h in range(2):
                    lanes = slice(h * 128, h * 128 + 128)
                    column = wide[h, pl.ds(first + c, BX, stride=16), :]
                    out[at + c, :, lanes] = column.astype(BF)
    for copy in copies[4:]:
        copy.wait()


def pack(fields, cot):
    rows = jax.ShapeDtypeStruct((HF + HC, BY, W), BF)
    columns = jax.ShapeDtypeStruct((HF + HC, BX, W), BF)
    return pl.pallas_call(
        pack_kernel,
        out_shape=(rows, rows, columns, columns),
        in_specs=[pl.BlockSpec(memory_space=pl.ANY)] * 2,
        scratch_shapes=[
            pltpu.VMEM((4, BX, 16, W), BF),
            pltpu.VMEM((2, BX * 16, 128), F32),
            pltpu.SemaphoreType.DMA((8,)),
        ],
        compiler_params=pltpu.CompilerParams(vmem_limit_bytes=56 * 1024 * 1024),
        name="pack",
    )(fields, cot)


def exchange(fields, cot):
    first_x, last_x, first_y, last_y = pack(fields, cot)
    ylo = lax.ppermute(last_y, "gy", ring("gy", 1))
    yhi = lax.ppermute(first_y, "gy", ring("gy", -1))
    xlo = lax.ppermute(last_x, "gx", ring("gx", 1))
    xhi = lax.ppermute(first_x, "gx", ring("gx", -1))
    last_c = jnp.concatenate([ylo[:, BX - 8 :], yhi[:, BX - 8 :]], axis=0)
    first_c = jnp.concatenate([ylo[:, :8], yhi[:, :8]], axis=0)
    clo = lax.ppermute(last_c, "gx", ring("gx", 1))
    chi = lax.ppermute(first_c, "gx", ring("gx", -1))
    return (xlo, xhi, ylo, yhi, clo, chi)


def reduce_groups(nx, ny):
    flat = lambda x, y: x * ny + y
    near = [[flat(x, 2 * z + e) for x in range(nx) for e in range(2)] for z in range(ny // 2)]
    far = [[flat(x, 2 * z + e) for z in range(ny // 2)] for x in range(nx) for e in range(2)]
    return near, far


def per_device(fields, w_down, w_pool, w_mid, w_unpool, w_up, cotangent):
    nx, ny = lax.axis_size("gx"), lax.axis_size("gy")
    near, far = reduce_groups(nx, ny)
    n1, n2 = len(near[0]), len(far[0])
    rows = -(-TILES * 32 // (8 * n1)) * 8
    bands = build_bands(w_down, w_pool, w_mid, w_unpool, w_up)
    halos = exchange(fields, cotangent)
    terms, skip_rows, down_rows = main_call(fields, cotangent, halos, bands, n1 * rows)
    swap = functools.partial(
        lax.all_to_all, axis_name=("gx", "gy"), split_axis=0, concat_axis=0, tiled=True
    )
    part = swap(terms.reshape(n1, rows, 128), axis_index_groups=near)
    output, grad_fields = finish_call(fields, cotangent, skip_rows, down_rows, bands)
    cells = fields.shape[0] * fields.shape[1] * 8 * nx * ny
    root = 1.0 / math.sqrt(math.sqrt(cells))
    part = (jnp.sum(part.astype(F32), axis=0) * root).astype(BF)
    part = swap(jnp.broadcast_to(part, (n2, rows, 128)), axis_index_groups=far).astype(F32)
    part = (jnp.sum(part, axis=0) * root).astype(BF)
    whole = swap(jnp.broadcast_to(part, (n1, rows, 128)), axis_index_groups=near)
    down, pool, mid, unpool, up = unpack(whole.reshape(n1 * rows, 128))
    return (
        output,
        grad_fields,
        down.reshape(w_down.shape),
        pool.reshape(w_pool.shape),
        mid.reshape(w_mid.shape),
        unpool.reshape(2, 2, 2, 32, 64).transpose(0, 1, 2, 4, 3),
        up.reshape(w_up.shape),
    )


def solution(mesh):
    placed = (P("gx", "gy", None), P(), P(), P(), P(), P(), P("gx", "gy", None))
    return jax.shard_map(
        per_device,
        mesh=mesh,
        in_specs=placed,
        out_specs=(P("gx", "gy", None), P("gx", "gy", None), P(), P(), P(), P(), P()),
        check_vma=False,
    )
```

```python
import functools
import math

import jax
import jax.numpy as jnp
from jax import lax
from jax.experimental import pallas as pl
from jax.experimental.pallas import tpu as pltpu
from jax.sharding import PartitionSpec as P

BF = jnp.bfloat16
F32 = jnp.float32
NN = (((1,), (0,)), ((), ()))
NT = (((1,), (1,)), ((), ()))
TN = (((0,), (0,)), ((), ()))

HF = 7
HC = 5
EX, EY = 32, 48
CX, CY = 16, 32
BX, BY = 16, 32
W = 256
TILES = 50


def dot(a, b, dims=NN):
    return lax.dot_general(a, b, dims, preferred_element_type=F32)


def rounded(v):
    return v.astype(BF).astype(F32)


DOWN, D_UP, UP = 7, 6, 3
MOST = 64


def loop(n, body, most=None):
    together = max(k for k in range(1, (most or MOST) + 1) if n % k == 0)

    def step(i, carry):
        for k in range(together):
            body(i * together + k)
        return carry

    if together == n:
        step(0, 0)
    else:
        lax.fori_loop(0, n // together, step, 0)


def aligned(at):
    return at if isinstance(at, int) else pl.multiple_of(at, 8)


def repeat_matrix(rows, cols, period, first):
    r = lax.broadcasted_iota(jnp.int32, (rows, cols), 0)
    c = lax.broadcasted_iota(jnp.int32, (rows, cols), 1)
    return (lax.rem(c, period) == r + first).astype(F32).astype(BF)


def bands_kernel(wd, wp, wm, wu, wup, bd, pm, bm, um, bu, wide, wide_mid):
    def band(w, out, wide, ch):
        planes = W // ch
        wide[...] = dot(w[...], repeat_matrix(ch, W, ch, 0))
        group = lax.broadcasted_iota(jnp.int32, (ch, W), 1) // ch

        def tap(t):
            base = t * 3 * ch if isinstance(t, int) else pl.multiple_of(t * 3 * ch, ch)
            t0 = wide[pl.ds(base, ch), :]
            t1 = wide[pl.ds(base + ch, ch), :]
            t2 = wide[pl.ds(base + 2 * ch, ch), :]
            for p in range(planes):
                rows = jnp.where(group == p, t1, 0.0)
                if p + 1 < planes:
                    rows = jnp.where(group == p + 1, t0, rows)
                if p > 0:
                    rows = jnp.where(group == p - 1, t2, rows)
                out[pl.ds(pl.multiple_of(t * W + p * ch, ch), ch), :] = rows.astype(BF)

        loop(9, tap)

    band(wd, bd, wide, 32)
    band(wup, bu, wide, 32)
    band(wm, bm, wide_mid, 64)
    group = lax.broadcasted_iota(jnp.int32, (64, W), 1) // 64
    same = repeat_matrix(64, W, 64, 0)
    low = repeat_matrix(32, W, 64, 0)
    high = repeat_matrix(32, W, 64, 32)
    for q in range(4):
        pool = dot(wp[q], same)
        unpool = dot(wu[2 * q], low, TN) + dot(wu[2 * q + 1], high, TN)
        for y in range(4):
            rows = slice(q * W + y * 64, q * W + y * 64 + 64)
            pm[rows, :] = jnp.where(group == y, pool, 0.0).astype(BF)
            um[rows, :] = jnp.where(group == y, unpool, 0.0).astype(BF)


def build_bands(w_down, w_pool, w_mid, w_unpool, w_up):
    wide = jax.ShapeDtypeStruct((9 * W, W), BF)
    four = jax.ShapeDtypeStruct((4 * W, W), BF)
    return pl.pallas_call(
        bands_kernel,
        out_shape=(wide, four, wide, four, wide),
        scratch_shapes=[pltpu.VMEM((27 * 32, W), F32), pltpu.VMEM((27 * 64, W), F32)],
        compiler_params=pltpu.CompilerParams(vmem_limit_bytes=24 * 1024 * 1024),
        cost_estimate=pl.CostEstimate(flops=2 * 10**9, bytes_accessed=8 * 10**6, transcendentals=0),
        name="bands",
    )(
        w_down.reshape(27 * 32, 32),
        w_pool.reshape(4, 64, 64),
        w_mid.reshape(27 * 64, 64),
        w_unpool.transpose(0, 1, 2, 4, 3).reshape(8, 32, 64),
        w_up.reshape(27 * 32, 32),
    )


def get_row(src, row):
    if len(src.shape) == 3 and src.shape[2] == 128:
        at = pl.ds(aligned(row * EY), EY)
        return jnp.concatenate([src[0, at, :], src[1, at, :]], axis=1)
    if len(src.shape) == 3:
        return src[row]
    return jnp.concatenate([src[0, row], src[1, row]], axis=1)


def get_rows(src, rows):
    return jnp.concatenate([src[0, rows], src[1, rows]], axis=2)


def put_row(dst, row, value):
    dst[row] = value.astype(BF)


def put_rows(dst, rows, value):
    dst[0, rows] = value[..., 0:128]
    dst[1, rows] = value[..., 128:256]


def get_every_second(src, row, first, count):
    at = pl.ds(first, count, stride=2)
    return jnp.concatenate([src[0, row, at, :], src[1, row, at, :]], axis=1)


def put_every_second(dst, row, first, value):
    at = pl.ds(first, value.shape[0], stride=2)
    dst[0, row, at, :] = value[:, 0:128]
    dst[1, row, at, :] = value[:, 128:256]


def taps_to_lanes(src, row, out, at, lo, size):
    v = get_row(src, row).astype(F32)
    n = v.shape[0]
    out[at, :, 0:W] = pltpu.roll(v, 1, 0)[lo : lo + size].astype(BF)
    out[at, :, W : 2 * W] = v[lo : lo + size].astype(BF)
    out[at, :, 2 * W : 3 * W] = pltpu.roll(v, n - 1, 0)[lo : lo + size].astype(BF)


def conv_rows(v3, first, rows, band):
    total = None
    for a in range(3):
        piece = v3[pl.ds(first + a, rows)]
        piece = piece.reshape(rows * piece.shape[1], 3 * W)
        part = dot(piece, band[a * 3 * W : (a + 1) * 3 * W, :])
        total = part if total is None else total + part
    return total


def conv_t_rows(v3, first, rows, band):
    total = None
    for a in range(3):
        piece = v3[pl.ds(first + a, rows)]
        piece = piece.reshape(rows * piece.shape[1], 3 * W)
        for b in range(3):
            tap = (2 - a) * 3 + (2 - b)
            part = dot(piece[:, b * W : (b + 1) * W], band[tap * W : (tap + 1) * W, :], NT)
            total = part if total is None else total + part
    return total


def pick(d, lanes, shift, ch, width):
    group = lax.broadcasted_iota(jnp.int32, (ch, 128), 1) // ch
    p0 = (lanes % width) // ch
    out = jnp.zeros((ch, 128), F32)
    for g in range(128 // ch):
        z = p0 + g - shift
        if 0 <= z < W // ch:
            out = jnp.where(group == g, d[z * ch : (z + 1) * ch, lanes : lanes + 128], out)
    return out


def put_split(value, hi, lo, row, lanes):
    top = value.astype(BF)
    hi[row : row + value.shape[0], lanes : lanes + 128] = top
    lo[row : row + value.shape[0], lanes : lanes + 128] = (value - top.astype(F32)).astype(BF)


def conv_weight_terms(dout_t, v3, rows, ch, hi, lo, dsc):
    units = 27 * ch
    pad = hi.shape[0] - units
    hi[units:, :] = jnp.zeros((pad, W), BF)
    lo[units:, :] = jnp.zeros((pad, W), BF)
    for a in range(3):
        piece = v3[a : a + rows]
        piece = piece.reshape(rows * piece.shape[1], 3 * W)
        dsc[...] = dot(dout_t, piece)
        for b in range(3):
            for k in range(3):
                unit = (a * 3 + b) * 3 + k
                for t in range(2):
                    value = pick(dsc, b * W + t * 128, k - 1, ch, W)
                    put_split(value, hi, lo, unit * ch, t * 128)


def main_kernel(
    fc, cc, xlo, xhi, ylo, yhi, clo, chi, bd, pm, bm, um, bu,
    terms, skip_rows, down_rows,
    fe, ce, hid, ds_down, skp, dup, ddn,
    v3f, v3c, v3fl, v3s,
    parts, d_parts, co, mid, ds_pool, ds_mid, dmid, v3m, v3dm, v3ml,
    hi, lo, him, lom, dsc,
):
    def gather(dst, count, center, off):
        def put(row, value):
            at = pl.ds(aligned(row * EY + 8), BY)
            dst[0, at, :] = value[:, 0:128]
            dst[1, at, :] = value[:, 128:256]

        loop(BX, lambda i: put(8 + i, center[i].astype(F32)))

        def edge(i):
            put(8 - count + i, xlo[off + i].astype(F32))
            put(24 + i, xhi[off + i].astype(F32))

        loop(count, edge)
        for c in range(count):
            for side, y, other in ((ylo, 8 - count + c, 0), (yhi, 40 + c, HF + HC)):
                column = jnp.concatenate(
                    [
                        clo[other + off + c].astype(F32),
                        side[off + c].astype(F32),
                        chi[other + off + c].astype(F32),
                    ],
                    axis=0,
                )
                for h in range(2):
                    dst[h, pl.ds(y, EX, stride=EY), :] = column[:, h * 128 : h * 128 + 128]

    gather(fe, HF, fc, 0)
    gather(ce, HC, cc, HF)

    loop(30, lambda i: taps_to_lanes(fe, 1 + i, v3f, i, 0, EY))
    loop(18, lambda i: taps_to_lanes(fe, 7 + i, v3fl, i, 8, BY))
    zero = jnp.zeros((2, EY, W), F32)
    put_rows(hid, slice(0, 2), zero)
    put_rows(hid, slice(30, 32), zero)

    def down(i):
        pre = conv_rows(v3f, DOWN * i, DOWN, bd)
        sig = jax.nn.sigmoid(pre)
        at = pl.ds(2 + DOWN * i, DOWN)
        put_rows(hid, at, rounded(pre * sig).reshape(DOWN, EY, W))
        put_rows(ds_down, at, (sig * (1.0 + pre * (1.0 - sig))).reshape(DOWN, EY, W))

    loop(28 // DOWN, down)

    loop(26, lambda i: taps_to_lanes(ce, 3 + i, v3c, i, 0, EY))

    def d_up(i):
        total = conv_t_rows(v3c, D_UP * i, D_UP, bu)
        put_rows(dup, pl.ds(4 + D_UP * i, D_UP), total.reshape(D_UP, EY, W))

    loop(24 // D_UP, d_up)

    pad = jnp.zeros((CY - EY // 2, W), F32)

    def to_parts(src, x):
        for i in range(2):
            for j in range(2):
                half = get_every_second(src, 2 * x + i, j, EY // 2)
                parts[2 * i + j, x] = jnp.concatenate([half, pad], axis=0).astype(BF)

    loop(CX, lambda x: to_parts(hid, x))

    def pool(i):
        pre = None
        for q in range(4):
            piece = parts[q, pl.ds(8 * i, 8)].reshape(8 * CY, W)
            part = dot(piece, pm[q * W : (q + 1) * W, :])
            pre = part if pre is None else pre + part
        sig = jax.nn.sigmoid(pre)
        co[pl.ds(8 * i, 8)] = rounded(pre * sig).reshape(8, CY, W)
        ds_pool[pl.ds(8 * i, 8)] = (sig * (1.0 + pre * (1.0 - sig))).reshape(8, CY, W)

    loop(2, pool)

    loop(14, lambda i: taps_to_lanes(co, 1 + i, v3m, i, 0, CY))

    pre_mid = conv_rows(v3m, 0, 12, bm)
    sig_mid = jax.nn.sigmoid(pre_mid)
    own_mid = co[2:14].reshape(12 * CY, W)
    mid[2:14] = (own_mid + pre_mid * sig_mid).astype(BF).reshape(12, CY, W)
    ds_mid[2:14] = (sig_mid * (1.0 + pre_mid * (1.0 - sig_mid))).reshape(12, CY, W)

    def up(x):
        m = mid[pl.ds(2 + UP * x, UP)].reshape(UP * CY, W)
        for i in range(2):
            for j in range(2):
                q = 2 * i + j
                lifted = dot(m, um[q * W : (q + 1) * W, :])
                for r in range(UP):
                    at = 2 + UP * x + r
                    own = parts[q, at].astype(F32)[0 : EY // 2]
                    pre = own + lifted[r * CY : r * CY + EY // 2]
                    sig = jax.nn.sigmoid(pre)
                    put_every_second(skp, 2 * at + i, j, rounded(pre * sig))
                    raw = get_every_second(dup, 2 * at + i, j, EY // 2)
                    d_up = raw * (sig * (1.0 + pre * (1.0 - sig)))
                    d_parts[q, at] = jnp.concatenate([d_up, pad], axis=0).astype(BF)

    loop(12 // UP, up)

    loop(18, lambda i: taps_to_lanes(skp, 7 + i, v3s, i, 8, BY))
    loop(18, lambda i: put_row(skip_rows, i, get_row(skp, 7 + i)))

    cot_t = cc[...].reshape(BX * BY, W).astype(F32).T.astype(BF)
    fold = repeat_matrix(32, W, 32, 0)
    fold_mid = repeat_matrix(64, W, 64, 0)

    def fold_to(matrix, hi, lo, tile, count):
        total = dot(matrix, hi[...], NT) + dot(matrix, lo[...], NT)
        for t in range(count):
            rows = matrix.shape[0]
            part = total[:, t * 128 : (t + 1) * 128]
            terms[(tile * 32 + t * rows) : (tile * 32 + (t + 1) * rows), :] = part.astype(BF)

    conv_weight_terms(cot_t, v3s, BX, 32, hi, lo, dsc)
    fold_to(fold, hi, lo, 7, 7)

    def own_parts(src, q):
        return src[q, 4:12].astype(F32)[:, 4:20].reshape(128, W).astype(BF)

    mid_t = mid[4:12].astype(F32)[:, 0:24][:, 4:20].reshape(128, W).T.astype(BF)

    def fold_four(tile):
        total = dot(fold_mid, him[0:256, :], NT) + dot(fold_mid, lom[0:256, :], NT)
        for t in range(2):
            rows = slice(tile * 32 + t * 64, tile * 32 + (t + 1) * 64)
            terms[rows, :] = total[:, t * 128 : (t + 1) * 128].astype(BF)

    def plain_terms(left, src, q, row):
        d = dot(left, own_parts(src, q))
        for t in range(2):
            group = lax.broadcasted_iota(jnp.int32, (64, 128), 1) // 64
            low = d[(2 * t) * 64 : (2 * t + 1) * 64, t * 128 : (t + 1) * 128]
            high = d[(2 * t + 1) * 64 : (2 * t + 2) * 64, t * 128 : (t + 1) * 128]
            put_split(jnp.where(group == 0, low, high), him, lom, row, t * 128)

    for q in range(4):
        plain_terms(mid_t, d_parts, q, 64 * q)
    fold_four(46)

    d_middle = None
    for q in range(4):
        part = dot(d_parts[q, 2:14].reshape(12 * CY, W), um[q * W : (q + 1) * W, :], NT)
        d_middle = part if d_middle is None else d_middle + part
    dmid[2:14] = rounded(d_middle * ds_mid[2:14].reshape(12 * CY, W)).reshape(12, CY, W)
    ds_mid[2:14] = d_middle.reshape(12, CY, W)

    loop(12, lambda i: taps_to_lanes(dmid, 2 + i, v3dm, i, 0, CY))

    def coarse_local(i):
        v = co[3 + i]
        for b in range(3):
            v3ml[i, :, b * W : (b + 1) * W] = v[3 + b : 19 + b].astype(BF)

    loop(10, coarse_local)
    dmid_t = dmid[4:12][:, 4:20].reshape(128, W).T.astype(BF)
    conv_weight_terms(dmid_t, v3ml, 8, 64, him, lom, dsc)
    fold_to(fold_mid, him, lom, 14, 14)

    d_coarse = ds_mid[3:13] + conv_t_rows(v3dm, 0, 10, bm).reshape(10, CY, W)
    ds_pool[3:13] = rounded(d_coarse * ds_pool[3:13])

    dp = ds_pool[3:13].reshape(10 * CY, W).astype(BF)
    for i in range(2):
        for j in range(2):
            q = 2 * i + j
            back = dot(dp, pm[q * W : (q + 1) * W, :], NT)
            for r in range(10):
                row = 2 * (3 + r) + i
                own = d_parts[q, 3 + r].astype(F32)[0 : EY // 2]
                d_hidden = own + back[r * CY : r * CY + EY // 2]
                slope = get_every_second(ds_down, row, j, EY // 2)
                put_every_second(ddn, row, j, rounded(d_hidden * slope))

    loop(18, lambda i: put_row(down_rows, i, get_row(ddn, 7 + i)))

    down_t = get_rows(ddn, slice(8, 24))[:, 8:40].reshape(BX * BY, W).T.astype(BF)
    conv_weight_terms(down_t, v3fl, BX, 32, hi, lo, dsc)
    fold_to(fold, hi, lo, 0, 7)

    pool_t = ds_pool[4:12][:, 4:20].reshape(128, W).T.astype(BF)
    for q in range(4):
        plain_terms(pool_t, parts, q, 64 * q)
    fold_four(42)
    rest = terms.shape[0] - TILES * 32
    if rest > 0:
        terms[TILES * 32 :, :] = jnp.zeros((rest, 128), BF)


def finish_kernel(fc, cc, skip_rows, down_rows, bd, bu, out, gf, v3):
    loop(18, lambda i: taps_to_lanes(skip_rows, i, v3, i, 8, BY))
    total = conv_rows(v3, 0, BX, bu).reshape(BX, BY, W)
    out[...] = (fc[...].astype(F32) + total).astype(BF)
    loop(18, lambda i: taps_to_lanes(down_rows, i, v3, i, 8, BY))
    total = conv_t_rows(v3, 0, BX, bd).reshape(BX, BY, W)
    gf[...] = (cc[...].astype(F32) + total).astype(BF)


def finish_call(fields, cot, skip_rows, down_rows, bands):
    block = jax.ShapeDtypeStruct((BX, BY, W), BF)
    return pl.pallas_call(
        finish_kernel,
        out_shape=(block, block),
        scratch_shapes=[pltpu.VMEM((18, BY, 3 * W), BF)],
        compiler_params=pltpu.CompilerParams(vmem_limit_bytes=16 * 1024 * 1024),
        cost_estimate=pl.CostEstimate(flops=3 * 10**9, bytes_accessed=10**7, transcendentals=0),
        name="finish",
    )(fields, cot, skip_rows, down_rows, bands[0], bands[4])


def main_call(fields, cot, halos, bands, term_rows):
    some = jax.ShapeDtypeStruct((18, EY, W), BF)
    flat = pltpu.VMEM((2, EX * EY, 128), F32)
    split = pltpu.VMEM((2, EX, EY, 128), F32)
    coarse = pltpu.VMEM((CX, CY, W), F32)
    return pl.pallas_call(
        main_kernel,
        out_shape=(jax.ShapeDtypeStruct((term_rows, 128), BF), some, some),
        scratch_shapes=[flat] * 2
        + [split] * 5
        + [
            pltpu.VMEM((30, EY, 3 * W), BF),
            pltpu.VMEM((26, EY, 3 * W), BF),
            pltpu.VMEM((18, BY, 3 * W), BF),
            pltpu.VMEM((18, BY, 3 * W), BF),
            pltpu.VMEM((4, CX, CY, W), BF),
            pltpu.VMEM((4, CX, CY, W), BF),
            coarse,
            pltpu.VMEM((CX, CY, W), BF),
            coarse,
            coarse,
            coarse,
            pltpu.VMEM((14, CY, 3 * W), BF),
            pltpu.VMEM((12, CY, 3 * W), BF),
            pltpu.VMEM((10, 16, 3 * W), BF),
            pltpu.VMEM((28 * 32, W), BF),
            pltpu.VMEM((28 * 32, W), BF),
            pltpu.VMEM((28 * 64, W), BF),
            pltpu.VMEM((28 * 64, W), BF),
            pltpu.VMEM((W, 3 * W), F32),
        ],
        compiler_params=pltpu.CompilerParams(vmem_limit_bytes=36 * 1024 * 1024),
        cost_estimate=pl.CostEstimate(flops=10**10, bytes_accessed=10**7, transcendentals=10**6),
        name="network",
    )(fields, cot, *halos, *bands)


def unpack_kernel(
    terms, down, pool, mid, unpool, up, down_v, pool_v, mid_v, unpool_v, up_v, sems
):
    def send(k, src, dst):
        copy = pltpu.make_async_copy(src, dst, sems.at[k])
        copy.start()
        return copy

    copies = []
    for part in range(3):
        for u in range(9 * part, 9 * part + 9):
            row, lane = 14 * 32 + (u // 2) * 64, (u % 2) * 64
            mid_v[u] = terms[row : row + 64, lane : lane + 64].astype(F32)
        at = pl.ds(9 * part, 9)
        copies.append(send(part, mid_v.at[at], mid.at[at]))
    for first, src, dst in ((0, down_v, down), (224, up_v, up)):
        for u in range(27):
            row, lane = first + (u // 4) * 32, (u % 4) * 32
            src[u] = terms[row : row + 32, lane : lane + 32].astype(F32)
        copies.append(send(3 if first == 0 else 4, src, dst))
    for first, src, dst in ((42 * 32, pool_v, pool), (46 * 32, unpool_v, unpool)):
        for q in range(4):
            row, lane = first + (q // 2) * 64, (q % 2) * 64
            src[q] = terms[row : row + 64, lane : lane + 64].astype(F32)
        copies.append(send(5 if src is pool_v else 6, src, dst))
    for copy in copies:
        copy.wait()


def unpack(terms):
    shapes = ((27, 32, 32), (4, 64, 64), (27, 64, 64), (4, 64, 64), (27, 32, 32))
    return pl.pallas_call(
        unpack_kernel,
        out_shape=tuple(jax.ShapeDtypeStruct(s, F32) for s in shapes),
        in_specs=[pl.BlockSpec(memory_space=pltpu.VMEM)],
        out_specs=tuple(pl.BlockSpec(memory_space=pl.ANY) for _ in shapes),
        scratch_shapes=[pltpu.VMEM(s, F32) for s in shapes] + [pltpu.SemaphoreType.DMA((7,))],
        compiler_params=pltpu.CompilerParams(vmem_limit_bytes=8 * 1024 * 1024),
        name="unpack",
    )(terms)


def ring(axis, step):
    n = lax.axis_size(axis)
    return [(i, (i + step) % n) for i in range(n)]


def pack_kernel(fc, cc, first_x, last_x, first_y, last_y, side, wide, sems):
    copies = []

    def fetch(src, dst):
        copy = pltpu.make_async_copy(src, dst, sems.at[len(copies)])
        copy.start()
        copies.append(copy)

    for k, src in enumerate((fc, cc)):
        fetch(src.at[:, 0:16], side.at[2 * k])
        fetch(src.at[:, BY - 16 : BY], side.at[2 * k + 1])
    for src, count, at in ((fc, HF, 0), (cc, HC, HF)):
        fetch(src.at[0:count], first_x.at[at : at + count])
        fetch(src.at[BX - count : BX], last_x.at[at : at + count])
    for copy in copies[:4]:
        copy.wait()
    for k, (count, at) in enumerate(((HF, 0), (HC, HF))):
        for e, (out, first) in enumerate(((first_y, 0), (last_y, 16 - count))):
            for h in range(2):
                lanes = slice(h * 128, h * 128 + 128)
                wide[h] = side[2 * k + e, :, :, lanes].reshape(BX * 16, 128).astype(F32)
            for c in range(count):
                for h in range(2):
                    lanes = slice(h * 128, h * 128 + 128)
                    column = wide[h, pl.ds(first + c, BX, stride=16), :]
                    out[at + c, :, lanes] = column.astype(BF)
    for copy in copies[4:]:
        copy.wait()


def pack(fields, cot):
    rows = jax.ShapeDtypeStruct((HF + HC, BY, W), BF)
    columns = jax.ShapeDtypeStruct((HF + HC, BX, W), BF)
    return pl.pallas_call(
        pack_kernel,
        out_shape=(rows, rows, columns, columns),
        in_specs=[pl.BlockSpec(memory_space=pl.ANY)] * 2,
        scratch_shapes=[
            pltpu.VMEM((4, BX, 16, W), BF),
            pltpu.VMEM((2, BX * 16, 128), F32),
            pltpu.SemaphoreType.DMA((8,)),
        ],
        compiler_params=pltpu.CompilerParams(vmem_limit_bytes=56 * 1024 * 1024),
        name="pack",
    )(fields, cot)


def exchange(fields, cot):
    first_x, last_x, first_y, last_y = pack(fields, cot)
    ylo = lax.ppermute(last_y, "gy", ring("gy", 1))
    yhi = lax.ppermute(first_y, "gy", ring("gy", -1))
    xlo = lax.ppermute(last_x, "gx", ring("gx", 1))
    xhi = lax.ppermute(first_x, "gx", ring("gx", -1))
    last_c = jnp.concatenate([ylo[:, BX - 8 :], yhi[:, BX - 8 :]], axis=0)
    first_c = jnp.concatenate([ylo[:, :8], yhi[:, :8]], axis=0)
    clo = lax.ppermute(last_c, "gx", ring("gx", 1))
    chi = lax.ppermute(first_c, "gx", ring("gx", -1))
    return (xlo, xhi, ylo, yhi, clo, chi)


def reduce_groups(nx, ny):
    flat = lambda x, y: x * ny + y
    near = [[flat(x, 2 * z + e) for x in range(nx) for e in range(2)] for z in range(ny // 2)]
    far = [[flat(x, 2 * z + e) for z in range(ny // 2)] for x in range(nx) for e in range(2)]
    return near, far


def per_device(fields, w_down, w_pool, w_mid, w_unpool, w_up, cotangent):
    nx, ny = lax.axis_size("gx"), lax.axis_size("gy")
    near, far = reduce_groups(nx, ny)
    n1, n2 = len(near[0]), len(far[0])
    rows = -(-TILES * 32 // (8 * n1)) * 8
    bands = build_bands(w_down, w_pool, w_mid, w_unpool, w_up)
    halos = exchange(fields, cotangent)
    terms, skip_rows, down_rows = main_call(fields, cotangent, halos, bands, n1 * rows)
    swap = functools.partial(
        lax.all_to_all, axis_name=("gx", "gy"), split_axis=0, concat_axis=0, tiled=True
    )
    part = swap(terms.reshape(n1, rows, 128), axis_index_groups=near)
    output, grad_fields = finish_call(fields, cotangent, skip_rows, down_rows, bands)
    cells = fields.shape[0] * fields.shape[1] * 8 * nx * ny
    root = 1.0 / math.sqrt(math.sqrt(cells))
    part = (jnp.sum(part.astype(F32), axis=0) * root).astype(BF)
    part = swap(jnp.broadcast_to(part, (n2, rows, 128)), axis_index_groups=far).astype(F32)
    part = (jnp.sum(part, axis=0) * root).astype(BF)
    whole = swap(jnp.broadcast_to(part, (n1, rows, 128)), axis_index_groups=near)
    down, pool, mid, unpool, up = unpack(whole.reshape(n1 * rows, 128))
    return (
        output,
        grad_fields,
        down.reshape(w_down.shape),
        pool.reshape(w_pool.shape),
        mid.reshape(w_mid.shape),
        unpool.reshape(2, 2, 2, 32, 64).transpose(0, 1, 2, 4, 3),
        up.reshape(w_up.shape),
    )


def solution(mesh):
    placed = (P("gx", "gy", None), P(), P(), P(), P(), P(), P("gx", "gy", None))
    return jax.shard_map(
        per_device,
        mesh=mesh,
        in_specs=placed,
        out_specs=(P("gx", "gy", None), P("gx", "gy", None), P(), P(), P(), P(), P()),
        check_vma=False,
    )
```

```python
import functools
import math

import jax
import jax.numpy as jnp
from jax import lax
from jax.experimental import pallas as pl
from jax.experimental.pallas import tpu as pltpu
from jax.sharding import PartitionSpec as P

BF = jnp.bfloat16
F32 = jnp.float32
NN = (((1,), (0,)), ((), ()))
NT = (((1,), (1,)), ((), ()))
TN = (((0,), (0,)), ((), ()))

HF = 7
HC = 5
EX, EY = 32, 48
CX, CY = 16, 32
BX, BY = 16, 32
W = 256
TILES = 50


def dot(a, b, dims=NN):
    return lax.dot_general(a, b, dims, preferred_element_type=F32)


def rounded(v):
    return v.astype(BF).astype(F32)


DOWN, D_UP, UP = 7, 6, 3
MOST = 64


def loop(n, body, most=None):
    together = max(k for k in range(1, (most or MOST) + 1) if n % k == 0)

    def step(i, carry):
        for k in range(together):
            body(i * together + k)
        return carry

    if together == n:
        step(0, 0)
    else:
        lax.fori_loop(0, n // together, step, 0)


def aligned(at):
    return at if isinstance(at, int) else pl.multiple_of(at, 8)


def repeat_matrix(rows, cols, period, first):
    r = lax.broadcasted_iota(jnp.int32, (rows, cols), 0)
    c = lax.broadcasted_iota(jnp.int32, (rows, cols), 1)
    return (lax.rem(c, period) == r + first).astype(F32).astype(BF)


def bands_kernel(wd, wp, wm, wu, wup, bd, pm, bm, um, bu, wide, wide_mid):
    def band(w, out, wide, ch):
        planes = W // ch
        wide[...] = dot(w[...], repeat_matrix(ch, W, ch, 0))
        group = lax.broadcasted_iota(jnp.int32, (ch, W), 1) // ch

        def tap(t):
            base = t * 3 * ch if isinstance(t, int) else pl.multiple_of(t * 3 * ch, ch)
            t0 = wide[pl.ds(base, ch), :]
            t1 = wide[pl.ds(base + ch, ch), :]
            t2 = wide[pl.ds(base + 2 * ch, ch), :]
            for p in range(planes):
                rows = jnp.where(group == p, t1, 0.0)
                if p + 1 < planes:
                    rows = jnp.where(group == p + 1, t0, rows)
                if p > 0:
                    rows = jnp.where(group == p - 1, t2, rows)
                out[pl.ds(pl.multiple_of(t * W + p * ch, ch), ch), :] = rows.astype(BF)

        loop(9, tap)

    band(wd, bd, wide, 32)
    band(wup, bu, wide, 32)
    band(wm, bm, wide_mid, 64)
    group = lax.broadcasted_iota(jnp.int32, (64, W), 1) // 64
    same = repeat_matrix(64, W, 64, 0)
    low = repeat_matrix(32, W, 64, 0)
    high = repeat_matrix(32, W, 64, 32)
    for q in range(4):
        pool = dot(wp[q], same)
        unpool = dot(wu[2 * q], low, TN) + dot(wu[2 * q + 1], high, TN)
        for y in range(4):
            rows = slice(q * W + y * 64, q * W + y * 64 + 64)
            pm[rows, :] = jnp.where(group == y, pool, 0.0).astype(BF)
            um[rows, :] = jnp.where(group == y, unpool, 0.0).astype(BF)


def build_bands(w_down, w_pool, w_mid, w_unpool, w_up):
    wide = jax.ShapeDtypeStruct((9 * W, W), BF)
    four = jax.ShapeDtypeStruct((4 * W, W), BF)
    return pl.pallas_call(
        bands_kernel,
        out_shape=(wide, four, wide, four, wide),
        scratch_shapes=[pltpu.VMEM((27 * 32, W), F32), pltpu.VMEM((27 * 64, W), F32)],
        compiler_params=pltpu.CompilerParams(vmem_limit_bytes=24 * 1024 * 1024),
        cost_estimate=pl.CostEstimate(flops=2 * 10**9, bytes_accessed=8 * 10**6, transcendentals=0),
        name="bands",
    )(
        w_down.reshape(27 * 32, 32),
        w_pool.reshape(4, 64, 64),
        w_mid.reshape(27 * 64, 64),
        w_unpool.transpose(0, 1, 2, 4, 3).reshape(8, 32, 64),
        w_up.reshape(27 * 32, 32),
    )


def get_row(src, row):
    if len(src.shape) == 3 and src.shape[2] == 128:
        at = pl.ds(aligned(row * EY), EY)
        return jnp.concatenate([src[0, at, :], src[1, at, :]], axis=1)
    if len(src.shape) == 3:
        return src[row]
    return jnp.concatenate([src[0, row], src[1, row]], axis=1)


def get_rows(src, rows):
    return jnp.concatenate([src[0, rows], src[1, rows]], axis=2)


def put_row(dst, row, value):
    dst[row] = value.astype(BF)


def put_rows(dst, rows, value):
    dst[0, rows] = value[..., 0:128]
    dst[1, rows] = value[..., 128:256]


def get_every_second(src, row, first, count):
    at = pl.ds(first, count, stride=2)
    return jnp.concatenate([src[0, row, at, :], src[1, row, at, :]], axis=1)


def put_every_second(dst, row, first, value):
    at = pl.ds(first, value.shape[0], stride=2)
    dst[0, row, at, :] = value[:, 0:128]
    dst[1, row, at, :] = value[:, 128:256]


def taps_to_lanes(src, row, out, at, lo, size):
    v = get_row(src, row).astype(F32)
    n = v.shape[0]
    out[at, :, 0:W] = pltpu.roll(v, 1, 0)[lo : lo + size].astype(BF)
    out[at, :, W : 2 * W] = v[lo : lo + size].astype(BF)
    out[at, :, 2 * W : 3 * W] = pltpu.roll(v, n - 1, 0)[lo : lo + size].astype(BF)


def conv_rows(v3, first, rows, band):
    total = None
    for a in range(3):
        piece = v3[pl.ds(first + a, rows)]
        piece = piece.reshape(rows * piece.shape[1], 3 * W)
        part = dot(piece, band[a * 3 * W : (a + 1) * 3 * W, :])
        total = part if total is None else total + part
    return total


def conv_t_rows(v3, first, rows, band):
    total = None
    for a in range(3):
        piece = v3[pl.ds(first + a, rows)]
        piece = piece.reshape(rows * piece.shape[1], 3 * W)
        for b in range(3):
            tap = (2 - a) * 3 + (2 - b)
            part = dot(piece[:, b * W : (b + 1) * W], band[tap * W : (tap + 1) * W, :], NT)
            total = part if total is None else total + part
    return total


def pick(d, lanes, shift, ch, width):
    group = lax.broadcasted_iota(jnp.int32, (ch, 128), 1) // ch
    p0 = (lanes % width) // ch
    out = jnp.zeros((ch, 128), F32)
    for g in range(128 // ch):
        z = p0 + g - shift
        if 0 <= z < W // ch:
            out = jnp.where(group == g, d[z * ch : (z + 1) * ch, lanes : lanes + 128], out)
    return out


def put_split(value, hi, lo, row, lanes):
    top = value.astype(BF)
    hi[row : row + value.shape[0], lanes : lanes + 128] = top
    lo[row : row + value.shape[0], lanes : lanes + 128] = (value - top.astype(F32)).astype(BF)


def conv_weight_terms(dout_t, v3, rows, ch, hi, lo, dsc):
    units = 27 * ch
    pad = hi.shape[0] - units
    hi[units:, :] = jnp.zeros((pad, W), BF)
    lo[units:, :] = jnp.zeros((pad, W), BF)
    for a in range(3):
        piece = v3[a : a + rows]
        piece = piece.reshape(rows * piece.shape[1], 3 * W)
        dsc[...] = dot(dout_t, piece)
        for b in range(3):
            for k in range(3):
                unit = (a * 3 + b) * 3 + k
                for t in range(2):
                    value = pick(dsc, b * W + t * 128, k - 1, ch, W)
                    put_split(value, hi, lo, unit * ch, t * 128)


def main_kernel(
    core, fc, cc, xlo, xhi, ylo, yhi, clo, chi, bd, pm, bm, um, bu,
    mine, other, skip_rows, down_rows,
    fe, ce, hid, ds_down, skp, dup, ddn,
    v3f, v3c, v3fl, v3s,
    parts, d_parts, co, mid, ds_pool, ds_mid, dmid, v3m, v3dm, v3ml,
    hi, lo, him, lom, dsc, terms,
):
    def gather(dst, count, center, off):
        def put(row, value):
            at = pl.ds(aligned(row * EY + 8), BY)
            dst[0, at, :] = value[:, 0:128]
            dst[1, at, :] = value[:, 128:256]

        loop(BX, lambda i: put(8 + i, center[i].astype(F32)))

        def edge(i):
            put(8 - count + i, xlo[off + i].astype(F32))
            put(24 + i, xhi[off + i].astype(F32))

        loop(count, edge)
        for c in range(count):
            for side, y, other in ((ylo, 8 - count + c, 0), (yhi, 40 + c, HF + HC)):
                column = jnp.concatenate(
                    [
                        clo[other + off + c].astype(F32),
                        side[off + c].astype(F32),
                        chi[other + off + c].astype(F32),
                    ],
                    axis=0,
                )
                for h in range(2):
                    dst[h, pl.ds(y, EX, stride=EY), :] = column[:, h * 128 : h * 128 + 128]

    gather(fe, HF, fc, 0)
    gather(ce, HC, cc, HF)

    loop(30, lambda i: taps_to_lanes(fe, 1 + i, v3f, i, 0, EY))
    loop(18, lambda i: taps_to_lanes(fe, 7 + i, v3fl, i, 8, BY))
    zero = jnp.zeros((2, EY, W), F32)
    put_rows(hid, slice(0, 2), zero)
    put_rows(hid, slice(30, 32), zero)

    def down(i):
        pre = conv_rows(v3f, DOWN * i, DOWN, bd)
        sig = jax.nn.sigmoid(pre)
        at = pl.ds(2 + DOWN * i, DOWN)
        put_rows(hid, at, rounded(pre * sig).reshape(DOWN, EY, W))
        put_rows(ds_down, at, (sig * (1.0 + pre * (1.0 - sig))).reshape(DOWN, EY, W))

    loop(28 // DOWN, down)

    loop(26, lambda i: taps_to_lanes(ce, 3 + i, v3c, i, 0, EY))

    def d_up(i):
        total = conv_t_rows(v3c, D_UP * i, D_UP, bu)
        put_rows(dup, pl.ds(4 + D_UP * i, D_UP), total.reshape(D_UP, EY, W))

    loop(24 // D_UP, d_up)

    pad = jnp.zeros((CY - EY // 2, W), F32)

    def to_parts(src, x):
        for i in range(2):
            for j in range(2):
                half = get_every_second(src, 2 * x + i, j, EY // 2)
                parts[2 * i + j, x] = jnp.concatenate([half, pad], axis=0).astype(BF)

    loop(CX, lambda x: to_parts(hid, x))

    def pool(i):
        pre = None
        for q in range(4):
            piece = parts[q, pl.ds(8 * i, 8)].reshape(8 * CY, W)
            part = dot(piece, pm[q * W : (q + 1) * W, :])
            pre = part if pre is None else pre + part
        sig = jax.nn.sigmoid(pre)
        co[pl.ds(8 * i, 8)] = rounded(pre * sig).reshape(8, CY, W)
        ds_pool[pl.ds(8 * i, 8)] = (sig * (1.0 + pre * (1.0 - sig))).reshape(8, CY, W)

    loop(2, pool)

    loop(14, lambda i: taps_to_lanes(co, 1 + i, v3m, i, 0, CY))

    pre_mid = conv_rows(v3m, 0, 12, bm)
    sig_mid = jax.nn.sigmoid(pre_mid)
    own_mid = co[2:14].reshape(12 * CY, W)
    mid[2:14] = (own_mid + pre_mid * sig_mid).astype(BF).reshape(12, CY, W)
    ds_mid[2:14] = (sig_mid * (1.0 + pre_mid * (1.0 - sig_mid))).reshape(12, CY, W)

    def up(x):
        m = mid[pl.ds(2 + UP * x, UP)].reshape(UP * CY, W)
        for i in range(2):
            for j in range(2):
                q = 2 * i + j
                lifted = dot(m, um[q * W : (q + 1) * W, :])
                for r in range(UP):
                    at = 2 + UP * x + r
                    own = parts[q, at].astype(F32)[0 : EY // 2]
                    pre = own + lifted[r * CY : r * CY + EY // 2]
                    sig = jax.nn.sigmoid(pre)
                    put_every_second(skp, 2 * at + i, j, rounded(pre * sig))
                    raw = get_every_second(dup, 2 * at + i, j, EY // 2)
                    d_up = raw * (sig * (1.0 + pre * (1.0 - sig)))
                    d_parts[q, at] = jnp.concatenate([d_up, pad], axis=0).astype(BF)

    loop(12 // UP, up)

    loop(18, lambda i: taps_to_lanes(skp, 7 + i, v3s, i, 8, BY))
    loop(18, lambda i: put_row(skip_rows, i, get_row(skp, 7 + i)))

    cot_t = cc[...].reshape(BX * BY, W).astype(F32).T.astype(BF)
    fold = repeat_matrix(32, W, 32, 0)
    fold_mid = repeat_matrix(64, W, 64, 0)

    def fold_to(matrix, hi, lo, tile, count):
        total = dot(matrix, hi[...], NT) + dot(matrix, lo[...], NT)
        for t in range(count):
            rows = matrix.shape[0]
            part = total[:, t * 128 : (t + 1) * 128]
            terms[(tile * 32 + t * rows) : (tile * 32 + (t + 1) * rows), :] = part.astype(BF)

    conv_weight_terms(cot_t, v3s, BX, 32, hi, lo, dsc)
    fold_to(fold, hi, lo, 7, 7)

    def own_parts(src, q):
        return src[q, 4:12].astype(F32)[:, 4:20].reshape(128, W).astype(BF)

    mid_t = mid[4:12].astype(F32)[:, 0:24][:, 4:20].reshape(128, W).T.astype(BF)

    def fold_four(tile):
        total = dot(fold_mid, him[0:256, :], NT) + dot(fold_mid, lom[0:256, :], NT)
        for t in range(2):
            rows = slice(tile * 32 + t * 64, tile * 32 + (t + 1) * 64)
            terms[rows, :] = total[:, t * 128 : (t + 1) * 128].astype(BF)

    def plain_terms(left, src, q, row):
        d = dot(left, own_parts(src, q))
        for t in range(2):
            group = lax.broadcasted_iota(jnp.int32, (64, 128), 1) // 64
            low = d[(2 * t) * 64 : (2 * t + 1) * 64, t * 128 : (t + 1) * 128]
            high = d[(2 * t + 1) * 64 : (2 * t + 2) * 64, t * 128 : (t + 1) * 128]
            put_split(jnp.where(group == 0, low, high), him, lom, row, t * 128)

    for q in range(4):
        plain_terms(mid_t, d_parts, q, 64 * q)
    fold_four(46)

    d_middle = None
    for q in range(4):
        part = dot(d_parts[q, 2:14].reshape(12 * CY, W), um[q * W : (q + 1) * W, :], NT)
        d_middle = part if d_middle is None else d_middle + part
    dmid[2:14] = rounded(d_middle * ds_mid[2:14].reshape(12 * CY, W)).reshape(12, CY, W)
    ds_mid[2:14] = d_middle.reshape(12, CY, W)

    loop(12, lambda i: taps_to_lanes(dmid, 2 + i, v3dm, i, 0, CY))

    def coarse_local(i):
        v = co[3 + i]
        for b in range(3):
            v3ml[i, :, b * W : (b + 1) * W] = v[3 + b : 19 + b].astype(BF)

    loop(10, coarse_local)
    dmid_t = dmid[4:12][:, 4:20].reshape(128, W).T.astype(BF)
    conv_weight_terms(dmid_t, v3ml, 8, 64, him, lom, dsc)
    fold_to(fold_mid, him, lom, 14, 14)

    d_coarse = ds_mid[3:13] + conv_t_rows(v3dm, 0, 10, bm).reshape(10, CY, W)
    ds_pool[3:13] = rounded(d_coarse * ds_pool[3:13])

    dp = ds_pool[3:13].reshape(10 * CY, W).astype(BF)
    for i in range(2):
        for j in range(2):
            q = 2 * i + j
            back = dot(dp, pm[q * W : (q + 1) * W, :], NT)
            for r in range(10):
                row = 2 * (3 + r) + i
                own = d_parts[q, 3 + r].astype(F32)[0 : EY // 2]
                d_hidden = own + back[r * CY : r * CY + EY // 2]
                slope = get_every_second(ds_down, row, j, EY // 2)
                put_every_second(ddn, row, j, rounded(d_hidden * slope))

    loop(18, lambda i: put_row(down_rows, i, get_row(ddn, 7 + i)))

    down_t = get_rows(ddn, slice(8, 24))[:, 8:40].reshape(BX * BY, W).T.astype(BF)
    conv_weight_terms(down_t, v3fl, BX, 32, hi, lo, dsc)
    fold_to(fold, hi, lo, 0, 7)

    pool_t = ds_pool[4:12][:, 4:20].reshape(128, W).T.astype(BF)
    for q in range(4):
        plain_terms(pool_t, parts, q, 64 * q)
    fold_four(42)
    rest = terms.shape[0] - TILES * 32
    if rest > 0:
        terms[TILES * 32 :, :] = jnp.zeros((rest, 128), BF)
    half = terms.shape[0] // 2

    @pl.when(core[0] == 0)
    def _():
        mine[...] = terms[0:half, :]
        other[...] = terms[half:, :]

    @pl.when(core[0] != 0)
    def _():
        mine[...] = terms[half:, :]
        other[...] = terms[0:half, :]


def finish_kernel(fc, cc, skip_rows, down_rows, bd, bu, out, gf, v3):
    loop(18, lambda i: taps_to_lanes(skip_rows, i, v3, i, 8, BY))
    total = conv_rows(v3, 0, BX, bu).reshape(BX, BY, W)
    out[...] = (fc[...].astype(F32) + total).astype(BF)
    loop(18, lambda i: taps_to_lanes(down_rows, i, v3, i, 8, BY))
    total = conv_t_rows(v3, 0, BX, bd).reshape(BX, BY, W)
    gf[...] = (cc[...].astype(F32) + total).astype(BF)


def finish_call(fields, cot, skip_rows, down_rows, bands):
    block = jax.ShapeDtypeStruct((BX, BY, W), BF)
    return pl.pallas_call(
        finish_kernel,
        out_shape=(block, block),
        scratch_shapes=[pltpu.VMEM((18, BY, 3 * W), BF)],
        compiler_params=pltpu.CompilerParams(vmem_limit_bytes=16 * 1024 * 1024),
        cost_estimate=pl.CostEstimate(flops=3 * 10**9, bytes_accessed=10**7, transcendentals=0),
        name="finish",
    )(fields, cot, skip_rows, down_rows, bands[0], bands[4])


def main_call(core, fields, cot, halos, bands, term_rows):
    half = jax.ShapeDtypeStruct((term_rows // 2, 128), BF)
    some = jax.ShapeDtypeStruct((18, EY, W), BF)
    flat = pltpu.VMEM((2, EX * EY, 128), F32)
    split = pltpu.VMEM((2, EX, EY, 128), F32)
    coarse = pltpu.VMEM((CX, CY, W), F32)
    return pl.pallas_call(
        main_kernel,
        out_shape=(half, half, some, some),
        in_specs=[pl.BlockSpec(memory_space=pltpu.SMEM)]
        + [pl.BlockSpec(memory_space=pltpu.VMEM)] * 13,
        scratch_shapes=[flat] * 2
        + [split] * 5
        + [
            pltpu.VMEM((30, EY, 3 * W), BF),
            pltpu.VMEM((26, EY, 3 * W), BF),
            pltpu.VMEM((18, BY, 3 * W), BF),
            pltpu.VMEM((18, BY, 3 * W), BF),
            pltpu.VMEM((4, CX, CY, W), BF),
            pltpu.VMEM((4, CX, CY, W), BF),
            coarse,
            pltpu.VMEM((CX, CY, W), BF),
            coarse,
            coarse,
            coarse,
            pltpu.VMEM((14, CY, 3 * W), BF),
            pltpu.VMEM((12, CY, 3 * W), BF),
            pltpu.VMEM((10, 16, 3 * W), BF),
            pltpu.VMEM((28 * 32, W), BF),
            pltpu.VMEM((28 * 32, W), BF),
            pltpu.VMEM((28 * 64, W), BF),
            pltpu.VMEM((28 * 64, W), BF),
            pltpu.VMEM((W, 3 * W), F32),
            pltpu.VMEM((term_rows, 128), BF),
        ],
        compiler_params=pltpu.CompilerParams(vmem_limit_bytes=36 * 1024 * 1024),
        cost_estimate=pl.CostEstimate(flops=10**10, bytes_accessed=10**7, transcendentals=10**6),
        name="network",
    )(core, fields, cot, *halos, *bands)


def unpack_kernel(
    core, mine, other, down, pool, mid, unpool, up,
    down_v, pool_v, mid_v, unpool_v, up_v, terms, sems,
):
    half = mine.shape[0]

    @pl.when(core[0] == 0)
    def _():
        terms[0:half, :] = mine[...]
        terms[half:, :] = other[...]

    @pl.when(core[0] != 0)
    def _():
        terms[0:half, :] = other[...]
        terms[half:, :] = mine[...]

    def send(k, src, dst):
        copy = pltpu.make_async_copy(src, dst, sems.at[k])
        copy.start()
        return copy

    copies = []
    for part in range(3):
        for u in range(9 * part, 9 * part + 9):
            row, lane = 14 * 32 + (u // 2) * 64, (u % 2) * 64
            mid_v[u] = terms[row : row + 64, lane : lane + 64].astype(F32)
        at = pl.ds(9 * part, 9)
        copies.append(send(part, mid_v.at[at], mid.at[at]))
    for first, src, dst in ((0, down_v, down), (224, up_v, up)):
        for u in range(27):
            row, lane = first + (u // 4) * 32, (u % 4) * 32
            src[u] = terms[row : row + 32, lane : lane + 32].astype(F32)
        copies.append(send(3 if first == 0 else 4, src, dst))
    for first, src, dst in ((42 * 32, pool_v, pool), (46 * 32, unpool_v, unpool)):
        for q in range(4):
            row, lane = first + (q // 2) * 64, (q % 2) * 64
            src[q] = terms[row : row + 64, lane : lane + 64].astype(F32)
        copies.append(send(5 if src is pool_v else 6, src, dst))
    for copy in copies:
        copy.wait()


def unpack(core, mine, other):
    shapes = ((27, 32, 32), (4, 64, 64), (27, 64, 64), (4, 64, 64), (27, 32, 32))
    return pl.pallas_call(
        unpack_kernel,
        out_shape=tuple(jax.ShapeDtypeStruct(s, F32) for s in shapes),
        in_specs=[pl.BlockSpec(memory_space=pltpu.SMEM)]
        + [pl.BlockSpec(memory_space=pltpu.VMEM)] * 2,
        out_specs=tuple(pl.BlockSpec(memory_space=pl.ANY) for _ in shapes),
        scratch_shapes=[pltpu.VMEM(s, F32) for s in shapes]
        + [pltpu.VMEM((2 * mine.shape[0], 128), BF), pltpu.SemaphoreType.DMA((7,))],
        compiler_params=pltpu.CompilerParams(vmem_limit_bytes=8 * 1024 * 1024),
        name="unpack",
    )(core, mine, other)


def ring(axis, step):
    n = lax.axis_size(axis)
    return [(i, (i + step) % n) for i in range(n)]


def pack_kernel(fc, cc, first_x, last_x, first_y, last_y, side, wide, columns, sems):
    copies = []

    def fetch(src, dst):
        copy = pltpu.make_async_copy(src, dst, sems.at[len(copies)])
        copy.start()
        copies.append(copy)

    for k, src in enumerate((fc, cc)):
        fetch(src.at[:, 0:16], side.at[2 * k])
        fetch(src.at[:, BY - 16 : BY], side.at[2 * k + 1])
    for src, count, at in ((fc, HF, 0), (cc, HC, HF)):
        fetch(src.at[0:count], first_x.at[at : at + count])
        fetch(src.at[BX - count : BX], last_x.at[at : at + count])
    for copy in copies[:4]:
        copy.wait()
    for k, (count, at) in enumerate(((HF, 0), (HC, HF))):
        for e, (out, first) in enumerate(((0, 0), (1, 16 - count))):
            for h in range(2):
                lanes = slice(h * 128, h * 128 + 128)
                wide[h] = side[2 * k + e, :, :, lanes].reshape(BX * 16, 128).astype(F32)
            for c in range(count):
                for h in range(2):
                    lanes = slice(h * 128, h * 128 + 128)
                    column = wide[h, pl.ds(first + c, BX, stride=16), :]
                    columns[out, at + c, :, lanes] = column.astype(BF)
    fetch(columns.at[0], first_y)
    fetch(columns.at[1], last_y)
    for copy in copies[4:]:
        copy.wait()


def pack(fields, cot):
    rows = jax.ShapeDtypeStruct((HF + HC, BY, W), BF)
    columns = jax.ShapeDtypeStruct((HF + HC, BX, W), BF)
    return pl.pallas_call(
        pack_kernel,
        out_shape=(rows, rows, columns, columns),
        in_specs=[pl.BlockSpec(memory_space=pl.ANY)] * 2,
        out_specs=(pl.BlockSpec(memory_space=pl.ANY),) * 4,
        scratch_shapes=[
            pltpu.VMEM((4, BX, 16, W), BF),
            pltpu.VMEM((2, BX * 16, 128), F32),
            pltpu.VMEM((2, HF + HC, BX, W), BF),
            pltpu.SemaphoreType.DMA((10,)),
        ],
        compiler_params=pltpu.CompilerParams(vmem_limit_bytes=56 * 1024 * 1024),
        name="pack",
    )(fields, cot)


def exchange(fields, cot):
    first_x, last_x, first_y, last_y = pack(fields, cot)
    ylo = lax.ppermute(last_y, "gy", ring("gy", 1))
    yhi = lax.ppermute(first_y, "gy", ring("gy", -1))
    xlo = lax.ppermute(last_x, "gx", ring("gx", 1))
    xhi = lax.ppermute(first_x, "gx", ring("gx", -1))
    last_c = jnp.concatenate([ylo[:, BX - 8 :], yhi[:, BX - 8 :]], axis=0)
    first_c = jnp.concatenate([ylo[:, :8], yhi[:, :8]], axis=0)
    clo = lax.ppermute(last_c, "gx", ring("gx", 1))
    chi = lax.ppermute(first_c, "gx", ring("gx", -1))
    return (xlo, xhi, ylo, yhi, clo, chi)


def reduce_groups(nx, ny):
    flat = lambda x, y: x * ny + y
    near = [
        [flat(x, 2 * z + e) for x in range(c, nx, 2) for e in range(2)]
        for c in range(2)
        for z in range(ny // 2)
    ]
    far = [[flat(x, 2 * z + e) for z in range(ny // 2)] for x in range(nx) for e in range(2)]
    return near, far


def per_device(fields, w_down, w_pool, w_mid, w_unpool, w_up, cotangent):
    nx, ny = lax.axis_size("gx"), lax.axis_size("gy")
    near, far = reduce_groups(nx, ny)
    n1, n2 = len(near[0]), len(far[0])
    rows = -(-TILES * 32 // (16 * n1)) * 8
    core = (lax.axis_index("gx") % 2).astype(jnp.int32).reshape(1)
    pairs = [(i, i + 1 - 2 * (i % 2)) for i in range(nx)]
    bands = build_bands(w_down, w_pool, w_mid, w_unpool, w_up)
    halos = exchange(fields, cotangent)
    mine, other, skip_rows, down_rows = main_call(
        core, fields, cotangent, halos, bands, 2 * n1 * rows
    )
    swap = functools.partial(
        lax.all_to_all, axis_name=("gx", "gy"), split_axis=0, concat_axis=0, tiled=True
    )
    cells = fields.shape[0] * fields.shape[1] * 8 * nx * ny
    root = 1.0 / math.sqrt(math.sqrt(cells))
    part = mine.astype(F32) + lax.ppermute(other, "gx", pairs).astype(F32)
    part = swap(part.astype(BF).reshape(n1, rows, 128), axis_index_groups=near)
    output, grad_fields = finish_call(fields, cotangent, skip_rows, down_rows, bands)
    part = (jnp.sum(part.astype(F32), axis=0) * root).astype(BF)
    part = swap(jnp.broadcast_to(part, (n2, rows, 128)), axis_index_groups=far).astype(F32)
    part = (jnp.sum(part, axis=0) * root).astype(BF)
    part = swap(jnp.broadcast_to(part, (n1, rows, 128)), axis_index_groups=near)
    part = part.reshape(n1 * rows, 128)
    down, pool, mid, unpool, up = unpack(core, part, lax.ppermute(part, "gx", pairs))
    return (
        output,
        grad_fields,
        down.reshape(w_down.shape),
        pool.reshape(w_pool.shape),
        mid.reshape(w_mid.shape),
        unpool.reshape(2, 2, 2, 32, 64).transpose(0, 1, 2, 4, 3),
        up.reshape(w_up.shape),
    )


def solution(mesh):
    placed = (P("gx", "gy", None), P(), P(), P(), P(), P(), P("gx", "gy", None))
    return jax.shard_map(
        per_device,
        mesh=mesh,
        in_specs=placed,
        out_specs=(P("gx", "gy", None), P("gx", "gy", None), P(), P(), P(), P(), P()),
        check_vma=False,
    )
```

```python
import functools
import math

import jax
import jax.numpy as jnp
from jax import lax
from jax.experimental import pallas as pl
from jax.experimental.pallas import tpu as pltpu
from jax.sharding import PartitionSpec as P

BF = jnp.bfloat16
F32 = jnp.float32
NN = (((1,), (0,)), ((), ()))
NT = (((1,), (1,)), ((), ()))
TN = (((0,), (0,)), ((), ()))

HF = 7
HC = 5
EX, EY = 32, 48
CX, CY = 16, 32
BX, BY = 16, 32
W = 256
TILES = 50


def dot(a, b, dims=NN):
    return lax.dot_general(a, b, dims, preferred_element_type=F32)


def rounded(v):
    return v.astype(BF).astype(F32)


DOWN, D_UP, UP = 7, 6, 3
MOST = 64


def loop(n, body, most=None):
    together = max(k for k in range(1, (most or MOST) + 1) if n % k == 0)

    def step(i, carry):
        for k in range(together):
            body(i * together + k)
        return carry

    if together == n:
        step(0, 0)
    else:
        lax.fori_loop(0, n // together, step, 0)


def aligned(at):
    return at if isinstance(at, int) else pl.multiple_of(at, 8)


def repeat_matrix(rows, cols, period, first):
    r = lax.broadcasted_iota(jnp.int32, (rows, cols), 0)
    c = lax.broadcasted_iota(jnp.int32, (rows, cols), 1)
    return (lax.rem(c, period) == r + first).astype(F32).astype(BF)


def bands_kernel(wd, wp, wm, wu, wup, bd, pm, bm, um, bu, wide, wide_mid):
    def band(w, out, wide, ch):
        planes = W // ch
        wide[...] = dot(w[...], repeat_matrix(ch, W, ch, 0))
        group = lax.broadcasted_iota(jnp.int32, (ch, W), 1) // ch

        def tap(t):
            base = t * 3 * ch if isinstance(t, int) else pl.multiple_of(t * 3 * ch, ch)
            t0 = wide[pl.ds(base, ch), :]
            t1 = wide[pl.ds(base + ch, ch), :]
            t2 = wide[pl.ds(base + 2 * ch, ch), :]
            for p in range(planes):
                rows = jnp.where(group == p, t1, 0.0)
                if p + 1 < planes:
                    rows = jnp.where(group == p + 1, t0, rows)
                if p > 0:
                    rows = jnp.where(group == p - 1, t2, rows)
                out[pl.ds(pl.multiple_of(t * W + p * ch, ch), ch), :] = rows.astype(BF)

        loop(9, tap)

    band(wd, bd, wide, 32)
    band(wup, bu, wide, 32)
    band(wm, bm, wide_mid, 64)
    group = lax.broadcasted_iota(jnp.int32, (64, W), 1) // 64
    same = repeat_matrix(64, W, 64, 0)
    low = repeat_matrix(32, W, 64, 0)
    high = repeat_matrix(32, W, 64, 32)
    for q in range(4):
        pool = dot(wp[q], same)
        unpool = dot(wu[2 * q], low, TN) + dot(wu[2 * q + 1], high, TN)
        for y in range(4):
            rows = slice(q * W + y * 64, q * W + y * 64 + 64)
            pm[rows, :] = jnp.where(group == y, pool, 0.0).astype(BF)
            um[rows, :] = jnp.where(group == y, unpool, 0.0).astype(BF)


def build_bands(w_down, w_pool, w_mid, w_unpool, w_up):
    wide = jax.ShapeDtypeStruct((9 * W, W), BF)
    four = jax.ShapeDtypeStruct((4 * W, W), BF)
    return pl.pallas_call(
        bands_kernel,
        out_shape=(wide, four, wide, four, wide),
        scratch_shapes=[pltpu.VMEM((27 * 32, W), F32), pltpu.VMEM((27 * 64, W), F32)],
        compiler_params=pltpu.CompilerParams(vmem_limit_bytes=24 * 1024 * 1024),
        cost_estimate=pl.CostEstimate(flops=2 * 10**9, bytes_accessed=8 * 10**6, transcendentals=0),
        name="bands",
    )(
        w_down.reshape(27 * 32, 32),
        w_pool.reshape(4, 64, 64),
        w_mid.reshape(27 * 64, 64),
        w_unpool.transpose(0, 1, 2, 4, 3).reshape(8, 32, 64),
        w_up.reshape(27 * 32, 32),
    )


def get_row(src, row):
    if len(src.shape) == 3 and src.shape[2] == 128:
        at = pl.ds(aligned(row * EY), EY)
        return jnp.concatenate([src[0, at, :], src[1, at, :]], axis=1)
    if len(src.shape) == 3:
        return src[row]
    return jnp.concatenate([src[0, row], src[1, row]], axis=1)


def get_rows(src, rows):
    return jnp.concatenate([src[0, rows], src[1, rows]], axis=2)


def put_row(dst, row, value):
    dst[row] = value.astype(BF)


def put_rows(dst, rows, value):
    dst[0, rows] = value[..., 0:128]
    dst[1, rows] = value[..., 128:256]


def get_every_second(src, row, first, count):
    at = pl.ds(first, count, stride=2)
    return jnp.concatenate([src[0, row, at, :], src[1, row, at, :]], axis=1)


def put_every_second(dst, row, first, value):
    at = pl.ds(first, value.shape[0], stride=2)
    dst[0, row, at, :] = value[:, 0:128]
    dst[1, row, at, :] = value[:, 128:256]


def taps_to_lanes(src, row, out, at, lo, size):
    v = get_row(src, row).astype(F32)
    n = v.shape[0]
    out[at, :, 0:W] = pltpu.roll(v, 1, 0)[lo : lo + size].astype(BF)
    out[at, :, W : 2 * W] = v[lo : lo + size].astype(BF)
    out[at, :, 2 * W : 3 * W] = pltpu.roll(v, n - 1, 0)[lo : lo + size].astype(BF)


def conv_rows(v3, first, rows, band):
    total = None
    for a in range(3):
        piece = v3[pl.ds(first + a, rows)]
        piece = piece.reshape(rows * piece.shape[1], 3 * W)
        part = dot(piece, band[a * 3 * W : (a + 1) * 3 * W, :])
        total = part if total is None else total + part
    return total


def conv_t_rows(v3, first, rows, band):
    total = None
    for a in range(3):
        piece = v3[pl.ds(first + a, rows)]
        piece = piece.reshape(rows * piece.shape[1], 3 * W)
        for b in range(3):
            tap = (2 - a) * 3 + (2 - b)
            part = dot(piece[:, b * W : (b + 1) * W], band[tap * W : (tap + 1) * W, :], NT)
            total = part if total is None else total + part
    return total


def pick(d, lanes, shift, ch, width):
    group = lax.broadcasted_iota(jnp.int32, (ch, 128), 1) // ch
    p0 = (lanes % width) // ch
    out = jnp.zeros((ch, 128), F32)
    for g in range(128 // ch):
        z = p0 + g - shift
        if 0 <= z < W // ch:
            out = jnp.where(group == g, d[z * ch : (z + 1) * ch, lanes : lanes + 128], out)
    return out


def put_split(value, hi, lo, row, lanes):
    top = value.astype(BF)
    hi[row : row + value.shape[0], lanes : lanes + 128] = top
    lo[row : row + value.shape[0], lanes : lanes + 128] = (value - top.astype(F32)).astype(BF)


def conv_weight_terms(dout_t, v3, rows, ch, hi, lo, dsc):
    units = 27 * ch
    pad = hi.shape[0] - units
    hi[units:, :] = jnp.zeros((pad, W), BF)
    lo[units:, :] = jnp.zeros((pad, W), BF)
    for a in range(3):
        piece = v3[a : a + rows]
        piece = piece.reshape(rows * piece.shape[1], 3 * W)
        dsc[...] = dot(dout_t, piece)
        for b in range(3):
            for k in range(3):
                unit = (a * 3 + b) * 3 + k
                for t in range(2):
                    value = pick(dsc, b * W + t * 128, k - 1, ch, W)
                    put_split(value, hi, lo, unit * ch, t * 128)


def main_kernel(
    core, fc, cc, xlo, xhi, ylo, yhi, clo, chi, bd, pm, bm, um, bu,
    mine, other, skip_rows, down_rows,
    fe, ce, hid, ds_down, skp, dup, ddn,
    v3f, v3c, v3fl, v3s,
    parts, d_parts, co, mid, ds_pool, ds_mid, dmid, v3m, v3dm, v3ml,
    hi, lo, him, lom, dsc, terms,
):
    def gather(dst, count, center, off):
        def put(row, value):
            at = pl.ds(aligned(row * EY + 8), BY)
            dst[0, at, :] = value[:, 0:128]
            dst[1, at, :] = value[:, 128:256]

        loop(BX, lambda i: put(8 + i, center[i].astype(F32)))

        def edge(i):
            put(8 - count + i, xlo[off + i].astype(F32))
            put(24 + i, xhi[off + i].astype(F32))

        loop(count, edge)
        for c in range(count):
            for side, y, other in ((ylo, 8 - count + c, 0), (yhi, 40 + c, HF + HC)):
                column = jnp.concatenate(
                    [
                        clo[other + off + c].astype(F32),
                        side[off + c].astype(F32),
                        chi[other + off + c].astype(F32),
                    ],
                    axis=0,
                )
                for h in range(2):
                    dst[h, pl.ds(y, EX, stride=EY), :] = column[:, h * 128 : h * 128 + 128]

    gather(fe, HF, fc, 0)
    gather(ce, HC, cc, HF)

    loop(30, lambda i: taps_to_lanes(fe, 1 + i, v3f, i, 0, EY))
    loop(18, lambda i: taps_to_lanes(fe, 7 + i, v3fl, i, 8, BY))
    zero = jnp.zeros((2, EY, W), F32)
    put_rows(hid, slice(0, 2), zero)
    put_rows(hid, slice(30, 32), zero)

    def down(i):
        pre = conv_rows(v3f, DOWN * i, DOWN, bd)
        sig = jax.nn.sigmoid(pre)
        at = pl.ds(2 + DOWN * i, DOWN)
        put_rows(hid, at, rounded(pre * sig).reshape(DOWN, EY, W))
        put_rows(ds_down, at, (sig * (1.0 + pre * (1.0 - sig))).reshape(DOWN, EY, W))

    loop(28 // DOWN, down)

    loop(26, lambda i: taps_to_lanes(ce, 3 + i, v3c, i, 0, EY))

    def d_up(i):
        total = conv_t_rows(v3c, D_UP * i, D_UP, bu)
        put_rows(dup, pl.ds(4 + D_UP * i, D_UP), total.reshape(D_UP, EY, W))

    loop(24 // D_UP, d_up)

    pad = jnp.zeros((CY - EY // 2, W), F32)

    def to_parts(src, x):
        for i in range(2):
            for j in range(2):
                half = get_every_second(src, 2 * x + i, j, EY // 2)
                parts[2 * i + j, x] = jnp.concatenate([half, pad], axis=0).astype(BF)

    loop(CX, lambda x: to_parts(hid, x))

    def pool(i):
        pre = None
        for q in range(4):
            piece = parts[q, pl.ds(8 * i, 8)].reshape(8 * CY, W)
            part = dot(piece, pm[q * W : (q + 1) * W, :])
            pre = part if pre is None else pre + part
        sig = jax.nn.sigmoid(pre)
        co[pl.ds(8 * i, 8)] = rounded(pre * sig).reshape(8, CY, W)
        ds_pool[pl.ds(8 * i, 8)] = (sig * (1.0 + pre * (1.0 - sig))).reshape(8, CY, W)

    loop(2, pool)

    loop(14, lambda i: taps_to_lanes(co, 1 + i, v3m, i, 0, CY))

    pre_mid = conv_rows(v3m, 0, 12, bm)
    sig_mid = jax.nn.sigmoid(pre_mid)
    own_mid = co[2:14].reshape(12 * CY, W)
    mid[2:14] = (own_mid + pre_mid * sig_mid).astype(BF).reshape(12, CY, W)
    ds_mid[2:14] = (sig_mid * (1.0 + pre_mid * (1.0 - sig_mid))).reshape(12, CY, W)

    def up(x):
        m = mid[pl.ds(2 + UP * x, UP)].reshape(UP * CY, W)
        for i in range(2):
            for j in range(2):
                q = 2 * i + j
                lifted = dot(m, um[q * W : (q + 1) * W, :])
                for r in range(UP):
                    at = 2 + UP * x + r
                    own = parts[q, at].astype(F32)[0 : EY // 2]
                    pre = own + lifted[r * CY : r * CY + EY // 2]
                    sig = jax.nn.sigmoid(pre)
                    put_every_second(skp, 2 * at + i, j, rounded(pre * sig))
                    raw = get_every_second(dup, 2 * at + i, j, EY // 2)
                    d_up = raw * (sig * (1.0 + pre * (1.0 - sig)))
                    d_parts[q, at] = jnp.concatenate([d_up, pad], axis=0).astype(BF)

    loop(12 // UP, up)

    loop(18, lambda i: taps_to_lanes(skp, 7 + i, v3s, i, 8, BY))
    loop(18, lambda i: put_row(skip_rows, i, get_row(skp, 7 + i)))

    cot_t = cc[...].reshape(BX * BY, W).astype(F32).T.astype(BF)
    fold = repeat_matrix(32, W, 32, 0)
    fold_mid = repeat_matrix(64, W, 64, 0)

    def fold_to(matrix, hi, lo, tile, count):
        total = dot(matrix, hi[...], NT) + dot(matrix, lo[...], NT)
        for t in range(count):
            rows = matrix.shape[0]
            part = total[:, t * 128 : (t + 1) * 128]
            terms[(tile * 32 + t * rows) : (tile * 32 + (t + 1) * rows), :] = part.astype(BF)

    conv_weight_terms(cot_t, v3s, BX, 32, hi, lo, dsc)
    fold_to(fold, hi, lo, 7, 7)

    def own_parts(src, q):
        return src[q, 4:12].astype(F32)[:, 4:20].reshape(128, W).astype(BF)

    mid_t = mid[4:12].astype(F32)[:, 0:24][:, 4:20].reshape(128, W).T.astype(BF)

    def fold_four(tile):
        total = dot(fold_mid, him[0:256, :], NT) + dot(fold_mid, lom[0:256, :], NT)
        for t in range(2):
            rows = slice(tile * 32 + t * 64, tile * 32 + (t + 1) * 64)
            terms[rows, :] = total[:, t * 128 : (t + 1) * 128].astype(BF)

    def plain_terms(left, src, q, row):
        d = dot(left, own_parts(src, q))
        for t in range(2):
            group = lax.broadcasted_iota(jnp.int32, (64, 128), 1) // 64
            low = d[(2 * t) * 64 : (2 * t + 1) * 64, t * 128 : (t + 1) * 128]
            high = d[(2 * t + 1) * 64 : (2 * t + 2) * 64, t * 128 : (t + 1) * 128]
            put_split(jnp.where(group == 0, low, high), him, lom, row, t * 128)

    for q in range(4):
        plain_terms(mid_t, d_parts, q, 64 * q)
    fold_four(46)

    d_middle = None
    for q in range(4):
        part = dot(d_parts[q, 2:14].reshape(12 * CY, W), um[q * W : (q + 1) * W, :], NT)
        d_middle = part if d_middle is None else d_middle + part
    dmid[2:14] = rounded(d_middle * ds_mid[2:14].reshape(12 * CY, W)).reshape(12, CY, W)
    ds_mid[2:14] = d_middle.reshape(12, CY, W)

    loop(12, lambda i: taps_to_lanes(dmid, 2 + i, v3dm, i, 0, CY))

    def coarse_local(i):
        v = co[3 + i]
        for b in range(3):
            v3ml[i, :, b * W : (b + 1) * W] = v[3 + b : 19 + b].astype(BF)

    loop(10, coarse_local)
    dmid_t = dmid[4:12][:, 4:20].reshape(128, W).T.astype(BF)
    conv_weight_terms(dmid_t, v3ml, 8, 64, him, lom, dsc)
    fold_to(fold_mid, him, lom, 14, 14)

    d_coarse = ds_mid[3:13] + conv_t_rows(v3dm, 0, 10, bm).reshape(10, CY, W)
    ds_pool[3:13] = rounded(d_coarse * ds_pool[3:13])

    dp = ds_pool[3:13].reshape(10 * CY, W).astype(BF)
    for i in range(2):
        for j in range(2):
            q = 2 * i + j
            back = dot(dp, pm[q * W : (q + 1) * W, :], NT)
            for r in range(10):
                row = 2 * (3 + r) + i
                own = d_parts[q, 3 + r].astype(F32)[0 : EY // 2]
                d_hidden = own + back[r * CY : r * CY + EY // 2]
                slope = get_every_second(ds_down, row, j, EY // 2)
                put_every_second(ddn, row, j, rounded(d_hidden * slope))

    loop(18, lambda i: put_row(down_rows, i, get_row(ddn, 7 + i)))

    down_t = get_rows(ddn, slice(8, 24))[:, 8:40].reshape(BX * BY, W).T.astype(BF)
    conv_weight_terms(down_t, v3fl, BX, 32, hi, lo, dsc)
    fold_to(fold, hi, lo, 0, 7)

    pool_t = ds_pool[4:12][:, 4:20].reshape(128, W).T.astype(BF)
    for q in range(4):
        plain_terms(pool_t, parts, q, 64 * q)
    fold_four(42)
    rest = terms.shape[0] - TILES * 32
    if rest > 0:
        terms[TILES * 32 :, :] = jnp.zeros((rest, 128), BF)
    half = terms.shape[0] // 2

    @pl.when(core[0] == 0)
    def _():
        mine[...] = terms[0:half, :]
        other[...] = terms[half:, :]

    @pl.when(core[0] != 0)
    def _():
        mine[...] = terms[half:, :]
        other[...] = terms[0:half, :]


def finish_kernel(conv, base, rows, band, out, v3):
    loop(18, lambda i: taps_to_lanes(rows, i, v3, i, 8, BY))
    total = conv(v3, 0, BX, band).reshape(BX, BY, W)
    out[...] = (base[...].astype(F32) + total).astype(BF)


def finish_call(conv, base, rows, band):
    return pl.pallas_call(
        functools.partial(finish_kernel, conv),
        out_shape=jax.ShapeDtypeStruct((BX, BY, W), BF),
        scratch_shapes=[pltpu.VMEM((18, BY, 3 * W), BF)],
        compiler_params=pltpu.CompilerParams(vmem_limit_bytes=16 * 1024 * 1024),
        cost_estimate=pl.CostEstimate(flops=10**9, bytes_accessed=10**6, transcendentals=0),
        name="finish",
    )(base, rows, band)


def main_call(core, fields, cot, halos, bands, term_rows):
    half = jax.ShapeDtypeStruct((term_rows // 2, 128), BF)
    some = jax.ShapeDtypeStruct((18, EY, W), BF)
    flat = pltpu.VMEM((2, EX * EY, 128), F32)
    split = pltpu.VMEM((2, EX, EY, 128), F32)
    coarse = pltpu.VMEM((CX, CY, W), F32)
    return pl.pallas_call(
        main_kernel,
        out_shape=(half, half, some, some),
        in_specs=[pl.BlockSpec(memory_space=pltpu.SMEM)]
        + [pl.BlockSpec(memory_space=pltpu.VMEM)] * 13,
        scratch_shapes=[flat] * 2
        + [split] * 5
        + [
            pltpu.VMEM((30, EY, 3 * W), BF),
            pltpu.VMEM((26, EY, 3 * W), BF),
            pltpu.VMEM((18, BY, 3 * W), BF),
            pltpu.VMEM((18, BY, 3 * W), BF),
            pltpu.VMEM((4, CX, CY, W), BF),
            pltpu.VMEM((4, CX, CY, W), BF),
            coarse,
            pltpu.VMEM((CX, CY, W), BF),
            coarse,
            coarse,
            coarse,
            pltpu.VMEM((14, CY, 3 * W), BF),
            pltpu.VMEM((12, CY, 3 * W), BF),
            pltpu.VMEM((10, 16, 3 * W), BF),
            pltpu.VMEM((28 * 32, W), BF),
            pltpu.VMEM((28 * 32, W), BF),
            pltpu.VMEM((28 * 64, W), BF),
            pltpu.VMEM((28 * 64, W), BF),
            pltpu.VMEM((W, 3 * W), F32),
            pltpu.VMEM((term_rows, 128), BF),
        ],
        compiler_params=pltpu.CompilerParams(vmem_limit_bytes=36 * 1024 * 1024),
        cost_estimate=pl.CostEstimate(flops=10**10, bytes_accessed=10**7, transcendentals=10**6),
        name="network",
    )(core, fields, cot, *halos, *bands)


def unpack_kernel(
    core, mine, other, down, pool, mid, unpool, up,
    down_v, pool_v, mid_v, unpool_v, up_v, terms, sems,
):
    half = mine.shape[0]

    @pl.when(core[0] == 0)
    def _():
        terms[0:half, :] = mine[...]
        terms[half:, :] = other[...]

    @pl.when(core[0] != 0)
    def _():
        terms[0:half, :] = other[...]
        terms[half:, :] = mine[...]

    def send(k, src, dst):
        copy = pltpu.make_async_copy(src, dst, sems.at[k])
        copy.start()
        return copy

    copies = []
    for part in range(3):
        for u in range(9 * part, 9 * part + 9):
            row, lane = 14 * 32 + (u // 2) * 64, (u % 2) * 64
            mid_v[u] = terms[row : row + 64, lane : lane + 64].astype(F32)
        at = pl.ds(9 * part, 9)
        copies.append(send(part, mid_v.at[at], mid.at[at]))
    for first, src, dst in ((0, down_v, down), (224, up_v, up)):
        for u in range(27):
            row, lane = first + (u // 4) * 32, (u % 4) * 32
            src[u] = terms[row : row + 32, lane : lane + 32].astype(F32)
        copies.append(send(3 if first == 0 else 4, src, dst))
    for first, src, dst in ((42 * 32, pool_v, pool), (46 * 32, unpool_v, unpool)):
        for q in range(4):
            row, lane = first + (q // 2) * 64, (q % 2) * 64
            src[q] = terms[row : row + 64, lane : lane + 64].astype(F32)
        copies.append(send(5 if src is pool_v else 6, src, dst))
    for copy in copies:
        copy.wait()


def unpack(core, mine, other):
    shapes = ((27, 32, 32), (4, 64, 64), (27, 64, 64), (4, 64, 64), (27, 32, 32))
    return pl.pallas_call(
        unpack_kernel,
        out_shape=tuple(jax.ShapeDtypeStruct(s, F32) for s in shapes),
        in_specs=[pl.BlockSpec(memory_space=pltpu.SMEM)]
        + [pl.BlockSpec(memory_space=pltpu.VMEM)] * 2,
        out_specs=tuple(pl.BlockSpec(memory_space=pl.ANY) for _ in shapes),
        scratch_shapes=[pltpu.VMEM(s, F32) for s in shapes]
        + [pltpu.VMEM((2 * mine.shape[0], 128), BF), pltpu.SemaphoreType.DMA((7,))],
        compiler_params=pltpu.CompilerParams(vmem_limit_bytes=8 * 1024 * 1024),
        name="unpack",
    )(core, mine, other)


def ring(axis, step):
    n = lax.axis_size(axis)
    return [(i, (i + step) % n) for i in range(n)]


def pack_kernel(fc, cc, first_x, last_x, first_y, last_y, side, wide, rows, columns, sems):
    copies = []

    def fetch(src, dst):
        copy = pltpu.make_async_copy(src, dst, sems.at[len(copies)])
        copy.start()
        copies.append(copy)

    for k, src in enumerate((fc, cc)):
        fetch(src.at[:, 0:16], side.at[2 * k])
        fetch(src.at[:, BY - 16 : BY], side.at[2 * k + 1])
    for src, count, at in ((fc, HF, 0), (cc, HC, HF)):
        fetch(src.at[0:count], rows.at[0, at : at + count])
        fetch(src.at[BX - count : BX], rows.at[1, at : at + count])
    for copy in copies:
        copy.wait()
    fetch(rows.at[0], first_x)
    fetch(rows.at[1], last_x)
    for k, (count, at) in enumerate(((HF, 0), (HC, HF))):
        for e, (out, first) in enumerate(((0, 0), (1, 16 - count))):
            for h in range(2):
                lanes = slice(h * 128, h * 128 + 128)
                wide[h] = side[2 * k + e, :, :, lanes].reshape(BX * 16, 128).astype(F32)
            for c in range(count):
                for h in range(2):
                    lanes = slice(h * 128, h * 128 + 128)
                    column = wide[h, pl.ds(first + c, BX, stride=16), :]
                    columns[out, at + c, :, lanes] = column.astype(BF)
    fetch(columns.at[0], first_y)
    fetch(columns.at[1], last_y)
    for copy in copies[8:]:
        copy.wait()


def pack(fields, cot):
    rows = jax.ShapeDtypeStruct((HF + HC, BY, W), BF)
    columns = jax.ShapeDtypeStruct((HF + HC, BX, W), BF)
    return pl.pallas_call(
        pack_kernel,
        out_shape=(rows, rows, columns, columns),
        in_specs=[pl.BlockSpec(memory_space=pl.ANY)] * 2,
        out_specs=(pl.BlockSpec(memory_space=pl.ANY),) * 4,
        scratch_shapes=[
            pltpu.VMEM((4, BX, 16, W), BF),
            pltpu.VMEM((2, BX * 16, 128), F32),
            pltpu.VMEM((2, HF + HC, BY, W), BF),
            pltpu.VMEM((2, HF + HC, BX, W), BF),
            pltpu.SemaphoreType.DMA((12,)),
        ],
        compiler_params=pltpu.CompilerParams(vmem_limit_bytes=56 * 1024 * 1024),
        name="pack",
    )(fields, cot)


def exchange(fields, cot):
    first_x, last_x, first_y, last_y = pack(fields, cot)
    ylo = lax.ppermute(last_y, "gy", ring("gy", 1))
    yhi = lax.ppermute(first_y, "gy", ring("gy", -1))
    xlo = lax.ppermute(last_x, "gx", ring("gx", 1))
    xhi = lax.ppermute(first_x, "gx", ring("gx", -1))
    last_c = jnp.concatenate([ylo[:, BX - 8 :], yhi[:, BX - 8 :]], axis=0)
    first_c = jnp.concatenate([ylo[:, :8], yhi[:, :8]], axis=0)
    clo = lax.ppermute(last_c, "gx", ring("gx", 1))
    chi = lax.ppermute(first_c, "gx", ring("gx", -1))
    return (xlo, xhi, ylo, yhi, clo, chi)


def reduce_groups(nx, ny):
    flat = lambda x, y: x * ny + y
    near = [
        [flat(x, 2 * z + e) for x in range(c, nx, 2) for e in range(2)]
        for c in range(2)
        for z in range(ny // 2)
    ]
    far = [[flat(x, 2 * z + e) for z in range(ny // 2)] for x in range(nx) for e in range(2)]
    return near, far


def per_device(fields, w_down, w_pool, w_mid, w_unpool, w_up, cotangent):
    nx, ny = lax.axis_size("gx"), lax.axis_size("gy")
    near, far = reduce_groups(nx, ny)
    n1, n2 = len(near[0]), len(far[0])
    rows = -(-TILES * 32 // (16 * n1)) * 8
    core = (lax.axis_index("gx") % 2).astype(jnp.int32).reshape(1)
    pairs = [(i, i + 1 - 2 * (i % 2)) for i in range(nx)]
    bands = build_bands(w_down, w_pool, w_mid, w_unpool, w_up)
    halos = exchange(fields, cotangent)
    mine, other, skip_rows, down_rows = main_call(
        core, fields, cotangent, halos, bands, 2 * n1 * rows
    )
    swap = functools.partial(
        lax.all_to_all, axis_name=("gx", "gy"), split_axis=0, concat_axis=0, tiled=True
    )
    cells = fields.shape[0] * fields.shape[1] * 8 * nx * ny
    root = 1.0 / math.sqrt(math.sqrt(cells))
    theirs = lax.ppermute(other, "gx", pairs)
    output = finish_call(conv_rows, fields, skip_rows, bands[4])
    theirs, output = lax.optimization_barrier((theirs, output))
    part = mine.astype(F32) + theirs.astype(F32)
    part = swap(part.astype(BF).reshape(n1, rows, 128), axis_index_groups=near)
    part = (jnp.sum(part.astype(F32), axis=0) * root).astype(BF)
    part = swap(jnp.broadcast_to(part, (n2, rows, 128)), axis_index_groups=far).astype(F32)
    part = (jnp.sum(part, axis=0) * root).astype(BF)
    part = swap(jnp.broadcast_to(part, (n1, rows, 128)), axis_index_groups=near)
    part = part.reshape(n1 * rows, 128)
    theirs = lax.ppermute(part, "gx", pairs)
    grad_fields = finish_call(conv_t_rows, cotangent, down_rows, bands[0])
    down, pool, mid, unpool, up = unpack(core, part, theirs)
    return (
        output,
        grad_fields,
        down.reshape(w_down.shape),
        pool.reshape(w_pool.shape),
        mid.reshape(w_mid.shape),
        unpool.reshape(2, 2, 2, 32, 64).transpose(0, 1, 2, 4, 3),
        up.reshape(w_up.shape),
    )


def solution(mesh):
    placed = (P("gx", "gy", None), P(), P(), P(), P(), P(), P("gx", "gy", None))
    return jax.shard_map(
        per_device,
        mesh=mesh,
        in_specs=placed,
        out_specs=(P("gx", "gy", None), P("gx", "gy", None), P(), P(), P(), P(), P()),
        check_vma=False,
    )
```

```python
import functools
import math

import jax
import jax.numpy as jnp
from jax import lax
from jax.experimental import pallas as pl
from jax.experimental.pallas import tpu as pltpu
from jax.sharding import PartitionSpec as P

BF = jnp.bfloat16
F32 = jnp.float32
NN = (((1,), (0,)), ((), ()))
NT = (((1,), (1,)), ((), ()))
TN = (((0,), (0,)), ((), ()))

HF = 7
HC = 5
EX, EY = 32, 48
CX, CY = 16, 32
BX, BY = 16, 32
W = 256
TILES = 50


def dot(a, b, dims=NN):
    return lax.dot_general(a, b, dims, preferred_element_type=F32)


def rounded(v):
    return v.astype(BF).astype(F32)


DOWN, D_UP, UP = 7, 6, 3
MOST = 64


def loop(n, body, most=None):
    together = max(k for k in range(1, (most or MOST) + 1) if n % k == 0)

    def step(i, carry):
        for k in range(together):
            body(i * together + k)
        return carry

    if together == n:
        step(0, 0)
    else:
        lax.fori_loop(0, n // together, step, 0)


def aligned(at):
    return at if isinstance(at, int) else pl.multiple_of(at, 8)


def repeat_matrix(rows, cols, period, first):
    r = lax.broadcasted_iota(jnp.int32, (rows, cols), 0)
    c = lax.broadcasted_iota(jnp.int32, (rows, cols), 1)
    return (lax.rem(c, period) == r + first).astype(F32).astype(BF)


def bands_kernel(wd, wp, wm, wu, wup, bd, pm, bm, um, bu, wide, wide_mid):
    def band(w, out, wide, ch):
        planes = W // ch
        wide[...] = dot(w[...], repeat_matrix(ch, W, ch, 0))
        group = lax.broadcasted_iota(jnp.int32, (ch, W), 1) // ch

        def tap(t):
            base = t * 3 * ch if isinstance(t, int) else pl.multiple_of(t * 3 * ch, ch)
            t0 = wide[pl.ds(base, ch), :]
            t1 = wide[pl.ds(base + ch, ch), :]
            t2 = wide[pl.ds(base + 2 * ch, ch), :]
            for p in range(planes):
                rows = jnp.where(group == p, t1, 0.0)
                if p + 1 < planes:
                    rows = jnp.where(group == p + 1, t0, rows)
                if p > 0:
                    rows = jnp.where(group == p - 1, t2, rows)
                out[pl.ds(pl.multiple_of(t * W + p * ch, ch), ch), :] = rows.astype(BF)

        loop(9, tap)

    band(wd, bd, wide, 32)
    band(wup, bu, wide, 32)
    band(wm, bm, wide_mid, 64)
    group = lax.broadcasted_iota(jnp.int32, (64, W), 1) // 64
    same = repeat_matrix(64, W, 64, 0)
    low = repeat_matrix(32, W, 64, 0)
    high = repeat_matrix(32, W, 64, 32)
    for q in range(4):
        pool = dot(wp[q], same)
        unpool = dot(wu[2 * q], low, TN) + dot(wu[2 * q + 1], high, TN)
        for y in range(4):
            rows = slice(q * W + y * 64, q * W + y * 64 + 64)
            pm[rows, :] = jnp.where(group == y, pool, 0.0).astype(BF)
            um[rows, :] = jnp.where(group == y, unpool, 0.0).astype(BF)


def build_bands(w_down, w_pool, w_mid, w_unpool, w_up):
    wide = jax.ShapeDtypeStruct((9 * W, W), BF)
    four = jax.ShapeDtypeStruct((4 * W, W), BF)
    return pl.pallas_call(
        bands_kernel,
        out_shape=(wide, four, wide, four, wide),
        scratch_shapes=[pltpu.VMEM((27 * 32, W), F32), pltpu.VMEM((27 * 64, W), F32)],
        compiler_params=pltpu.CompilerParams(vmem_limit_bytes=24 * 1024 * 1024),
        cost_estimate=pl.CostEstimate(flops=2 * 10**9, bytes_accessed=8 * 10**6, transcendentals=0),
        name="bands",
    )(
        w_down.reshape(27 * 32, 32),
        w_pool.reshape(4, 64, 64),
        w_mid.reshape(27 * 64, 64),
        w_unpool.transpose(0, 1, 2, 4, 3).reshape(8, 32, 64),
        w_up.reshape(27 * 32, 32),
    )


def get_row(src, row):
    if len(src.shape) == 3 and src.shape[2] == 128:
        at = pl.ds(aligned(row * EY), EY)
        return jnp.concatenate([src[0, at, :], src[1, at, :]], axis=1)
    if len(src.shape) == 3:
        return src[row]
    return jnp.concatenate([src[0, row], src[1, row]], axis=1)


def get_rows(src, rows):
    return jnp.concatenate([src[0, rows], src[1, rows]], axis=2)


def put_row(dst, row, value):
    dst[row] = value.astype(BF)


def put_rows(dst, rows, value):
    dst[0, rows] = value[..., 0:128]
    dst[1, rows] = value[..., 128:256]


def get_every_second(src, row, first, count):
    at = pl.ds(first, count, stride=2)
    return jnp.concatenate([src[0, row, at, :], src[1, row, at, :]], axis=1)


def put_every_second(dst, row, first, value):
    at = pl.ds(first, value.shape[0], stride=2)
    dst[0, row, at, :] = value[:, 0:128]
    dst[1, row, at, :] = value[:, 128:256]


def taps_to_lanes(src, row, out, at, lo, size):
    v = get_row(src, row).astype(F32)
    n = v.shape[0]
    out[at, :, 0:W] = pltpu.roll(v, 1, 0)[lo : lo + size].astype(BF)
    out[at, :, W : 2 * W] = v[lo : lo + size].astype(BF)
    out[at, :, 2 * W : 3 * W] = pltpu.roll(v, n - 1, 0)[lo : lo + size].astype(BF)


def three_rows(v3, first, rows):
    pieces = [v3[pl.ds(first + a, rows)] for a in range(3)]
    pieces = [piece.reshape(rows * piece.shape[1], 3 * W) for piece in pieces]
    return jnp.concatenate(pieces, axis=1)


def conv_rows(v3, first, rows, band):
    return dot(three_rows(v3, first, rows), band[...])


def conv_t_rows(v3, first, rows, band):
    taps = [band[tap * W : (tap + 1) * W, :] for tap in range(8, -1, -1)]
    return dot(three_rows(v3, first, rows), jnp.concatenate(taps, axis=1), NT)


def pick(d, lanes, shift, ch, width):
    group = lax.broadcasted_iota(jnp.int32, (ch, 128), 1) // ch
    p0 = (lanes % width) // ch
    out = jnp.zeros((ch, 128), F32)
    for g in range(128 // ch):
        z = p0 + g - shift
        if 0 <= z < W // ch:
            out = jnp.where(group == g, d[z * ch : (z + 1) * ch, lanes : lanes + 128], out)
    return out


def put_split(value, hi, lo, row, lanes):
    top = value.astype(BF)
    hi[row : row + value.shape[0], lanes : lanes + 128] = top
    lo[row : row + value.shape[0], lanes : lanes + 128] = (value - top.astype(F32)).astype(BF)


def conv_weight_terms(dout_t, v3, rows, ch, hi, lo, dsc):
    units = 27 * ch
    pad = hi.shape[0] - units
    hi[units:, :] = jnp.zeros((pad, W), BF)
    lo[units:, :] = jnp.zeros((pad, W), BF)
    for a in range(3):
        piece = v3[a : a + rows]
        piece = piece.reshape(rows * piece.shape[1], 3 * W)
        dsc[...] = dot(dout_t, piece)
        for b in range(3):
            for k in range(3):
                unit = (a * 3 + b) * 3 + k
                for t in range(2):
                    value = pick(dsc, b * W + t * 128, k - 1, ch, W)
                    put_split(value, hi, lo, unit * ch, t * 128)


def main_kernel(
    core, fc, cc, xlo, xhi, ylo, yhi, clo, chi, bd, pm, bm, um, bu,
    mine, other, skip_rows, down_rows,
    fe, ce, hid, ds_down, skp, dup, ddn,
    v3f, v3c, v3fl, v3s,
    parts, d_parts, co, mid, ds_pool, ds_mid, dmid, v3m, v3dm, v3ml,
    hi, lo, him, lom, dsc, terms,
):
    def gather(dst, count, center, off):
        def put(row, value):
            at = pl.ds(aligned(row * EY + 8), BY)
            dst[0, at, :] = value[:, 0:128]
            dst[1, at, :] = value[:, 128:256]

        loop(BX, lambda i: put(8 + i, center[i].astype(F32)))

        def edge(i):
            put(8 - count + i, xlo[off + i].astype(F32))
            put(24 + i, xhi[off + i].astype(F32))

        loop(count, edge)
        for c in range(count):
            for side, y, other in ((ylo, 8 - count + c, 0), (yhi, 40 + c, HF + HC)):
                column = jnp.concatenate(
                    [
                        clo[other + off + c].astype(F32),
                        side[off + c].astype(F32),
                        chi[other + off + c].astype(F32),
                    ],
                    axis=0,
                )
                for h in range(2):
                    dst[h, pl.ds(y, EX, stride=EY), :] = column[:, h * 128 : h * 128 + 128]

    gather(fe, HF, fc, 0)
    gather(ce, HC, cc, HF)

    loop(30, lambda i: taps_to_lanes(fe, 1 + i, v3f, i, 0, EY))
    loop(18, lambda i: taps_to_lanes(fe, 7 + i, v3fl, i, 8, BY))
    zero = jnp.zeros((2, EY, W), F32)
    put_rows(hid, slice(0, 2), zero)
    put_rows(hid, slice(30, 32), zero)

    def down(i):
        pre = conv_rows(v3f, DOWN * i, DOWN, bd)
        sig = jax.nn.sigmoid(pre)
        at = pl.ds(2 + DOWN * i, DOWN)
        put_rows(hid, at, rounded(pre * sig).reshape(DOWN, EY, W))
        put_rows(ds_down, at, (sig * (1.0 + pre * (1.0 - sig))).reshape(DOWN, EY, W))

    loop(28 // DOWN, down)

    loop(26, lambda i: taps_to_lanes(ce, 3 + i, v3c, i, 0, EY))

    def d_up(i):
        total = conv_t_rows(v3c, D_UP * i, D_UP, bu)
        put_rows(dup, pl.ds(4 + D_UP * i, D_UP), total.reshape(D_UP, EY, W))

    loop(24 // D_UP, d_up)

    pad = jnp.zeros((CY - EY // 2, W), F32)

    def to_parts(src, x):
        for i in range(2):
            for j in range(2):
                half = get_every_second(src, 2 * x + i, j, EY // 2)
                parts[2 * i + j, x] = jnp.concatenate([half, pad], axis=0).astype(BF)

    loop(CX, lambda x: to_parts(hid, x))

    def pool(i):
        pieces = [parts[q, pl.ds(8 * i, 8)].reshape(8 * CY, W) for q in range(4)]
        pre = dot(jnp.concatenate(pieces, axis=1), pm[...])
        sig = jax.nn.sigmoid(pre)
        co[pl.ds(8 * i, 8)] = rounded(pre * sig).reshape(8, CY, W)
        ds_pool[pl.ds(8 * i, 8)] = (sig * (1.0 + pre * (1.0 - sig))).reshape(8, CY, W)

    loop(2, pool)

    loop(14, lambda i: taps_to_lanes(co, 1 + i, v3m, i, 0, CY))

    pre_mid = conv_rows(v3m, 0, 12, bm)
    sig_mid = jax.nn.sigmoid(pre_mid)
    own_mid = co[2:14].reshape(12 * CY, W)
    mid[2:14] = (own_mid + pre_mid * sig_mid).astype(BF).reshape(12, CY, W)
    ds_mid[2:14] = (sig_mid * (1.0 + pre_mid * (1.0 - sig_mid))).reshape(12, CY, W)

    def up(x):
        m = mid[pl.ds(2 + UP * x, UP)].reshape(UP * CY, W)
        for i in range(2):
            for j in range(2):
                q = 2 * i + j
                lifted = dot(m, um[q * W : (q + 1) * W, :])
                for r in range(UP):
                    at = 2 + UP * x + r
                    own = parts[q, at].astype(F32)[0 : EY // 2]
                    pre = own + lifted[r * CY : r * CY + EY // 2]
                    sig = jax.nn.sigmoid(pre)
                    put_every_second(skp, 2 * at + i, j, rounded(pre * sig))
                    raw = get_every_second(dup, 2 * at + i, j, EY // 2)
                    d_up = raw * (sig * (1.0 + pre * (1.0 - sig)))
                    d_parts[q, at] = jnp.concatenate([d_up, pad], axis=0).astype(BF)

    loop(12 // UP, up)

    loop(18, lambda i: taps_to_lanes(skp, 7 + i, v3s, i, 8, BY))
    loop(18, lambda i: put_row(skip_rows, i, get_row(skp, 7 + i)))

    cot_t = cc[...].reshape(BX * BY, W).astype(F32).T.astype(BF)
    fold = repeat_matrix(32, W, 32, 0)
    fold_mid = repeat_matrix(64, W, 64, 0)

    def fold_to(matrix, hi, lo, tile, count):
        total = dot(matrix, hi[...], NT) + dot(matrix, lo[...], NT)
        for t in range(count):
            rows = matrix.shape[0]
            part = total[:, t * 128 : (t + 1) * 128]
            terms[(tile * 32 + t * rows) : (tile * 32 + (t + 1) * rows), :] = part.astype(BF)

    conv_weight_terms(cot_t, v3s, BX, 32, hi, lo, dsc)
    fold_to(fold, hi, lo, 7, 7)

    def own_parts(src, q):
        return src[q, 4:12].astype(F32)[:, 4:20].reshape(128, W).astype(BF)

    mid_t = mid[4:12].astype(F32)[:, 0:24][:, 4:20].reshape(128, W).T.astype(BF)

    def fold_four(tile):
        total = dot(fold_mid, him[0:256, :], NT) + dot(fold_mid, lom[0:256, :], NT)
        for t in range(2):
            rows = slice(tile * 32 + t * 64, tile * 32 + (t + 1) * 64)
            terms[rows, :] = total[:, t * 128 : (t + 1) * 128].astype(BF)

    def plain_terms(left, src, q, row):
        d = dot(left, own_parts(src, q))
        for t in range(2):
            group = lax.broadcasted_iota(jnp.int32, (64, 128), 1) // 64
            low = d[(2 * t) * 64 : (2 * t + 1) * 64, t * 128 : (t + 1) * 128]
            high = d[(2 * t + 1) * 64 : (2 * t + 2) * 64, t * 128 : (t + 1) * 128]
            put_split(jnp.where(group == 0, low, high), him, lom, row, t * 128)

    for q in range(4):
        plain_terms(mid_t, d_parts, q, 64 * q)
    fold_four(46)

    pieces = [d_parts[q, 2:14].reshape(12 * CY, W) for q in range(4)]
    lanes = [um[q * W : (q + 1) * W, :] for q in range(4)]
    d_middle = dot(jnp.concatenate(pieces, axis=1), jnp.concatenate(lanes, axis=1), NT)
    dmid[2:14] = rounded(d_middle * ds_mid[2:14].reshape(12 * CY, W)).reshape(12, CY, W)
    ds_mid[2:14] = d_middle.reshape(12, CY, W)

    loop(12, lambda i: taps_to_lanes(dmid, 2 + i, v3dm, i, 0, CY))

    def coarse_local(i):
        v = co[3 + i]
        for b in range(3):
            v3ml[i, :, b * W : (b + 1) * W] = v[3 + b : 19 + b].astype(BF)

    loop(10, coarse_local)
    dmid_t = dmid[4:12][:, 4:20].reshape(128, W).T.astype(BF)
    conv_weight_terms(dmid_t, v3ml, 8, 64, him, lom, dsc)
    fold_to(fold_mid, him, lom, 14, 14)

    d_coarse = ds_mid[3:13] + conv_t_rows(v3dm, 0, 10, bm).reshape(10, CY, W)
    ds_pool[3:13] = rounded(d_coarse * ds_pool[3:13])

    dp = ds_pool[3:13].reshape(10 * CY, W).astype(BF)
    for i in range(2):
        for j in range(2):
            q = 2 * i + j
            back = dot(dp, pm[q * W : (q + 1) * W, :], NT)
            for r in range(10):
                row = 2 * (3 + r) + i
                own = d_parts[q, 3 + r].astype(F32)[0 : EY // 2]
                d_hidden = own + back[r * CY : r * CY + EY // 2]
                slope = get_every_second(ds_down, row, j, EY // 2)
                put_every_second(ddn, row, j, rounded(d_hidden * slope))

    loop(18, lambda i: put_row(down_rows, i, get_row(ddn, 7 + i)))

    down_t = get_rows(ddn, slice(8, 24))[:, 8:40].reshape(BX * BY, W).T.astype(BF)
    conv_weight_terms(down_t, v3fl, BX, 32, hi, lo, dsc)
    fold_to(fold, hi, lo, 0, 7)

    pool_t = ds_pool[4:12][:, 4:20].reshape(128, W).T.astype(BF)
    for q in range(4):
        plain_terms(pool_t, parts, q, 64 * q)
    fold_four(42)
    rest = terms.shape[0] - TILES * 32
    if rest > 0:
        terms[TILES * 32 :, :] = jnp.zeros((rest, 128), BF)
    half = terms.shape[0] // 2

    @pl.when(core[0] == 0)
    def _():
        mine[...] = terms[0:half, :]
        other[...] = terms[half:, :]

    @pl.when(core[0] != 0)
    def _():
        mine[...] = terms[half:, :]
        other[...] = terms[0:half, :]


def finish_kernel(conv, base, rows, band, out, v3):
    loop(18, lambda i: taps_to_lanes(rows, i, v3, i, 8, BY))
    total = conv(v3, 0, BX, band).reshape(BX, BY, W)
    out[...] = (base[...].astype(F32) + total).astype(BF)


def finish_call(conv, base, rows, band):
    return pl.pallas_call(
        functools.partial(finish_kernel, conv),
        out_shape=jax.ShapeDtypeStruct((BX, BY, W), BF),
        scratch_shapes=[pltpu.VMEM((18, BY, 3 * W), BF)],
        compiler_params=pltpu.CompilerParams(vmem_limit_bytes=16 * 1024 * 1024),
        cost_estimate=pl.CostEstimate(flops=10**9, bytes_accessed=10**6, transcendentals=0),
        name="finish",
    )(base, rows, band)


def main_call(core, fields, cot, halos, bands, term_rows):
    half = jax.ShapeDtypeStruct((term_rows // 2, 128), BF)
    some = jax.ShapeDtypeStruct((18, EY, W), BF)
    flat = pltpu.VMEM((2, EX * EY, 128), F32)
    split = pltpu.VMEM((2, EX, EY, 128), F32)
    coarse = pltpu.VMEM((CX, CY, W), F32)
    return pl.pallas_call(
        main_kernel,
        out_shape=(half, half, some, some),
        in_specs=[pl.BlockSpec(memory_space=pltpu.SMEM)]
        + [pl.BlockSpec(memory_space=pltpu.VMEM)] * 13,
        scratch_shapes=[flat] * 2
        + [split] * 5
        + [
            pltpu.VMEM((30, EY, 3 * W), BF),
            pltpu.VMEM((26, EY, 3 * W), BF),
            pltpu.VMEM((18, BY, 3 * W), BF),
            pltpu.VMEM((18, BY, 3 * W), BF),
            pltpu.VMEM((4, CX, CY, W), BF),
            pltpu.VMEM((4, CX, CY, W), BF),
            coarse,
            pltpu.VMEM((CX, CY, W), BF),
            coarse,
            coarse,
            coarse,
            pltpu.VMEM((14, CY, 3 * W), BF),
            pltpu.VMEM((12, CY, 3 * W), BF),
            pltpu.VMEM((10, 16, 3 * W), BF),
            pltpu.VMEM((28 * 32, W), BF),
            pltpu.VMEM((28 * 32, W), BF),
            pltpu.VMEM((28 * 64, W), BF),
            pltpu.VMEM((28 * 64, W), BF),
            pltpu.VMEM((W, 3 * W), F32),
            pltpu.VMEM((term_rows, 128), BF),
        ],
        compiler_params=pltpu.CompilerParams(vmem_limit_bytes=36 * 1024 * 1024),
        cost_estimate=pl.CostEstimate(flops=10**10, bytes_accessed=10**7, transcendentals=10**6),
        name="network",
    )(core, fields, cot, *halos, *bands)


def unpack_kernel(
    core, mine, other, down, pool, mid, unpool, up,
    down_v, pool_v, mid_v, unpool_v, up_v, terms, sems,
):
    half = mine.shape[0]

    @pl.when(core[0] == 0)
    def _():
        terms[0:half, :] = mine[...]
        terms[half:, :] = other[...]

    @pl.when(core[0] != 0)
    def _():
        terms[0:half, :] = other[...]
        terms[half:, :] = mine[...]

    def send(k, src, dst):
        copy = pltpu.make_async_copy(src, dst, sems.at[k])
        copy.start()
        return copy

    copies = []
    for part in range(3):
        for u in range(9 * part, 9 * part + 9):
            row, lane = 14 * 32 + (u // 2) * 64, (u % 2) * 64
            mid_v[u] = terms[row : row + 64, lane : lane + 64].astype(F32)
        at = pl.ds(9 * part, 9)
        copies.append(send(part, mid_v.at[at], mid.at[at]))
    for first, src, dst in ((0, down_v, down), (224, up_v, up)):
        for u in range(27):
            row, lane = first + (u // 4) * 32, (u % 4) * 32
            src[u] = terms[row : row + 32, lane : lane + 32].astype(F32)
        copies.append(send(3 if first == 0 else 4, src, dst))
    for first, src, dst in ((42 * 32, pool_v, pool), (46 * 32, unpool_v, unpool)):
        for q in range(4):
            row, lane = first + (q // 2) * 64, (q % 2) * 64
            src[q] = terms[row : row + 64, lane : lane + 64].astype(F32)
        copies.append(send(5 if src is pool_v else 6, src, dst))
    for copy in copies:
        copy.wait()


def unpack(core, mine, other):
    shapes = ((27, 32, 32), (4, 64, 64), (27, 64, 64), (4, 64, 64), (27, 32, 32))
    return pl.pallas_call(
        unpack_kernel,
        out_shape=tuple(jax.ShapeDtypeStruct(s, F32) for s in shapes),
        in_specs=[pl.BlockSpec(memory_space=pltpu.SMEM)]
        + [pl.BlockSpec(memory_space=pltpu.VMEM)] * 2,
        out_specs=tuple(pl.BlockSpec(memory_space=pl.ANY) for _ in shapes),
        scratch_shapes=[pltpu.VMEM(s, F32) for s in shapes]
        + [pltpu.VMEM((2 * mine.shape[0], 128), BF), pltpu.SemaphoreType.DMA((7,))],
        compiler_params=pltpu.CompilerParams(vmem_limit_bytes=8 * 1024 * 1024),
        name="unpack",
    )(core, mine, other)


def ring(axis, step):
    n = lax.axis_size(axis)
    return [(i, (i + step) % n) for i in range(n)]


def pack_kernel(fc, cc, first_x, last_x, first_y, last_y, side, wide, sems):
    copies = []

    def fetch(src, dst):
        copy = pltpu.make_async_copy(src, dst, sems.at[len(copies)])
        copy.start()
        copies.append(copy)

    for k, src in enumerate((fc, cc)):
        fetch(src.at[:, 0:16], side.at[2 * k])
        fetch(src.at[:, BY - 16 : BY], side.at[2 * k + 1])
    for src, count, at in ((fc, HF, 0), (cc, HC, HF)):
        fetch(src.at[0:count], first_x.at[at : at + count])
        fetch(src.at[BX - count : BX], last_x.at[at : at + count])
    for copy in copies[:4]:
        copy.wait()
    for k, (count, at) in enumerate(((HF, 0), (HC, HF))):
        for e, (out, first) in enumerate(((first_y, 0), (last_y, 16 - count))):
            for h in range(2):
                lanes = slice(h * 128, h * 128 + 128)
                wide[h] = side[2 * k + e, :, :, lanes].reshape(BX * 16, 128).astype(F32)
            for c in range(count):
                for h in range(2):
                    lanes = slice(h * 128, h * 128 + 128)
                    column = wide[h, pl.ds(first + c, BX, stride=16), :]
                    out[at + c, :, lanes] = column.astype(BF)
    for copy in copies[4:]:
        copy.wait()


def pack(fields, cot):
    rows = jax.ShapeDtypeStruct((HF + HC, BY, W), BF)
    columns = jax.ShapeDtypeStruct((HF + HC, BX, W), BF)
    return pl.pallas_call(
        pack_kernel,
        out_shape=(rows, rows, columns, columns),
        in_specs=[pl.BlockSpec(memory_space=pl.ANY)] * 2,
        scratch_shapes=[
            pltpu.VMEM((4, BX, 16, W), BF),
            pltpu.VMEM((2, BX * 16, 128), F32),
            pltpu.SemaphoreType.DMA((8,)),
        ],
        compiler_params=pltpu.CompilerParams(vmem_limit_bytes=54592 * 1024),
        name="pack",
    )(fields, cot)


def exchange(fields, cot):
    first_x, last_x, first_y, last_y = pack(fields, cot)
    ylo = lax.ppermute(last_y, "gy", ring("gy", 1))
    yhi = lax.ppermute(first_y, "gy", ring("gy", -1))
    xlo = lax.ppermute(last_x, "gx", ring("gx", 1))
    xhi = lax.ppermute(first_x, "gx", ring("gx", -1))
    last_c = jnp.concatenate([ylo[:, BX - 8 :], yhi[:, BX - 8 :]], axis=0)
    first_c = jnp.concatenate([ylo[:, :8], yhi[:, :8]], axis=0)
    clo = lax.ppermute(last_c, "gx", ring("gx", 1))
    chi = lax.ppermute(first_c, "gx", ring("gx", -1))
    return (xlo, xhi, ylo, yhi, clo, chi)


def reduce_groups(nx, ny):
    flat = lambda x, y: x * ny + y
    near = [
        [flat(x, 2 * z + e) for x in range(c, nx, 2) for e in range(2)]
        for c in range(2)
        for z in range(ny // 2)
    ]
    far = [[flat(x, 2 * z + e) for z in range(ny // 2)] for x in range(nx) for e in range(2)]
    return near, far


def per_device(fields, w_down, w_pool, w_mid, w_unpool, w_up, cotangent):
    nx, ny = lax.axis_size("gx"), lax.axis_size("gy")
    near, far = reduce_groups(nx, ny)
    n1, n2 = len(near[0]), len(far[0])
    rows = -(-TILES * 32 // (16 * n1)) * 8
    core = (lax.axis_index("gx") % 2).astype(jnp.int32).reshape(1)
    pairs = [(i, i + 1 - 2 * (i % 2)) for i in range(nx)]
    bands = build_bands(w_down, w_pool, w_mid, w_unpool, w_up)
    halos = exchange(fields, cotangent)
    mine, other, skip_rows, down_rows = main_call(
        core, fields, cotangent, halos, bands, 2 * n1 * rows
    )
    swap = functools.partial(
        lax.all_to_all, axis_name=("gx", "gy"), split_axis=0, concat_axis=0, tiled=True
    )
    cells = fields.shape[0] * fields.shape[1] * 8 * nx * ny
    root = 1.0 / math.sqrt(math.sqrt(cells))
    theirs = lax.ppermute(other, "gx", pairs)
    output = finish_call(conv_rows, fields, skip_rows, bands[4])
    theirs, output = lax.optimization_barrier((theirs, output))
    part = mine.astype(F32) + theirs.astype(F32)
    part = swap(part.astype(BF).reshape(n1, rows, 128), axis_index_groups=near)
    part = (jnp.sum(part.astype(F32), axis=0) * root).astype(BF)
    part = swap(jnp.broadcast_to(part, (n2, rows, 128)), axis_index_groups=far).astype(F32)
    part = (jnp.sum(part, axis=0) * root).astype(BF)
    part = swap(jnp.broadcast_to(part, (n1, rows, 128)), axis_index_groups=near)
    part = part.reshape(n1 * rows, 128)
    theirs = lax.ppermute(part, "gx", pairs)
    grad_fields = finish_call(conv_t_rows, cotangent, down_rows, bands[0])
    down, pool, mid, unpool, up = unpack(core, part, theirs)
    return (
        output,
        grad_fields,
        down.reshape(w_down.shape),
        pool.reshape(w_pool.shape),
        mid.reshape(w_mid.shape),
        unpool.reshape(2, 2, 2, 32, 64).transpose(0, 1, 2, 4, 3),
        up.reshape(w_up.shape),
    )


def solution(mesh):
    placed = (P("gx", "gy", None), P(), P(), P(), P(), P(), P("gx", "gy", None))
    return jax.shard_map(
        per_device,
        mesh=mesh,
        in_specs=placed,
        out_specs=(P("gx", "gy", None), P("gx", "gy", None), P(), P(), P(), P(), P()),
        check_vma=False,
    )
```

```python
import functools
import math

import jax
import jax.numpy as jnp
from jax import lax
from jax.experimental import pallas as pl
from jax.experimental.pallas import tpu as pltpu
from jax.sharding import PartitionSpec as P

BF = jnp.bfloat16
F32 = jnp.float32
NN = (((1,), (0,)), ((), ()))
NT = (((1,), (1,)), ((), ()))
TN = (((0,), (0,)), ((), ()))

HF = 7
HC = 5
EX, EY = 32, 48
CX, CY = 16, 32
BX, BY = 16, 32
W = 256
TILES = 50


def dot(a, b, dims=NN):
    return lax.dot_general(a, b, dims, preferred_element_type=F32)


def rounded(v):
    return v.astype(BF).astype(F32)


DOWN, D_UP, UP = 14, 24, 6
MOST = 64


def loop(n, body, most=None):
    together = max(k for k in range(1, (most or MOST) + 1) if n % k == 0)

    def step(i, carry):
        for k in range(together):
            body(i * together + k)
        return carry

    if together == n:
        step(0, 0)
    else:
        lax.fori_loop(0, n // together, step, 0)


def aligned(at):
    return at if isinstance(at, int) else pl.multiple_of(at, 8)


def repeat_matrix(rows, cols, period, first):
    r = lax.broadcasted_iota(jnp.int32, (rows, cols), 0)
    c = lax.broadcasted_iota(jnp.int32, (rows, cols), 1)
    return (lax.rem(c, period) == r + first).astype(F32).astype(BF)


def bands_kernel(wd, wp, wm, wu, wup, bd, pm, bm, um, bu, wide, wide_mid):
    def band(w, out, wide, ch):
        planes = W // ch
        wide[...] = dot(w[...], repeat_matrix(ch, W, ch, 0))
        group = lax.broadcasted_iota(jnp.int32, (ch, W), 1) // ch

        def tap(t):
            base = t * 3 * ch if isinstance(t, int) else pl.multiple_of(t * 3 * ch, ch)
            t0 = wide[pl.ds(base, ch), :]
            t1 = wide[pl.ds(base + ch, ch), :]
            t2 = wide[pl.ds(base + 2 * ch, ch), :]
            for p in range(planes):
                rows = jnp.where(group == p, t1, 0.0)
                if p + 1 < planes:
                    rows = jnp.where(group == p + 1, t0, rows)
                if p > 0:
                    rows = jnp.where(group == p - 1, t2, rows)
                out[pl.ds(pl.multiple_of(t * W + p * ch, ch), ch), :] = rows.astype(BF)

        loop(9, tap)

    band(wd, bd, wide, 32)
    band(wup, bu, wide, 32)
    band(wm, bm, wide_mid, 64)
    group = lax.broadcasted_iota(jnp.int32, (64, W), 1) // 64
    same = repeat_matrix(64, W, 64, 0)
    low = repeat_matrix(32, W, 64, 0)
    high = repeat_matrix(32, W, 64, 32)
    for q in range(4):
        pool = dot(wp[q], same)
        unpool = dot(wu[2 * q], low, TN) + dot(wu[2 * q + 1], high, TN)
        for y in range(4):
            rows = slice(q * W + y * 64, q * W + y * 64 + 64)
            pm[rows, :] = jnp.where(group == y, pool, 0.0).astype(BF)
            um[rows, :] = jnp.where(group == y, unpool, 0.0).astype(BF)


def build_bands(w_down, w_pool, w_mid, w_unpool, w_up):
    wide = jax.ShapeDtypeStruct((9 * W, W), BF)
    four = jax.ShapeDtypeStruct((4 * W, W), BF)
    return pl.pallas_call(
        bands_kernel,
        out_shape=(wide, four, wide, four, wide),
        scratch_shapes=[pltpu.VMEM((27 * 32, W), F32), pltpu.VMEM((27 * 64, W), F32)],
        compiler_params=pltpu.CompilerParams(vmem_limit_bytes=24 * 1024 * 1024),
        cost_estimate=pl.CostEstimate(flops=2 * 10**9, bytes_accessed=8 * 10**6, transcendentals=0),
        name="bands",
    )(
        w_down.reshape(27 * 32, 32),
        w_pool.reshape(4, 64, 64),
        w_mid.reshape(27 * 64, 64),
        w_unpool.transpose(0, 1, 2, 4, 3).reshape(8, 32, 64),
        w_up.reshape(27 * 32, 32),
    )


def get_row(src, row):
    if len(src.shape) == 3 and src.shape[2] == 128:
        at = pl.ds(aligned(row * EY), EY)
        return jnp.concatenate([src[0, at, :], src[1, at, :]], axis=1)
    if len(src.shape) == 3:
        return src[row]
    return jnp.concatenate([src[0, row], src[1, row]], axis=1)


def get_rows(src, rows):
    return jnp.concatenate([src[0, rows], src[1, rows]], axis=2)


def put_row(dst, row, value):
    dst[row] = value.astype(BF)


def put_rows(dst, rows, value):
    dst[0, rows] = value[..., 0:128]
    dst[1, rows] = value[..., 128:256]


def get_every_second(src, row, first, count):
    at = pl.ds(first, count, stride=2)
    return jnp.concatenate([src[0, row, at, :], src[1, row, at, :]], axis=1)


def put_every_second(dst, row, first, value):
    at = pl.ds(first, value.shape[0], stride=2)
    dst[0, row, at, :] = value[:, 0:128]
    dst[1, row, at, :] = value[:, 128:256]


def taps_to_lanes(src, row, out, at, lo, size):
    v = get_row(src, row).astype(F32)
    n = v.shape[0]
    out[at, :, 0:W] = pltpu.roll(v, 1, 0)[lo : lo + size].astype(BF)
    out[at, :, W : 2 * W] = v[lo : lo + size].astype(BF)
    out[at, :, 2 * W : 3 * W] = pltpu.roll(v, n - 1, 0)[lo : lo + size].astype(BF)


def three_rows(v3, first, rows):
    pieces = [v3[pl.ds(first + a, rows)] for a in range(3)]
    pieces = [piece.reshape(rows * piece.shape[1], 3 * W) for piece in pieces]
    return jnp.concatenate(pieces, axis=1)


def conv_rows(v3, first, rows, band):
    return dot(three_rows(v3, first, rows), band[...])


def conv_t_rows(v3, first, rows, band):
    taps = [band[tap * W : (tap + 1) * W, :] for tap in range(8, -1, -1)]
    return dot(three_rows(v3, first, rows), jnp.concatenate(taps, axis=1), NT)


def pick(d, lanes, shift, ch, width):
    group = lax.broadcasted_iota(jnp.int32, (ch, 128), 1) // ch
    p0 = (lanes % width) // ch
    out = jnp.zeros((ch, 128), F32)
    for g in range(128 // ch):
        z = p0 + g - shift
        if 0 <= z < W // ch:
            out = jnp.where(group == g, d[z * ch : (z + 1) * ch, lanes : lanes + 128], out)
    return out


def put_split(value, hi, lo, row, lanes):
    top = value.astype(BF)
    hi[row : row + value.shape[0], lanes : lanes + 128] = top
    lo[row : row + value.shape[0], lanes : lanes + 128] = (value - top.astype(F32)).astype(BF)


def conv_weight_terms(dout_t, v3, rows, ch, hi, lo, dsc):
    units = 27 * ch
    pad = hi.shape[0] - units
    hi[units:, :] = jnp.zeros((pad, W), BF)
    lo[units:, :] = jnp.zeros((pad, W), BF)
    for a in range(3):
        piece = v3[a : a + rows]
        piece = piece.reshape(rows * piece.shape[1], 3 * W)
        dsc[...] = dot(dout_t, piece)
        for b in range(3):
            for k in range(3):
                unit = (a * 3 + b) * 3 + k
                for t in range(2):
                    value = pick(dsc, b * W + t * 128, k - 1, ch, W)
                    put_split(value, hi, lo, unit * ch, t * 128)


def main_kernel(
    core, fc, cc, xlo, xhi, ylo, yhi, clo, chi, bd, pm, bm, um, bu,
    mine, other, skip_rows, down_rows,
    fe, ce, hid, ds_down, skp, dup, ddn,
    v3f, v3c, v3fl, v3s,
    parts, d_parts, co, mid, ds_pool, ds_mid, dmid, v3m, v3dm, v3ml,
    hi, lo, him, lom, dsc, terms,
):
    def gather(dst, count, center, off):
        def put(row, value):
            at = pl.ds(aligned(row * EY + 8), BY)
            dst[0, at, :] = value[:, 0:128]
            dst[1, at, :] = value[:, 128:256]

        loop(BX, lambda i: put(8 + i, center[i].astype(F32)))

        def edge(i):
            put(8 - count + i, xlo[off + i].astype(F32))
            put(24 + i, xhi[off + i].astype(F32))

        loop(count, edge)
        for c in range(count):
            for side, y, other in ((ylo, 8 - count + c, 0), (yhi, 40 + c, HF + HC)):
                column = jnp.concatenate(
                    [
                        clo[other + off + c].astype(F32),
                        side[off + c].astype(F32),
                        chi[other + off + c].astype(F32),
                    ],
                    axis=0,
                )
                for h in range(2):
                    dst[h, pl.ds(y, EX, stride=EY), :] = column[:, h * 128 : h * 128 + 128]

    gather(fe, HF, fc, 0)
    gather(ce, HC, cc, HF)

    loop(30, lambda i: taps_to_lanes(fe, 1 + i, v3f, i, 0, EY))
    loop(18, lambda i: taps_to_lanes(fe, 7 + i, v3fl, i, 8, BY))
    zero = jnp.zeros((2, EY, W), F32)
    put_rows(hid, slice(0, 2), zero)
    put_rows(hid, slice(30, 32), zero)

    def down(i):
        pre = conv_rows(v3f, DOWN * i, DOWN, bd)
        sig = jax.nn.sigmoid(pre)
        at = pl.ds(2 + DOWN * i, DOWN)
        put_rows(hid, at, rounded(pre * sig).reshape(DOWN, EY, W))
        put_rows(ds_down, at, (sig * (1.0 + pre * (1.0 - sig))).reshape(DOWN, EY, W))

    loop(28 // DOWN, down)

    loop(26, lambda i: taps_to_lanes(ce, 3 + i, v3c, i, 0, EY))

    def d_up(i):
        total = conv_t_rows(v3c, D_UP * i, D_UP, bu)
        put_rows(dup, pl.ds(4 + D_UP * i, D_UP), total.reshape(D_UP, EY, W))

    loop(24 // D_UP, d_up)

    pad = jnp.zeros((CY - EY // 2, W), F32)

    def to_parts(src, x):
        for i in range(2):
            for j in range(2):
                half = get_every_second(src, 2 * x + i, j, EY // 2)
                parts[2 * i + j, x] = jnp.concatenate([half, pad], axis=0).astype(BF)

    loop(CX, lambda x: to_parts(hid, x))

    def pool(i):
        pieces = [parts[q, pl.ds(8 * i, 8)].reshape(8 * CY, W) for q in range(4)]
        pre = dot(jnp.concatenate(pieces, axis=1), pm[...])
        sig = jax.nn.sigmoid(pre)
        co[pl.ds(8 * i, 8)] = rounded(pre * sig).reshape(8, CY, W)
        ds_pool[pl.ds(8 * i, 8)] = (sig * (1.0 + pre * (1.0 - sig))).reshape(8, CY, W)

    loop(2, pool)

    loop(14, lambda i: taps_to_lanes(co, 1 + i, v3m, i, 0, CY))

    pre_mid = conv_rows(v3m, 0, 12, bm)
    sig_mid = jax.nn.sigmoid(pre_mid)
    own_mid = co[2:14].reshape(12 * CY, W)
    mid[2:14] = (own_mid + pre_mid * sig_mid).astype(BF).reshape(12, CY, W)
    ds_mid[2:14] = (sig_mid * (1.0 + pre_mid * (1.0 - sig_mid))).reshape(12, CY, W)

    def up(x):
        m = mid[pl.ds(2 + UP * x, UP)].reshape(UP * CY, W)
        for i in range(2):
            for j in range(2):
                q = 2 * i + j
                lifted = dot(m, um[q * W : (q + 1) * W, :])
                for r in range(UP):
                    at = 2 + UP * x + r
                    own = parts[q, at].astype(F32)[0 : EY // 2]
                    pre = own + lifted[r * CY : r * CY + EY // 2]
                    sig = jax.nn.sigmoid(pre)
                    put_every_second(skp, 2 * at + i, j, rounded(pre * sig))
                    raw = get_every_second(dup, 2 * at + i, j, EY // 2)
                    d_up = raw * (sig * (1.0 + pre * (1.0 - sig)))
                    d_parts[q, at] = jnp.concatenate([d_up, pad], axis=0).astype(BF)

    loop(12 // UP, up)

    loop(18, lambda i: taps_to_lanes(skp, 7 + i, v3s, i, 8, BY))
    loop(18, lambda i: put_row(skip_rows, i, get_row(skp, 7 + i)))

    cot_t = cc[...].reshape(BX * BY, W).astype(F32).T.astype(BF)
    fold = repeat_matrix(32, W, 32, 0)
    fold_mid = repeat_matrix(64, W, 64, 0)

    def fold_to(matrix, hi, lo, tile, count):
        total = dot(matrix, hi[...], NT) + dot(matrix, lo[...], NT)
        for t in range(count):
            rows = matrix.shape[0]
            part = total[:, t * 128 : (t + 1) * 128]
            terms[(tile * 32 + t * rows) : (tile * 32 + (t + 1) * rows), :] = part.astype(BF)

    conv_weight_terms(cot_t, v3s, BX, 32, hi, lo, dsc)
    fold_to(fold, hi, lo, 7, 7)

    def own_parts(src, q):
        return src[q, 4:12].astype(F32)[:, 4:20].reshape(128, W).astype(BF)

    mid_t = mid[4:12].astype(F32)[:, 0:24][:, 4:20].reshape(128, W).T.astype(BF)

    def fold_four(tile):
        total = dot(fold_mid, him[0:256, :], NT) + dot(fold_mid, lom[0:256, :], NT)
        for t in range(2):
            rows = slice(tile * 32 + t * 64, tile * 32 + (t + 1) * 64)
            terms[rows, :] = total[:, t * 128 : (t + 1) * 128].astype(BF)

    def plain_terms(left, src, q, row):
        d = dot(left, own_parts(src, q))
        for t in range(2):
            group = lax.broadcasted_iota(jnp.int32, (64, 128), 1) // 64
            low = d[(2 * t) * 64 : (2 * t + 1) * 64, t * 128 : (t + 1) * 128]
            high = d[(2 * t + 1) * 64 : (2 * t + 2) * 64, t * 128 : (t + 1) * 128]
            put_split(jnp.where(group == 0, low, high), him, lom, row, t * 128)

    for q in range(4):
        plain_terms(mid_t, d_parts, q, 64 * q)
    fold_four(46)

    pieces = [d_parts[q, 2:14].reshape(12 * CY, W) for q in range(4)]
    lanes = [um[q * W : (q + 1) * W, :] for q in range(4)]
    d_middle = dot(jnp.concatenate(pieces, axis=1), jnp.concatenate(lanes, axis=1), NT)
    dmid[2:14] = rounded(d_middle * ds_mid[2:14].reshape(12 * CY, W)).reshape(12, CY, W)
    ds_mid[2:14] = d_middle.reshape(12, CY, W)

    loop(12, lambda i: taps_to_lanes(dmid, 2 + i, v3dm, i, 0, CY))

    def coarse_local(i):
        v = co[3 + i]
        for b in range(3):
            v3ml[i, :, b * W : (b + 1) * W] = v[3 + b : 19 + b].astype(BF)

    loop(10, coarse_local)
    dmid_t = dmid[4:12][:, 4:20].reshape(128, W).T.astype(BF)
    conv_weight_terms(dmid_t, v3ml, 8, 64, him, lom, dsc)
    fold_to(fold_mid, him, lom, 14, 14)

    d_coarse = ds_mid[3:13] + conv_t_rows(v3dm, 0, 10, bm).reshape(10, CY, W)
    ds_pool[3:13] = rounded(d_coarse * ds_pool[3:13])

    dp = ds_pool[3:13].reshape(10 * CY, W).astype(BF)
    for i in range(2):
        for j in range(2):
            q = 2 * i + j
            back = dot(dp, pm[q * W : (q + 1) * W, :], NT)
            for r in range(10):
                row = 2 * (3 + r) + i
                own = d_parts[q, 3 + r].astype(F32)[0 : EY // 2]
                d_hidden = own + back[r * CY : r * CY + EY // 2]
                slope = get_every_second(ds_down, row, j, EY // 2)
                put_every_second(ddn, row, j, rounded(d_hidden * slope))

    loop(18, lambda i: put_row(down_rows, i, get_row(ddn, 7 + i)))

    down_t = get_rows(ddn, slice(8, 24))[:, 8:40].reshape(BX * BY, W).T.astype(BF)
    conv_weight_terms(down_t, v3fl, BX, 32, hi, lo, dsc)
    fold_to(fold, hi, lo, 0, 7)

    pool_t = ds_pool[4:12][:, 4:20].reshape(128, W).T.astype(BF)
    for q in range(4):
        plain_terms(pool_t, parts, q, 64 * q)
    fold_four(42)
    rest = terms.shape[0] - TILES * 32
    if rest > 0:
        terms[TILES * 32 :, :] = jnp.zeros((rest, 128), BF)
    half = terms.shape[0] // 2

    @pl.when(core[0] == 0)
    def _():
        mine[...] = terms[0:half, :]
        other[...] = terms[half:, :]

    @pl.when(core[0] != 0)
    def _():
        mine[...] = terms[half:, :]
        other[...] = terms[0:half, :]


def finish_kernel(conv, base, rows, band, out, v3):
    loop(18, lambda i: taps_to_lanes(rows, i, v3, i, 8, BY))
    total = conv(v3, 0, BX, band).reshape(BX, BY, W)
    out[...] = (base[...].astype(F32) + total).astype(BF)


def finish_call(conv, base, rows, band):
    return pl.pallas_call(
        functools.partial(finish_kernel, conv),
        out_shape=jax.ShapeDtypeStruct((BX, BY, W), BF),
        scratch_shapes=[pltpu.VMEM((18, BY, 3 * W), BF)],
        compiler_params=pltpu.CompilerParams(vmem_limit_bytes=16 * 1024 * 1024),
        cost_estimate=pl.CostEstimate(flops=10**9, bytes_accessed=10**6, transcendentals=0),
        name="finish",
    )(base, rows, band)


def main_call(core, fields, cot, halos, bands, term_rows):
    half = jax.ShapeDtypeStruct((term_rows // 2, 128), BF)
    some = jax.ShapeDtypeStruct((18, EY, W), BF)
    flat = pltpu.VMEM((2, EX * EY, 128), F32)
    split = pltpu.VMEM((2, EX, EY, 128), F32)
    coarse = pltpu.VMEM((CX, CY, W), F32)
    return pl.pallas_call(
        main_kernel,
        out_shape=(half, half, some, some),
        in_specs=[pl.BlockSpec(memory_space=pltpu.SMEM)]
        + [pl.BlockSpec(memory_space=pltpu.VMEM)] * 13,
        scratch_shapes=[flat] * 2
        + [split] * 5
        + [
            pltpu.VMEM((30, EY, 3 * W), BF),
            pltpu.VMEM((26, EY, 3 * W), BF),
            pltpu.VMEM((18, BY, 3 * W), BF),
            pltpu.VMEM((18, BY, 3 * W), BF),
            pltpu.VMEM((4, CX, CY, W), BF),
            pltpu.VMEM((4, CX, CY, W), BF),
            coarse,
            pltpu.VMEM((CX, CY, W), BF),
            coarse,
            coarse,
            coarse,
            pltpu.VMEM((14, CY, 3 * W), BF),
            pltpu.VMEM((12, CY, 3 * W), BF),
            pltpu.VMEM((10, 16, 3 * W), BF),
            pltpu.VMEM((28 * 32, W), BF),
            pltpu.VMEM((28 * 32, W), BF),
            pltpu.VMEM((28 * 64, W), BF),
            pltpu.VMEM((28 * 64, W), BF),
            pltpu.VMEM((W, 3 * W), F32),
            pltpu.VMEM((term_rows, 128), BF),
        ],
        compiler_params=pltpu.CompilerParams(vmem_limit_bytes=36 * 1024 * 1024),
        cost_estimate=pl.CostEstimate(flops=10**10, bytes_accessed=10**7, transcendentals=10**6),
        name="network",
    )(core, fields, cot, *halos, *bands)


def unpack_kernel(
    core, mine, other, down, pool, mid, unpool, up,
    down_v, pool_v, mid_v, unpool_v, up_v, terms, sems,
):
    half = mine.shape[0]

    @pl.when(core[0] == 0)
    def _():
        terms[0:half, :] = mine[...]
        terms[half:, :] = other[...]

    @pl.when(core[0] != 0)
    def _():
        terms[0:half, :] = other[...]
        terms[half:, :] = mine[...]

    def send(k, src, dst):
        copy = pltpu.make_async_copy(src, dst, sems.at[k])
        copy.start()
        return copy

    copies = []
    for part in range(3):
        for u in range(9 * part, 9 * part + 9):
            row, lane = 14 * 32 + (u // 2) * 64, (u % 2) * 64
            mid_v[u] = terms[row : row + 64, lane : lane + 64].astype(F32)
        at = pl.ds(9 * part, 9)
        copies.append(send(part, mid_v.at[at], mid.at[at]))
    for first, src, dst in ((0, down_v, down), (224, up_v, up)):
        for u in range(27):
            row, lane = first + (u // 4) * 32, (u % 4) * 32
            src[u] = terms[row : row + 32, lane : lane + 32].astype(F32)
        copies.append(send(3 if first == 0 else 4, src, dst))
    for first, src, dst in ((42 * 32, pool_v, pool), (46 * 32, unpool_v, unpool)):
        for q in range(4):
            row, lane = first + (q // 2) * 64, (q % 2) * 64
            src[q] = terms[row : row + 64, lane : lane + 64].astype(F32)
        copies.append(send(5 if src is pool_v else 6, src, dst))
    for copy in copies:
        copy.wait()


def unpack(core, mine, other):
    shapes = ((27, 32, 32), (4, 64, 64), (27, 64, 64), (4, 64, 64), (27, 32, 32))
    return pl.pallas_call(
        unpack_kernel,
        out_shape=tuple(jax.ShapeDtypeStruct(s, F32) for s in shapes),
        in_specs=[pl.BlockSpec(memory_space=pltpu.SMEM)]
        + [pl.BlockSpec(memory_space=pltpu.VMEM)] * 2,
        out_specs=tuple(pl.BlockSpec(memory_space=pl.ANY) for _ in shapes),
        scratch_shapes=[pltpu.VMEM(s, F32) for s in shapes]
        + [pltpu.VMEM((2 * mine.shape[0], 128), BF), pltpu.SemaphoreType.DMA((7,))],
        compiler_params=pltpu.CompilerParams(vmem_limit_bytes=8 * 1024 * 1024),
        name="unpack",
    )(core, mine, other)


def ring(axis, step):
    n = lax.axis_size(axis)
    return [(i, (i + step) % n) for i in range(n)]


def pack_kernel(fc, cc, first_x, last_x, first_y, last_y, side, wide, sems):
    copies = []

    def fetch(src, dst):
        copy = pltpu.make_async_copy(src, dst, sems.at[len(copies)])
        copy.start()
        copies.append(copy)

    for k, src in enumerate((fc, cc)):
        fetch(src.at[:, 0:16], side.at[2 * k])
        fetch(src.at[:, BY - 16 : BY], side.at[2 * k + 1])
    for src, count, at in ((fc, HF, 0), (cc, HC, HF)):
        fetch(src.at[0:count], first_x.at[at : at + count])
        fetch(src.at[BX - count : BX], last_x.at[at : at + count])
    for copy in copies[:4]:
        copy.wait()
    for k, (count, at) in enumerate(((HF, 0), (HC, HF))):
        for e, (out, first) in enumerate(((first_y, 0), (last_y, 16 - count))):
            for h in range(2):
                lanes = slice(h * 128, h * 128 + 128)
                wide[h] = side[2 * k + e, :, :, lanes].reshape(BX * 16, 128).astype(F32)
            for c in range(count):
                for h in range(2):
                    lanes = slice(h * 128, h * 128 + 128)
                    column = wide[h, pl.ds(first + c, BX, stride=16), :]
                    out[at + c, :, lanes] = column.astype(BF)
    for copy in copies[4:]:
        copy.wait()


def pack(fields, cot):
    rows = jax.ShapeDtypeStruct((HF + HC, BY, W), BF)
    columns = jax.ShapeDtypeStruct((HF + HC, BX, W), BF)
    return pl.pallas_call(
        pack_kernel,
        out_shape=(rows, rows, columns, columns),
        in_specs=[pl.BlockSpec(memory_space=pl.ANY)] * 2,
        scratch_shapes=[
            pltpu.VMEM((4, BX, 16, W), BF),
            pltpu.VMEM((2, BX * 16, 128), F32),
            pltpu.SemaphoreType.DMA((8,)),
        ],
        compiler_params=pltpu.CompilerParams(vmem_limit_bytes=54592 * 1024),
        name="pack",
    )(fields, cot)


def exchange(fields, cot):
    first_x, last_x, first_y, last_y = pack(fields, cot)
    ylo = lax.ppermute(last_y, "gy", ring("gy", 1))
    yhi = lax.ppermute(first_y, "gy", ring("gy", -1))
    xlo = lax.ppermute(last_x, "gx", ring("gx", 1))
    xhi = lax.ppermute(first_x, "gx", ring("gx", -1))
    last_c = jnp.concatenate([ylo[:, BX - 8 :], yhi[:, BX - 8 :]], axis=0)
    first_c = jnp.concatenate([ylo[:, :8], yhi[:, :8]], axis=0)
    clo = lax.ppermute(last_c, "gx", ring("gx", 1))
    chi = lax.ppermute(first_c, "gx", ring("gx", -1))
    return (xlo, xhi, ylo, yhi, clo, chi)


def reduce_groups(nx, ny):
    flat = lambda x, y: x * ny + y
    near = [
        [flat(x, 2 * z + e) for x in range(c, nx, 2) for e in range(2)]
        for c in range(2)
        for z in range(ny // 2)
    ]
    far = [[flat(x, 2 * z + e) for z in range(ny // 2)] for x in range(nx) for e in range(2)]
    return near, far


def per_device(fields, w_down, w_pool, w_mid, w_unpool, w_up, cotangent):
    nx, ny = lax.axis_size("gx"), lax.axis_size("gy")
    near, far = reduce_groups(nx, ny)
    n1, n2 = len(near[0]), len(far[0])
    rows = -(-TILES * 32 // (16 * n1)) * 8
    core = (lax.axis_index("gx") % 2).astype(jnp.int32).reshape(1)
    pairs = [(i, i + 1 - 2 * (i % 2)) for i in range(nx)]
    bands = build_bands(w_down, w_pool, w_mid, w_unpool, w_up)
    halos = exchange(fields, cotangent)
    mine, other, skip_rows, down_rows = main_call(
        core, fields, cotangent, halos, bands, 2 * n1 * rows
    )
    swap = functools.partial(
        lax.all_to_all, axis_name=("gx", "gy"), split_axis=0, concat_axis=0, tiled=True
    )
    cells = fields.shape[0] * fields.shape[1] * 8 * nx * ny
    root = 1.0 / math.sqrt(math.sqrt(cells))
    theirs = lax.ppermute(other, "gx", pairs)
    output = finish_call(conv_rows, fields, skip_rows, bands[4])
    theirs, output = lax.optimization_barrier((theirs, output))
    part = mine.astype(F32) + theirs.astype(F32)
    part = swap(part.astype(BF).reshape(n1, rows, 128), axis_index_groups=near)
    part = (jnp.sum(part.astype(F32), axis=0) * root).astype(BF)
    part = swap(jnp.broadcast_to(part, (n2, rows, 128)), axis_index_groups=far).astype(F32)
    part = (jnp.sum(part, axis=0) * root).astype(BF)
    part = swap(jnp.broadcast_to(part, (n1, rows, 128)), axis_index_groups=near)
    part = part.reshape(n1 * rows, 128)
    theirs = lax.ppermute(part, "gx", pairs)
    grad_fields = finish_call(conv_t_rows, cotangent, down_rows, bands[0])
    down, pool, mid, unpool, up = unpack(core, part, theirs)
    return (
        output,
        grad_fields,
        down.reshape(w_down.shape),
        pool.reshape(w_pool.shape),
        mid.reshape(w_mid.shape),
        unpool.reshape(2, 2, 2, 32, 64).transpose(0, 1, 2, 4, 3),
        up.reshape(w_up.shape),
    )


def solution(mesh):
    placed = (P("gx", "gy", None), P(), P(), P(), P(), P(), P("gx", "gy", None))
    return jax.shard_map(
        per_device,
        mesh=mesh,
        in_specs=placed,
        out_specs=(P("gx", "gy", None), P("gx", "gy", None), P(), P(), P(), P(), P()),
        check_vma=False,
    )
```
